32 devices in a mesh: ctx: 4 (over y, x), exp: 8 (over z, core).
Axes of the slice: x: 2, y: 2, z: 4, core: 2. Of those that a mesh axis runs over, the one named last changes fastest.
Arguments:
- out_grad: bfloat16 [8192, 4096], P(('ctx', 'exp')), may hold values from -6 to 6
- gate_in: bfloat16 [8192, 4096], P(('ctx', 'exp')), may hold values from -6 to 6
- conv_in: bfloat16 [8192, 4096], P(('ctx', 'exp')), may hold values from -6 to 6
- scan_grad: bfloat16 [8192, 4096], P(('ctx', 'exp')), may hold values from -6 to 6
- conv_weight: float32 [4, 8192], P(None, ('ctx', 'exp')), may hold values from -3 to 3
- conv_bias: float32 [8192], P(('ctx', 'exp')), may hold values from -3 to 3
- skip_scale: float32 [8192], P(('ctx', 'exp')), may hold values from 0.5 to 1.5
- projection: bfloat16 [8192, 4096], P(('ctx', 'exp')), may hold values from -0.09375 to 0.09375
- resid_grad: bfloat16 [4096, 4096], P(('ctx', 'exp')), may hold values from -6 to 6
- routes: int32 [4096, 2], P(('ctx', 'exp')), may hold values from 0 to 7, as said below
- gate_probs: float32 [4096, 2], P(('ctx', 'exp')), may hold values from 0.05 to 0.95
Outputs:
- expert_rows: bfloat16 [8, 1792, 4096], P('exp', 'ctx')
The draws below stay inside these ranges and needn't reach their ends.
Inputs may be any that keep to these rules, and one draw needn't show every extreme that they name: `routes`: each row names 2 different experts. In every aligned block of 128 rows (the rows of one device) no expert is named by more than 56 rows, and in each run of 8 consecutive blocks one expert is named by exactly 56 rows of every block.
All inputs are finite; a program needn't handle non-finite values.
Results may differ from the reference program's by a relative error of at most 0.012.
Values may be sent and summed in bfloat16 or wider, within the bound.
No kernel may reach another device: no remote copies, remote signals or barrier semaphores. Data moves between devices by JAX's collectives and lax.ppermute only.
A program may use at most 128 MiB of HBM per device.

```python
import jax
import jax.numpy as jnp
from jax import lax

D = 4096
E = 8192
CONV = 4
TOP = 2
TOK_DEV = 128
EXPERTS = 8
CAP = 56
TOKENS = 4096
N_CTX = 4
N_EXP = 8


def route_block(block_key, hot_expert):
    key_pick, key_order, key_flip = jax.random.split(block_key, 3)
    others = EXPERTS - 1
    spare_count = 2 * TOK_DEV - CAP
    chosen = jax.random.permutation(key_pick, others * CAP)[:spare_count]
    other_ids = (chosen // CAP).astype(jnp.int32)
    other_ids = other_ids + (other_ids >= hot_expert).astype(jnp.int32)
    listing = jnp.sort(jnp.concatenate([jnp.full((CAP,), hot_expert, jnp.int32), other_ids]))
    first_half = listing[:TOK_DEV]
    second_half = listing[TOK_DEV:]
    flip_bits = jax.random.randint(key_flip, (TOK_DEV,), 0, 2)
    left_ids = jnp.where(flip_bits == 1, second_half, first_half)
    right_ids = jnp.where(flip_bits == 1, first_half, second_half)
    token_order = jax.random.permutation(key_order, TOK_DEV)
    return jnp.stack([left_ids[token_order], right_ids[token_order]], axis=1)


def draw_routes(key, part):
    key = jax.random.fold_in(key, 11)
    block_count = TOKENS // TOK_DEV
    hot_group = jax.random.randint(jax.random.fold_in(key, 1), (block_count // N_EXP,), 0, EXPERTS)
    hot_block = jnp.repeat(hot_group, N_EXP).astype(jnp.int32)
    block_keys = jax.random.split(jax.random.fold_in(key, 2), block_count)
    picked = jax.vmap(route_block)(block_keys, hot_block)
    return picked.reshape(TOKENS, 2).astype(jnp.int32)


def levels(rng, dims, cuts, smallest, top_value):
    def one(axis_at, shards_of):
        heights = jax.random.uniform(jax.random.fold_in(jax.random.fold_in(rng, 6), axis_at), (shards_of,), jnp.float32, smallest / len(cuts), top_value / len(cuts))
        return jnp.repeat(jnp.exp(heights), dims[axis_at] // shards_of).reshape((-1,) + (1,) * (len(dims) - axis_at - 1))

    level = one(*cuts[0])
    for cut in cuts[1:]:
        level = level * one(*cut)
    return level


def bell_draw(stream_key, extent, scale, reach, shards=(), kind=jnp.bfloat16):
    factor_of = levels(stream_key, extent, shards, -0.22, 0.18) if shards else 1.0
    entries = jax.random.normal(stream_key, extent, jnp.float32) * scale * factor_of
    return jnp.minimum(jnp.maximum(entries, -reach), reach).astype(kind)


def setup_inputs(seed: int = 0) -> dict:
    key_list = jax.random.split(jax.random.key(seed), 12)
    return {
        "out_grad": bell_draw(key_list[0], (E, TOKENS), 1.0, 6.0, ((0, 32),)),
        "gate_in": bell_draw(key_list[1], (E, TOKENS), 1.0, 6.0, ((0, 32),)),
        "conv_in": bell_draw(key_list[2], (E, TOKENS), 1.0, 6.0, ((0, 32),)),
        "scan_grad": bell_draw(key_list[3], (E, TOKENS), 1.0, 6.0, ((0, 32),)),
        "conv_weight": bell_draw(key_list[4], (CONV, E), CONV ** -0.5, 3.0, ((1, 32),), jnp.float32),
        "conv_bias": bell_draw(key_list[5], (E,), 0.5, 3.0, ((0, 32),), jnp.float32),
        "skip_scale": jnp.clip(0.5 + 1.0 * jax.random.uniform(key_list[6], (E,), jnp.float32) ** levels(key_list[6], (E,), ((0, 32),), -0.2, 0.2), 0.5, 1.5),
        "projection": bell_draw(key_list[7], (E, D), D ** -0.5, 0.09375, ((0, 32),)),
        "resid_grad": bell_draw(key_list[8], (TOKENS, D), 1.0, 6.0, ((0, 32),)),
        "routes": draw_routes(jax.random.fold_in(key_list[11], 71), 0),
        "gate_probs": jnp.clip(0.05 + 0.9 * jax.random.uniform(key_list[10], (TOKENS, TOP), jnp.float32) ** levels(key_list[10], (TOKENS, TOP), ((0, 32),), -0.2, 0.2), 0.05, 0.95),
    }


def conv_block(pieces):
    out_grad, gate_in, conv_in, scan_grad, conv_weight, conv_bias, skip_scale = pieces
    kernel_taps = conv_weight.shape[0]
    length = conv_in.shape[1]
    gate_value = gate_in.astype(jnp.float32)
    gated = out_grad.astype(jnp.float32) * gate_value * jax.nn.sigmoid(gate_value)
    padded = jnp.pad(conv_in.astype(jnp.float32), ((0, 0), (kernel_taps - 1, 0)))
    pre_act = conv_bias[:, None] + conv_weight[0][:, None] * padded[:, 0:length]
    for tap in range(1, kernel_taps):
        pre_act = pre_act + conv_weight[tap][:, None] * padded[:, tap:tap + length]
    sig_value = jax.nn.sigmoid(pre_act)
    pre_grad = (scan_grad.astype(jnp.float32) + skip_scale[:, None] * gated) * sig_value * (1.0 + pre_act * (1.0 - sig_value))
    back_pad = jnp.pad(pre_grad, ((0, 0), (0, kernel_taps - 1)))
    input_grad = conv_weight[0][:, None] * back_pad[:, kernel_taps - 1:kernel_taps - 1 + length]
    for tap in range(1, kernel_taps):
        start_at = kernel_taps - 1 - tap
        input_grad = input_grad + conv_weight[tap][:, None] * back_pad[:, start_at:start_at + length]
    return input_grad.astype(jnp.bfloat16)


def reference(out_grad, gate_in, conv_in, scan_grad, conv_weight, conv_bias, skip_scale, projection, resid_grad, routes, gate_probs):
    width_blk = E // N_CTX
    shaped = (
        out_grad.reshape(N_CTX, width_blk, TOKENS),
        gate_in.reshape(N_CTX, width_blk, TOKENS),
        conv_in.reshape(N_CTX, width_blk, TOKENS),
        scan_grad.reshape(N_CTX, width_blk, TOKENS),
        conv_weight.reshape(CONV, N_CTX, width_blk).transpose(1, 0, 2),
        conv_bias.reshape(N_CTX, width_blk),
        skip_scale.reshape(N_CTX, width_blk),
    )
    input_grad = lax.map(conv_block, shaped)
    weight_blocks = projection.reshape(N_CTX, width_blk, D)

    def add_block(running, pair):
        grad_block, weight_block = pair
        product = jnp.dot(grad_block.T, weight_block, preferred_element_type=jnp.float32)
        product = lax.optimization_barrier(product.astype(jnp.bfloat16))
        return running + product.astype(jnp.float32), None

    summed, _ = lax.scan(add_block, jnp.zeros((TOKENS, D), jnp.float32), (input_grad, weight_blocks))
    feature_grad = (resid_grad.astype(jnp.float32) + summed).astype(jnp.bfloat16)

    block_count = TOKENS // TOK_DEV
    flat_routes = routes.reshape(block_count, TOK_DEV * TOP)
    onehot = (flat_routes[:, :, None] == jnp.arange(EXPERTS, dtype=jnp.int32)[None, None, :]).astype(jnp.int32)
    before = jnp.cumsum(onehot, axis=1) - onehot
    rank_in = jnp.sum(before * onehot, axis=2).astype(jnp.int32)
    slot_id = flat_routes * CAP + rank_in
    block_base = jnp.arange(block_count, dtype=jnp.int32)[:, None] * (EXPERTS * CAP)
    flat_index = (block_base + slot_id).reshape(-1).astype(jnp.int32)
    values = gate_probs.reshape(block_count, TOK_DEV, TOP)[:, :, :, None] * feature_grad.reshape(block_count, TOK_DEV, 1, D).astype(jnp.float32)
    values = values.astype(jnp.bfloat16).reshape(block_count * TOK_DEV * TOP, D)
    table = jnp.zeros((block_count * EXPERTS * CAP, D), jnp.bfloat16).at[flat_index].set(values)
    table = table.reshape(N_CTX, N_EXP, EXPERTS, CAP, D).transpose(2, 0, 1, 3, 4)
    return table.reshape(EXPERTS, N_CTX * N_EXP * CAP, D)
```

```python
import functools

import jax
import jax.numpy as jnp
from jax import lax
from jax.experimental import pallas as pl
from jax.experimental.pallas import tpu as pltpu
from jax.sharding import PartitionSpec as P

EXP_DEV = 1
FEATURE_CHUNKS = 4
SKEW = 2
VMEM_BYTES = 48 * 1024 * 1024


def sigmoid(value):
    return 0.5 * jnp.tanh(0.5 * value) + 0.5


def conv_kernel(tile, out_grad, gate_in, conv_in, scan_grad, taps, bias, skip, turned, flat):
    channels, length = out_grad.shape
    kernel_taps = taps.shape[1]
    rows_at_once = 16

    def row_group(group, _):
        row_at = pl.multiple_of(group * rows_at_once, rows_at_once)
        rows = pl.ds(row_at, rows_at_once)
        weights = [taps[rows, tap : tap + 1] for tap in range(kernel_taps)]
        bias_value = bias[rows, :]
        skip_value = skip[rows, :]

        def token_tile(step, carry):
            at = pl.multiple_of((length // tile - 1 - step) * tile, tile)
            columns = pl.ds(at, tile)
            gate = gate_in[rows, columns].astype(jnp.float32)
            gated = out_grad[rows, columns].astype(jnp.float32) * gate * sigmoid(gate)
            here = conv_in[rows, columns].astype(jnp.float32)
            before = conv_in[rows, pl.ds(pl.multiple_of(jnp.maximum(at - 128, 0), 128), 128)].astype(jnp.float32)
            before = jnp.where(at > 0, before, 0.0)
            wide = jnp.concatenate([before, here], axis=1)
            pre = bias_value + weights[kernel_taps - 1] * here
            for tap in range(kernel_taps - 1):
                back = kernel_taps - 1 - tap
                pre = pre + weights[tap] * pltpu.roll(wide, back, 1)[:, 128:]
            sig = sigmoid(pre)
            scan = scan_grad[rows, columns].astype(jnp.float32)
            pre_grad = (scan + skip_value * gated) * sig * (1.0 + pre * (1.0 - sig))
            wide_grad = jnp.concatenate([pre_grad, carry], axis=1)
            total = weights[kernel_taps - 1] * pre_grad
            for tap in range(kernel_taps - 1):
                ahead = kernel_taps - 1 - tap
                total = total + weights[tap] * pltpu.roll(wide_grad, tile + 128 - ahead, 1)[:, :tile]
            flat[rows, columns] = total.astype(flat.dtype)
            return pre_grad[:, :128]

        lax.fori_loop(0, length // tile, token_tile, jnp.zeros((rows_at_once, 128), jnp.float32))
        return 0

    lax.fori_loop(0, channels // rows_at_once, row_group, 0)

    def turn(step, _):
        at = pl.multiple_of(step * tile, tile)
        turned[pl.ds(at, tile), :] = flat[:, pl.ds(at, tile)].T
        return 0

    lax.fori_loop(0, length // tile, turn, 0)


def conv_grad(out_grad, gate_in, conv_in, scan_grad, conv_weight, conv_bias, skip_scale):
    channels, length = out_grad.shape
    block = min(128, channels)
    tile = min(512, length)
    whole = pl.BlockSpec((block, length), lambda step: (step, 0))
    return pl.pallas_call(
        functools.partial(conv_kernel, tile),
        grid=(channels // block,),
        in_specs=[whole] * 4
        + [
            pl.BlockSpec((block, conv_weight.shape[0]), lambda step: (step, 0)),
            pl.BlockSpec((block, 1), lambda step: (step, 0)),
            pl.BlockSpec((block, 1), lambda step: (step, 0)),
        ],
        out_specs=pl.BlockSpec((length, block), lambda step: (0, step)),
        out_shape=jax.ShapeDtypeStruct((length, channels), jnp.bfloat16),
        scratch_shapes=[pltpu.VMEM((block, length), jnp.bfloat16)],
        compiler_params=pltpu.CompilerParams(vmem_limit_bytes=VMEM_BYTES),
        cost_estimate=pl.CostEstimate(
            flops=40 * channels * length, bytes_accessed=10 * channels * length, transcendentals=2 * channels * length
        ),
        name="conv_grad",
    )(out_grad, gate_in, conv_in, scan_grad, conv_weight.T, conv_bias[:, None], skip_scale[:, None])


def matmul_kernel(lefts, rights, place, *refs):
    left_refs = refs[:lefts]
    right_refs = refs[lefts : lefts + rights]
    resid = refs[lefts + rights]
    out = refs[lefts + rights + 1]
    per_right = lefts // rights
    depth = left_refs[0].shape[1]
    total = None
    for index, left in enumerate(left_refs):
        right = right_refs[index // per_right]
        part = jnp.dot(
            left[...], right[pl.ds((index % per_right) * depth, depth), :], preferred_element_type=jnp.float32
        )
        total = part if total is None else total + part
    mine = pl.program_id(0) == place[0]
    total = total + jnp.where(mine, resid[...].astype(jnp.float32), 0.0)
    out[...] = total.astype(out.dtype)


def matmul(lefts, rights, resid, place):
    tokens, depth = lefts[0].shape
    wide, width = rights[0].shape
    tile = resid.shape[0]
    flops = 2 * tokens * depth * len(lefts) * width
    moved = 2 * (tokens * depth * len(lefts) + wide * len(rights) * width + tokens * width)
    return pl.pallas_call(
        functools.partial(matmul_kernel, len(lefts), len(rights)),
        grid_spec=pltpu.PrefetchScalarGridSpec(
            num_scalar_prefetch=1,
            grid=(tokens // tile,),
            in_specs=[pl.BlockSpec((tile, depth), lambda step, place: (step, 0))] * len(lefts)
            + [pl.BlockSpec((wide, width), lambda step, place: (0, 0))] * len(rights)
            + [pl.BlockSpec(resid.shape, lambda step, place: (0, 0))],
            out_specs=pl.BlockSpec((tile, width), lambda step, place: (step, 0)),
        ),
        out_shape=jax.ShapeDtypeStruct((tokens, width), jnp.bfloat16),
        compiler_params=pltpu.CompilerParams(vmem_limit_bytes=VMEM_BYTES),
        cost_estimate=pl.CostEstimate(flops=flops, bytes_accessed=moved, transcendentals=0),
        name="partial_product",
    )(place, *lefts, *rights, resid)


def on_device(
    out_grad,
    gate_in,
    conv_in,
    scan_grad,
    conv_weight,
    conv_bias,
    skip_scale,
    projection,
    resid_grad,
    routes,
    gate_probs,
):
    ctx_count = lax.axis_size("ctx")
    exp_count = lax.axis_size("exp")
    chips = exp_count // 2
    ctx_at = lax.axis_index("ctx")
    exp_at = lax.axis_index("exp")
    chip_at = exp_at // 2
    core_at = exp_at % 2
    channels, length = out_grad.shape
    features = projection.shape[1]
    half = features // 2
    width = half // FEATURE_CHUNKS
    tok_rows = resid_grad.shape[0]
    window = tok_rows * exp_count
    tile = 2 * tok_rows

    def to_core(array):
        return lax.ppermute(array, "exp", [(place, place ^ 1) for place in range(exp_count)])

    def to_ctx(array, offset):
        return lax.ppermute(array, "ctx", [(place, place ^ offset) for place in range(ctx_count)])

    def up(array):
        return lax.ppermute(array, "exp", [(place, place + 2) for place in range(exp_count - 2)])

    def down(array):
        return lax.ppermute(array, "exp", [(place + 2, place) for place in range(exp_count - 2)])

    def columns_of(array, core):
        return lax.dynamic_slice_in_dim(array, core * half, half, 1)

    rows_here = columns_of(projection, core_at)
    rows_there = to_core(columns_of(projection, 1 - core_at))
    chip_rows = jnp.concatenate([rows_here, rows_there], axis=0)
    rights = []
    for chunk in range(FEATURE_CHUNKS):
        piece = chip_rows[:, chunk * width : (chunk + 1) * width]
        rights.append([piece] + [to_ctx(piece, offset) for offset in range(1, ctx_count)])

    resid_here = columns_of(resid_grad, core_at)
    resid_there = to_core(columns_of(resid_grad, 1 - core_at))
    resid = jnp.where(
        core_at == 0,
        jnp.concatenate([resid_here, resid_there], axis=0),
        jnp.concatenate([resid_there, resid_here], axis=0),
    )

    packed = jnp.concatenate([routes.T.astype(jnp.float32), gate_probs.T], axis=0)
    packed = lax.all_gather(packed, "exp", axis=0, tiled=False)
    route_width = routes.shape[1]
    all_routes = packed[:, :route_width]
    all_probs = packed[:, route_width:]
    capacity = max(2, 14 * tok_rows // (4 * EXP_DEV * exp_count))
    experts = jnp.stack([exp_at, exp_at ^ 1]).astype(jnp.float32)
    named = all_routes[None] == experts[:, None, None, None]
    hit = jnp.any(named, axis=2)
    prob = jnp.sum(jnp.where(named, all_probs[None], 0.0), axis=2)
    count = hit.astype(jnp.int32)
    rank = jnp.cumsum(count, axis=2) - count
    slot = jnp.where(hit, rank + (jnp.arange(exp_count, dtype=jnp.int32) % 2)[None, :, None] * capacity, -1)
    slot = slot.reshape(2, chips, 1, tile)
    picks = slot == jnp.arange(2 * capacity, dtype=jnp.int32)[None, None, :, None]
    scale = jnp.sum(jnp.where(picks, prob.reshape(2, chips, 1, tile), 0.0), axis=3, keepdims=True)
    picks = picks.astype(jnp.bfloat16)

    turned = conv_grad(out_grad, gate_in, conv_in, scan_grad, conv_weight, conv_bias, skip_scale)
    lefts = []
    for offset in range(ctx_count):
        piece = lax.dynamic_slice_in_dim(turned, (ctx_at ^ offset) * window, window, 0)
        if offset:
            piece = to_ctx(piece, offset)
        lefts += [piece, to_core(piece)]
    if channels < 128:
        lefts = [jnp.concatenate(lefts, axis=1)]
        rights = [[jnp.concatenate(chunk, axis=0)] for chunk in rights]

    place = chip_at.astype(jnp.int32).reshape(1)
    own = []
    for chunk in range(FEATURE_CHUNKS):
        product = matmul(
            lefts, rights[chunk], resid[:, chunk * width : (chunk + 1) * width], place
        )
        own += [product[at * tile : (at + 1) * tile] for at in range(chips)]

    pieces = len(own)
    steps = pieces + SKEW * (chips - 2)

    def pick(options):
        options = [options(place) for place in range(chips)]
        return lax.select_n(chip_at.astype(jnp.int32), *options) if chips > 2 else jnp.where(
            chip_at == 0, options[0], options[1]
        )

    def own_at(index):
        return own[min(max(index, 0), pieces - 1)].astype(jnp.float32)

    ups, downs = [], []

    def received(listing, index):
        index = min(max(index, 0), steps - 1)
        return listing[index].astype(jnp.float32)

    for step in range(steps):
        raising = pick(lambda place: own_at(step - SKEW * place))
        lowering = pick(lambda place: own_at(step - SKEW * (chips - 1 - place)))
        if step >= SKEW:
            raising = raising + ups[step - SKEW].astype(jnp.float32)
            lowering = lowering + downs[step - SKEW].astype(jnp.float32)
        ups.append(up(raising.astype(jnp.bfloat16)))
        downs.append(down(lowering.astype(jnp.bfloat16)))

    rows_own, rows_got = [], []
    for chunk in range(FEATURE_CHUNKS):
        finished = []
        for at in range(chips):
            index = chunk * chips + at
            below = pick(lambda place: received(ups, index + SKEW * (place - 1)))
            above = pick(lambda place: received(downs, index + SKEW * (chips - 2 - place)))
            finished.append((own_at(index) + below + above).astype(jnp.bfloat16))
        grads = jnp.stack(finished)
        rows = jnp.einsum("eist,itf->eisf", picks, grads, preferred_element_type=jnp.float32)
        rows = (rows * scale).astype(jnp.bfloat16).reshape(2, chips * 2 * capacity, width)
        rows_own.append(rows[0])
        rows_got.append(to_core(rows[1]))
    result = jnp.where(
        core_at == 0,
        jnp.concatenate(rows_own + rows_got, axis=1),
        jnp.concatenate(rows_got + rows_own, axis=1),
    )
    return result[None]


def solution(mesh):
    placed = (
        P(("ctx", "exp"), None),
        P(("ctx", "exp"), None),
        P(("ctx", "exp"), None),
        P(("ctx", "exp"), None),
        P(None, ("ctx", "exp")),
        P(("ctx", "exp")),
        P(("ctx", "exp")),
        P(("ctx", "exp"), None),
        P(("ctx", "exp"), None),
        P(("ctx", "exp"), None),
        P(("ctx", "exp"), None),
    )
    return jax.shard_map(
        on_device, mesh=mesh, in_specs=placed, out_specs=P("exp", "ctx", None), check_vma=False
    )
```

```python
import functools

import jax
import jax.numpy as jnp
from jax import lax
from jax.experimental import pallas as pl
from jax.experimental.pallas import tpu as pltpu
from jax.sharding import PartitionSpec as P

EXP_DEV = 1
PIECES = 8
DELAY = 3
VMEM_BYTES = 48 * 1024 * 1024


def conv_kernel(tile, out_grad, gate_in, conv_in, scan_grad, taps, bias, skip, turned, flat):
    channels, length = out_grad.shape
    kernel_taps = taps.shape[1]
    rows_at_once = 16

    def row_group(group, _):
        row_at = pl.multiple_of(group * rows_at_once, rows_at_once)
        rows = pl.ds(row_at, rows_at_once)

        def spread(column):
            return jnp.concatenate([jnp.broadcast_to(column, (rows_at_once, 128))] * (tile // 128), axis=1)

        weights = [spread(taps[rows, tap : tap + 1]) for tap in range(kernel_taps)]
        bias_half = spread(bias[rows, :])
        skip_value = spread(skip[rows, :])
        after = jnp.zeros((rows_at_once, 128), jnp.float32)
        for at in range(length - tile, -1, -tile):
            columns = pl.ds(at, tile)
            gate = 0.5 * gate_in[rows, columns].astype(jnp.float32)
            gated = out_grad[rows, columns].astype(jnp.float32) * (gate + gate * jnp.tanh(gate))
            here = conv_in[rows, columns].astype(jnp.float32)
            if at:
                before = conv_in[rows, pl.ds(at - 128, 128)].astype(jnp.float32)
            else:
                before = jnp.zeros((rows_at_once, 128), jnp.float32)
            wide = jnp.concatenate([before, here], axis=1)
            half = bias_half + weights[kernel_taps - 1] * here
            for tap in range(kernel_taps - 1):
                back = kernel_taps - 1 - tap
                half = half + weights[tap] * pltpu.roll(wide, back, 1)[:, 128:]
            turn = jnp.tanh(half)
            scan = scan_grad[rows, columns].astype(jnp.float32)
            grad = (scan + skip_value * gated) * (1.0 + turn + half * (1.0 - turn * turn))
            wide_grad = jnp.concatenate([grad, after], axis=1)
            total = weights[kernel_taps - 1] * grad
            for tap in range(kernel_taps - 1):
                ahead = kernel_taps - 1 - tap
                total = total + weights[tap] * pltpu.roll(wide_grad, tile + 128 - ahead, 1)[:, :tile]
            flat[rows, columns] = total.astype(flat.dtype)
            after = grad[:, :128]
        return 0

    lax.fori_loop(0, channels // rows_at_once, row_group, 0)
    for at in range(0, length, tile):
        turned[pl.ds(at, tile), :] = flat[:, pl.ds(at, tile)].T


def conv_grad(out_grad, gate_in, conv_in, scan_grad, conv_weight, conv_bias, skip_scale):
    channels, length = out_grad.shape
    block = min(128, channels)
    tile = min(512, length)
    whole = pl.BlockSpec((block, length), lambda step: (step, 0))
    return pl.pallas_call(
        functools.partial(conv_kernel, tile),
        grid=(channels // block,),
        in_specs=[whole] * 4
        + [
            pl.BlockSpec((block, conv_weight.shape[0]), lambda step: (step, 0)),
            pl.BlockSpec((block, 1), lambda step: (step, 0)),
            pl.BlockSpec((block, 1), lambda step: (step, 0)),
        ],
        out_specs=pl.BlockSpec((length, block), lambda step: (0, step)),
        out_shape=jax.ShapeDtypeStruct((length, channels), jnp.bfloat16),
        scratch_shapes=[pltpu.VMEM((block, length), jnp.bfloat16)],
        compiler_params=pltpu.CompilerParams(vmem_limit_bytes=VMEM_BYTES),
        cost_estimate=pl.CostEstimate(
            flops=40 * channels * length, bytes_accessed=10 * channels * length, transcendentals=2 * channels * length
        ),
        name="conv_grad",
    )(out_grad, gate_in, conv_in, scan_grad, 0.5 * conv_weight.T, 0.5 * conv_bias[:, None], skip_scale[:, None])


def matmul_kernel(lefts, rights, place, *refs):
    left_refs = refs[:lefts]
    right_refs = refs[lefts : lefts + rights]
    resid = refs[lefts + rights]
    out = refs[lefts + rights + 1]
    left = jnp.concatenate([ref[...] for ref in left_refs], axis=1)
    right = jnp.concatenate([ref[...] for ref in right_refs], axis=0)
    total = jnp.dot(left, right, preferred_element_type=jnp.float32)
    mine = pl.program_id(0) == place[0]
    total = total + jnp.where(mine, resid[...].astype(jnp.float32), 0.0)
    out[...] = total.astype(out.dtype)


def matmul(lefts, rights, resid, place):
    tokens, depth = lefts[0].shape
    wide, width = rights[0].shape
    tile = resid.shape[0]
    flops = 2 * tokens * depth * len(lefts) * width
    moved = 2 * (tokens * depth * len(lefts) + wide * len(rights) * width + tokens * width)
    return pl.pallas_call(
        functools.partial(matmul_kernel, len(lefts), len(rights)),
        grid_spec=pltpu.PrefetchScalarGridSpec(
            num_scalar_prefetch=1,
            grid=(tokens // tile,),
            in_specs=[pl.BlockSpec((tile, depth), lambda step, place: (step, 0))] * len(lefts)
            + [pl.BlockSpec((wide, width), lambda step, place: (0, 0))] * len(rights)
            + [pl.BlockSpec(resid.shape, lambda step, place: (0, 0))],
            out_specs=pl.BlockSpec((tile, width), lambda step, place: (step, 0)),
        ),
        out_shape=jax.ShapeDtypeStruct((tokens, width), jnp.bfloat16),
        compiler_params=pltpu.CompilerParams(vmem_limit_bytes=VMEM_BYTES),
        cost_estimate=pl.CostEstimate(flops=flops, bytes_accessed=moved, transcendentals=0),
        name="partial_product",
    )(place, *lefts, *rights, resid)


def on_device(
    out_grad,
    gate_in,
    conv_in,
    scan_grad,
    conv_weight,
    conv_bias,
    skip_scale,
    projection,
    resid_grad,
    routes,
    gate_probs,
):
    ctx_count = lax.axis_size("ctx")
    exp_count = lax.axis_size("exp")
    chips = exp_count // 2
    ctx_at = lax.axis_index("ctx")
    exp_at = lax.axis_index("exp")
    chip_at = exp_at // 2
    core_at = exp_at % 2
    channels, length = out_grad.shape
    features = projection.shape[1]
    half = features // 2
    width = half // PIECES
    groups = [1, 1] + [2] * ((PIECES - 2) // 2)
    tok_rows = resid_grad.shape[0]
    window = tok_rows * exp_count
    tile = 2 * tok_rows

    def to_core(array):
        return lax.ppermute(array, "exp", [(place, place ^ 1) for place in range(exp_count)])

    def to_ctx(array, offset):
        return lax.ppermute(array, "ctx", [(place, place ^ offset) for place in range(ctx_count)])

    def swap_chips(array, low, inward=True, outward=True):
        pairs = set()
        for core in (0, 1):
            for near, far in ((low, low + 1), (chips - 1 - low, chips - 2 - low)):
                if inward:
                    pairs.add((2 * near + core, 2 * far + core))
                if outward:
                    pairs.add((2 * far + core, 2 * near + core))
        return lax.ppermute(array, "exp", sorted(pairs))

    def columns_of(array, core):
        return lax.dynamic_slice_in_dim(array, core * half, half, 1)

    rows_here = columns_of(projection, core_at)
    rows_there = to_core(columns_of(projection, 1 - core_at))
    chip_rows = jnp.concatenate([rows_here, rows_there], axis=0)
    rights = []
    at = 0
    for group in groups:
        piece = chip_rows[:, at : at + group * width]
        rights.append([piece] + [to_ctx(piece, offset) for offset in range(1, ctx_count)])
        at += group * width

    resid_here = columns_of(resid_grad, core_at)
    resid_there = to_core(columns_of(resid_grad, 1 - core_at))
    resid = jnp.where(
        core_at == 0,
        jnp.concatenate([resid_here, resid_there], axis=0),
        jnp.concatenate([resid_there, resid_here], axis=0),
    )

    turned = conv_grad(out_grad, gate_in, conv_in, scan_grad, conv_weight, conv_bias, skip_scale)
    turned, rights[0] = lax.optimization_barrier((turned, rights[0]))
    lefts = []
    for offset in range(ctx_count):
        piece = lax.dynamic_slice_in_dim(turned, (ctx_at ^ offset) * window, window, 0)
        if offset:
            piece = to_ctx(piece, offset)
        lefts += [piece, to_core(piece)]
    packed = jnp.concatenate([routes.T.astype(jnp.float32), gate_probs.T], axis=0)
    packed, lefts[0] = lax.optimization_barrier((packed, lefts[0]))
    routed = lax.all_gather(packed, "exp", axis=0, tiled=False)
    routed, lefts = lax.optimization_barrier((routed, lefts))
    if channels < 128:
        lefts = [jnp.concatenate(lefts, axis=1)]
        rights = [[jnp.concatenate(chunk, axis=0)] for chunk in rights]

    route_width = routes.shape[1]
    all_routes = routed[:, :route_width]
    all_probs = routed[:, route_width:]
    capacity = max(2, 14 * tok_rows // (4 * EXP_DEV * exp_count))
    experts = jnp.stack([exp_at, exp_at ^ 1]).astype(jnp.float32)
    named = all_routes[None] == experts[:, None, None, None]
    hit = jnp.any(named, axis=2)
    prob = jnp.sum(jnp.where(named, all_probs[None], 0.0), axis=2)
    count = hit.astype(jnp.int32)
    rank = jnp.cumsum(count, axis=2) - count
    slot = jnp.where(hit, rank + (jnp.arange(exp_count, dtype=jnp.int32) % 2)[None, :, None] * capacity, -1)
    slot = slot.reshape(2, chips, 1, tile)
    picks = slot == jnp.arange(2 * capacity, dtype=jnp.int32)[None, None, :, None]
    scale = jnp.sum(jnp.where(picks, prob.reshape(2, chips, 1, tile), 0.0), axis=3, keepdims=True)
    picks = picks.astype(jnp.bfloat16)

    place = chip_at.astype(jnp.int32).reshape(1)
    own = []
    at = 0
    for group, right in zip(groups, rights):
        product = matmul(lefts, right, resid[:, at : at + group * width], place)
        own += [product[:, part * width : (part + 1) * width] for part in range(group)]
        at += group * width

    middle = chips // 2
    distance = jnp.minimum(chip_at, chips - 1 - chip_at)
    rows_own, rows_got = [], []

    def add(one, other):
        return (one.astype(jnp.float32) + other.astype(jnp.float32)).astype(jnp.bfloat16)

    def finish(grads):
        rows = jnp.einsum("eist,itf->eisf", picks, grads.reshape(chips, tile, width), preferred_element_type=jnp.float32)
        rows = (rows * scale).astype(jnp.bfloat16).reshape(2, chips * 2 * capacity, width)
        rows_own.append(rows[0])
        rows_got.append(to_core(rows[1]))

    hops = middle - 1
    sums = [list(own)] + [[None] * PIECES for _ in range(hops)]
    ready = [[None] * PIECES for _ in range(hops + 1)]
    lag = DELAY - 1
    last = PIECES + lag * hops + DELAY * hops
    for step in range(last + 1):
        for hop in range(hops):
            inward = step - lag * hop
            outward = inward - DELAY - 2 * lag * (hops - 1 - hop)
            send_in = 0 <= inward < PIECES
            send_out = 0 <= outward < PIECES
            if not (send_in or send_out):
                continue
            if send_in and send_out:
                payload = jnp.where(distance == hop, sums[hop][inward], ready[hop + 1][outward])
            else:
                payload = sums[hop][inward] if send_in else ready[hop + 1][outward]
            got = swap_chips(payload, hop, send_in, send_out)
            if send_in:
                sums[hop + 1][inward] = add(sums[hop][inward], got)
                if hop == hops - 1:
                    crossed = swap_chips(sums[hop + 1][inward], middle - 1)
                    ready[hops][inward] = add(sums[hop + 1][inward], crossed)
            if send_out:
                ready[hop][outward] = jnp.where(distance == hop, got, ready[hop + 1][outward])
                if hop == 0:
                    finish(ready[0][outward])
    result = jnp.where(
        core_at == 0,
        jnp.concatenate(rows_own + rows_got, axis=1),
        jnp.concatenate(rows_got + rows_own, axis=1),
    )
    return result[None]


def solution(mesh):
    placed = (
        P(("ctx", "exp"), None),
        P(("ctx", "exp"), None),
        P(("ctx", "exp"), None),
        P(("ctx", "exp"), None),
        P(None, ("ctx", "exp")),
        P(("ctx", "exp")),
        P(("ctx", "exp")),
        P(("ctx", "exp"), None),
        P(("ctx", "exp"), None),
        P(("ctx", "exp"), None),
        P(("ctx", "exp"), None),
    )
    return jax.shard_map(
        on_device, mesh=mesh, in_specs=placed, out_specs=P("exp", "ctx", None), check_vma=False
    )
```

```python
import functools

import jax
import jax.numpy as jnp
from jax import lax
from jax.experimental import pallas as pl
from jax.experimental.pallas import tpu as pltpu
from jax.sharding import PartitionSpec as P

EXP_DEV = 1
GROUPS = ((1,), (1, 2), (2, 2), (2, 2), (2, 1, 1))
UNITS = sum(map(sum, GROUPS))
DELAY = 3
VMEM_BYTES = 48 * 1024 * 1024


def conv_kernel(tile, out_grad, gate_in, conv_in, scan_grad, taps, bias, skip, turned, flat):
    channels, length = out_grad.shape
    kernel_taps = taps.shape[1]
    rows_at_once = 16

    def row_group(group, _):
        row_at = pl.multiple_of(group * rows_at_once, rows_at_once)
        rows = pl.ds(row_at, rows_at_once)

        def spread(column):
            return jnp.concatenate([jnp.broadcast_to(column, (rows_at_once, 128))] * (tile // 128), axis=1)

        weights = [spread(taps[rows, tap : tap + 1]) for tap in range(kernel_taps)]
        bias_half = spread(bias[rows, :])
        skip_value = spread(skip[rows, :])
        after = jnp.zeros((rows_at_once, 128), jnp.float32)
        for at in range(length - tile, -1, -tile):
            columns = pl.ds(at, tile)
            gate = 0.5 * gate_in[rows, columns].astype(jnp.float32)
            gated = out_grad[rows, columns].astype(jnp.float32) * (gate + gate * jnp.tanh(gate))
            here = conv_in[rows, columns].astype(jnp.float32)
            if at:
                before = conv_in[rows, pl.ds(at - 128, 128)].astype(jnp.float32)
            else:
                before = jnp.zeros((rows_at_once, 128), jnp.float32)
            wide = jnp.concatenate([before, here], axis=1)
            half = bias_half + weights[kernel_taps - 1] * here
            for tap in range(kernel_taps - 1):
                back = kernel_taps - 1 - tap
                half = half + weights[tap] * pltpu.roll(wide, back, 1)[:, 128:]
            turn = jnp.tanh(half)
            scan = scan_grad[rows, columns].astype(jnp.float32)
            grad = (scan + skip_value * gated) * (1.0 + turn + half * (1.0 - turn * turn))
            wide_grad = jnp.concatenate([grad, after], axis=1)
            total = weights[kernel_taps - 1] * grad
            for tap in range(kernel_taps - 1):
                ahead = kernel_taps - 1 - tap
                total = total + weights[tap] * pltpu.roll(wide_grad, tile + 128 - ahead, 1)[:, :tile]
            flat[rows, columns] = total.astype(flat.dtype)
            after = grad[:, :128]
        return 0

    lax.fori_loop(0, channels // rows_at_once, row_group, 0)
    for at in range(0, length, tile):
        turned[pl.ds(at, tile), :] = flat[:, pl.ds(at, tile)].T


def conv_grad(part, parts, out_grad, gate_in, conv_in, scan_grad, taps_half, bias_half, skip):
    channels, length = out_grad.shape
    block = channels // parts
    tile = min(512, length)
    whole = pl.BlockSpec((block, length), lambda step: (part, 0))
    column = pl.BlockSpec((block, 1), lambda step: (part, 0))
    return pl.pallas_call(
        functools.partial(conv_kernel, tile),
        grid=(1,),
        in_specs=[whole] * 4 + [pl.BlockSpec((block, taps_half.shape[1]), lambda step: (part, 0)), column, column],
        out_specs=pl.BlockSpec((length, block), lambda step: (0, 0)),
        out_shape=jax.ShapeDtypeStruct((length, block), jnp.bfloat16),
        scratch_shapes=[pltpu.VMEM((block, length), jnp.bfloat16)],
        compiler_params=pltpu.CompilerParams(vmem_limit_bytes=VMEM_BYTES),
        cost_estimate=pl.CostEstimate(
            flops=40 * block * length, bytes_accessed=10 * block * length, transcendentals=2 * block * length
        ),
        name="conv_grad",
    )(out_grad, gate_in, conv_in, scan_grad, taps_half, bias_half, skip)


def matmul_kernel(lefts, rights, place, *refs):
    left_refs = refs[:lefts]
    right_refs = refs[lefts : lefts + rights]
    resid = refs[lefts + rights]
    outs = refs[lefts + rights + 1 :]
    left = jnp.concatenate([ref[...] for ref in left_refs], axis=1)
    right = jnp.concatenate([ref[...] for ref in right_refs], axis=0)
    total = jnp.dot(left, right, preferred_element_type=jnp.float32)
    mine = pl.program_id(0) == place[0]
    total = total + jnp.where(mine, resid[...].astype(jnp.float32), 0.0)
    at = 0
    for out in outs:
        out[...] = total[:, at : at + out.shape[1]].astype(out.dtype)
        at += out.shape[1]


def matmul(lefts, rights, resid, place, widths):
    tokens, depth = lefts[0].shape
    wide, width = rights[0].shape
    tile = resid.shape[0]
    flops = 2 * tokens * depth * len(lefts) * width
    moved = 2 * (tokens * depth * len(lefts) + wide * len(rights) * width + tokens * width)
    return pl.pallas_call(
        functools.partial(matmul_kernel, len(lefts), len(rights)),
        grid_spec=pltpu.PrefetchScalarGridSpec(
            num_scalar_prefetch=1,
            grid=(tokens // tile,),
            in_specs=[pl.BlockSpec((tile, depth), lambda step, place: (step, 0))] * len(lefts)
            + [pl.BlockSpec((wide, width), lambda step, place: (0, 0))] * len(rights)
            + [pl.BlockSpec(resid.shape, lambda step, place: (0, 0))],
            out_specs=[pl.BlockSpec((tile, part), lambda step, place: (step, 0)) for part in widths],
        ),
        out_shape=[jax.ShapeDtypeStruct((tokens, part), jnp.bfloat16) for part in widths],
        compiler_params=pltpu.CompilerParams(vmem_limit_bytes=VMEM_BYTES),
        cost_estimate=pl.CostEstimate(flops=flops, bytes_accessed=moved, transcendentals=0),
        name="partial_product",
    )(place, *lefts, *rights, resid)


def on_device(
    out_grad,
    gate_in,
    conv_in,
    scan_grad,
    conv_weight,
    conv_bias,
    skip_scale,
    projection,
    resid_grad,
    routes,
    gate_probs,
):
    ctx_count = lax.axis_size("ctx")
    exp_count = lax.axis_size("exp")
    chips = exp_count // 2
    ctx_at = lax.axis_index("ctx")
    exp_at = lax.axis_index("exp")
    chip_at = exp_at // 2
    core_at = exp_at % 2
    channels, length = out_grad.shape
    features = projection.shape[1]
    half = features // 2
    unit = half // UNITS
    widths = [[unit * part for part in group] for group in GROUPS]
    starts = [sum(map(sum, widths[:at])) for at in range(len(widths))]
    tok_rows = resid_grad.shape[0]
    window = tok_rows * exp_count
    tile = 2 * tok_rows

    def to_core(array):
        return lax.ppermute(array, "exp", [(place, place ^ 1) for place in range(exp_count)])

    def to_ctx(array, offset):
        return lax.ppermute(array, "ctx", [(place, place ^ offset) for place in range(ctx_count)])

    def swap_chips(array, low, inward=True, outward=True):
        pairs = set()
        for core in (0, 1):
            for near, far in ((low, low + 1), (chips - 1 - low, chips - 2 - low)):
                if inward:
                    pairs.add((2 * near + core, 2 * far + core))
                if outward:
                    pairs.add((2 * far + core, 2 * near + core))
        return lax.ppermute(array, "exp", sorted(pairs))

    def columns_of(array, core, at, width):
        return lax.dynamic_slice_in_dim(array, core * half + at, width, 1)

    def both_cores(array, at, width):
        here = columns_of(array, core_at, at, width)
        return here, to_core(columns_of(array, 1 - core_at, at, width))

    def spread(piece):
        return [piece] + [to_ctx(piece, offset) for offset in range(1, ctx_count)]

    first = sum(widths[0])
    rights = [spread(jnp.concatenate(both_cores(projection, 0, first), axis=0))]

    parts = 2 if channels % 256 == 0 else 1
    conv_args = [0.5 * conv_weight.T, 0.5 * conv_bias[:, None], skip_scale[:, None]]
    lefts = []
    routed = None
    packed = jnp.concatenate([routes.T.astype(jnp.float32), gate_probs.T], axis=0)
    for part in range(parts):
        if part == parts - 1:
            scan_grad, rights[0] = lax.optimization_barrier((scan_grad, rights[0]))
        turned = conv_grad(part, parts, out_grad, gate_in, conv_in, scan_grad, *conv_args)
        mine = [lax.dynamic_slice_in_dim(turned, (ctx_at ^ offset) * window, window, 0) for offset in range(ctx_count)]
        mine = mine[:1] + [to_ctx(mine[offset], offset) for offset in range(1, ctx_count)]
        if part == parts - 1:
            packed, projection, resid_grad, turned = lax.optimization_barrier((packed, projection, resid_grad, turned))
            routed = lax.all_gather(packed, "exp", axis=0, tiled=False)
            routed, mine[0] = lax.optimization_barrier((routed, mine[0]))
        for piece in mine:
            lefts.append((piece, to_core(piece)))

    rest_here, rest_there = both_cores(projection, first, half - first)
    for group, at in list(zip(widths, starts))[1:]:
        cut = slice(at - first, at - first + sum(group))
        rights.append(spread(jnp.concatenate([rest_here[:, cut], rest_there[:, cut]], axis=0)))
    resid_here, resid_there = both_cores(resid_grad, 0, half)
    resid = jnp.where(
        core_at == 0,
        jnp.concatenate([resid_here, resid_there], axis=0),
        jnp.concatenate([resid_there, resid_here], axis=0),
    )

    route_width = routes.shape[1]
    all_routes = routed[:, :route_width]
    all_probs = routed[:, route_width:]
    capacity = max(2, 14 * tok_rows // (4 * EXP_DEV * exp_count))
    experts = jnp.stack([exp_at, exp_at ^ 1]).astype(jnp.float32)
    named = all_routes[None] == experts[:, None, None, None]
    hit = jnp.any(named, axis=2)
    prob = jnp.sum(jnp.where(named, all_probs[None], 0.0), axis=2)
    count = hit.astype(jnp.int32)
    rank = jnp.cumsum(count, axis=2) - count
    slot = jnp.where(hit, rank + (jnp.arange(exp_count, dtype=jnp.int32) % 2)[None, :, None] * capacity, -1)
    slot = slot.reshape(2, chips, 1, tile)
    picks = slot == jnp.arange(2 * capacity, dtype=jnp.int32)[None, None, :, None]
    scale = jnp.sum(jnp.where(picks, prob.reshape(2, chips, 1, tile), 0.0), axis=3, keepdims=True)
    picks = picks.astype(jnp.bfloat16)
    picks, scale, lefts = lax.optimization_barrier((picks, scale, lefts))

    lefts = [
        lefts[part * ctx_count + offset][core]
        for offset in range(ctx_count)
        for core in (0, 1)
        for part in range(parts)
    ]
    if channels < 128:
        lefts = [jnp.concatenate(lefts, axis=1)]
        rights = [[jnp.concatenate(chunk, axis=0)] for chunk in rights]
    place = chip_at.astype(jnp.int32).reshape(1)
    own = []
    for group, at, right in zip(widths, starts, rights):
        own += matmul(lefts, right, resid[:, at : at + sum(group)], place, group)
    pieces = len(own)

    middle = chips // 2
    distance = jnp.minimum(chip_at, chips - 1 - chip_at)
    rows_own, rows_got = [], []

    def add(one, other):
        return (one.astype(jnp.float32) + other.astype(jnp.float32)).astype(jnp.bfloat16)

    def finish(grads):
        width = grads.shape[1]
        rows = jnp.einsum("eist,itf->eisf", picks, grads.reshape(chips, tile, width), preferred_element_type=jnp.float32)
        rows = (rows * scale).astype(jnp.bfloat16).reshape(2, chips * 2 * capacity, width)
        rows_own.append(rows[0])
        rows_got.append(to_core(rows[1]))

    hops = middle - 1
    sums = [list(own)] + [[None] * pieces for _ in range(hops)]
    ready = [[None] * pieces for _ in range(hops + 1)]
    lag = DELAY - 1
    last = pieces + lag * hops + DELAY * hops
    for step in range(last + 1):
        for hop in range(hops):
            inward = step - lag * hop
            outward = inward - DELAY - 2 * lag * (hops - 1 - hop)
            send_in = 0 <= inward < pieces
            send_out = 0 <= outward < pieces
            if send_in and 0 <= inward - 2:
                sums[hop][inward], sums[hop + 1][inward - 2] = lax.optimization_barrier(
                    (sums[hop][inward], sums[hop + 1][inward - 2])
                )
            rising = sums[hop][inward] if send_in else None
            falling = ready[hop + 1][outward] if send_out else None
            if send_in and send_out and rising.shape == falling.shape:
                got_in = got_out = swap_chips(jnp.where(distance == hop, rising, falling), hop)
            else:
                got_in = swap_chips(rising, hop, True, False) if send_in else None
                got_out = swap_chips(falling, hop, False, True) if send_out else None
            if send_in:
                sums[hop + 1][inward] = add(rising, got_in)
                if hop == hops - 1:
                    crossed = swap_chips(sums[hop + 1][inward], middle - 1)
                    ready[hops][inward] = add(sums[hop + 1][inward], crossed)
            if send_out:
                ready[hop][outward] = jnp.where(distance == hop, got_out, falling)
                if hop == 0:
                    finish(ready[0][outward])
    result = jnp.where(
        core_at == 0,
        jnp.concatenate(rows_own + rows_got, axis=1),
        jnp.concatenate(rows_got + rows_own, axis=1),
    )
    return result[None]


def solution(mesh):
    placed = (
        P(("ctx", "exp"), None),
        P(("ctx", "exp"), None),
        P(("ctx", "exp"), None),
        P(("ctx", "exp"), None),
        P(None, ("ctx", "exp")),
        P(("ctx", "exp")),
        P(("ctx", "exp")),
        P(("ctx", "exp"), None),
        P(("ctx", "exp"), None),
        P(("ctx", "exp"), None),
        P(("ctx", "exp"), None),
    )
    return jax.shard_map(
        on_device, mesh=mesh, in_specs=placed, out_specs=P("exp", "ctx", None), check_vma=False
    )
```

```python
import functools

import jax
import jax.numpy as jnp
from jax import lax
from jax.experimental import pallas as pl
from jax.experimental.pallas import tpu as pltpu
from jax.sharding import PartitionSpec as P

EXP_DEV = 1
GROUPS = ((1,), (1,), (1, 1), (1, 1), (1, 1))
UNITS = sum(map(sum, GROUPS))
DELAY = 3
VMEM_BYTES = 60 * 1024 * 1024


def conv_kernel(tile, out_grad, gate_in, conv_in, scan_grad, taps, bias, skip, turned, flat):
    channels, length = out_grad.shape
    kernel_taps = taps.shape[1]
    rows_at_once = 16

    def row_group(group, _):
        row_at = pl.multiple_of(group * rows_at_once, rows_at_once)
        rows = pl.ds(row_at, rows_at_once)

        def spread(column):
            return jnp.concatenate([jnp.broadcast_to(column, (rows_at_once, 128))] * (tile // 128), axis=1)

        weights = [spread(taps[rows, tap : tap + 1]) for tap in range(kernel_taps)]
        bias_half = spread(bias[rows, :])
        skip_value = spread(skip[rows, :])
        after = jnp.zeros((rows_at_once, 128), jnp.float32)
        for at in range(length - tile, -1, -tile):
            columns = pl.ds(at, tile)
            gate = 0.5 * gate_in[rows, columns].astype(jnp.float32)
            gated = out_grad[rows, columns].astype(jnp.float32) * (gate + gate * jnp.tanh(gate))
            here = conv_in[rows, columns].astype(jnp.float32)
            if at:
                before = conv_in[rows, pl.ds(at - 128, 128)].astype(jnp.float32)
            else:
                before = jnp.zeros((rows_at_once, 128), jnp.float32)
            wide = jnp.concatenate([before, here], axis=1)
            half = bias_half + weights[kernel_taps - 1] * here
            for tap in range(kernel_taps - 1):
                back = kernel_taps - 1 - tap
                half = half + weights[tap] * pltpu.roll(wide, back, 1)[:, 128:]
            turn = jnp.tanh(half)
            scan = scan_grad[rows, columns].astype(jnp.float32)
            grad = (scan + skip_value * gated) * (1.0 + turn + half * (1.0 - turn * turn))
            wide_grad = jnp.concatenate([grad, after], axis=1)
            total = weights[kernel_taps - 1] * grad
            for tap in range(kernel_taps - 1):
                ahead = kernel_taps - 1 - tap
                total = total + weights[tap] * pltpu.roll(wide_grad, tile + 128 - ahead, 1)[:, :tile]
            flat[rows, columns] = total.astype(flat.dtype)
            after = grad[:, :128]
        return 0

    lax.fori_loop(0, channels // rows_at_once, row_group, 0)
    for at in range(0, length, tile):
        turned[pl.ds(at, tile), :] = flat[:, pl.ds(at, tile)].T


def conv_grad(out_grad, gate_in, conv_in, scan_grad, taps_half, bias_half, skip):
    channels, length = out_grad.shape
    block = min(128, channels)
    tile = min(512, length)
    whole = pl.BlockSpec((block, length), lambda step: (step, 0))
    column = pl.BlockSpec((block, 1), lambda step: (step, 0))
    return pl.pallas_call(
        functools.partial(conv_kernel, tile),
        grid=(channels // block,),
        in_specs=[whole] * 4 + [pl.BlockSpec((block, taps_half.shape[1]), lambda step: (step, 0)), column, column],
        out_specs=pl.BlockSpec((length, block), lambda step: (0, step)),
        out_shape=jax.ShapeDtypeStruct((length, channels), jnp.bfloat16),
        scratch_shapes=[pltpu.VMEM((block, length), jnp.bfloat16)],
        compiler_params=pltpu.CompilerParams(vmem_limit_bytes=VMEM_BYTES),
        cost_estimate=pl.CostEstimate(
            flops=40 * channels * length, bytes_accessed=10 * channels * length, transcendentals=2 * channels * length
        ),
        name="conv_grad",
    )(out_grad, gate_in, conv_in, scan_grad, taps_half, bias_half, skip)


def matmul_kernel(lefts, rights, place, *refs):
    left_refs = refs[:lefts]
    right_refs = refs[lefts : lefts + rights]
    resid = refs[lefts + rights]
    outs = refs[lefts + rights + 1 :]
    left = jnp.concatenate([ref[...] for ref in left_refs], axis=1)
    right = jnp.concatenate([ref[...] for ref in right_refs], axis=0)
    total = jnp.dot(left, right, preferred_element_type=jnp.float32)
    mine = pl.program_id(0) == place[0]
    total = total + jnp.where(mine, resid[...].astype(jnp.float32), 0.0)
    at = 0
    for out in outs:
        out[...] = total[:, at : at + out.shape[1]].astype(out.dtype)
        at += out.shape[1]


def matmul(lefts, rights, resid, place, widths):
    tokens, depth = lefts[0].shape
    wide, width = rights[0].shape
    tile = resid.shape[0]
    flops = 2 * tokens * depth * len(lefts) * width
    moved = 2 * (tokens * depth * len(lefts) + wide * len(rights) * width + tokens * width)
    return pl.pallas_call(
        functools.partial(matmul_kernel, len(lefts), len(rights)),
        grid_spec=pltpu.PrefetchScalarGridSpec(
            num_scalar_prefetch=1,
            grid=(tokens // tile,),
            in_specs=[pl.BlockSpec((tile, depth), lambda step, place: (step, 0))] * len(lefts)
            + [pl.BlockSpec((wide, width), lambda step, place: (0, 0))] * len(rights)
            + [pl.BlockSpec(resid.shape, lambda step, place: (0, 0))],
            out_specs=[pl.BlockSpec((tile, part), lambda step, place: (step, 0)) for part in widths],
        ),
        out_shape=[jax.ShapeDtypeStruct((tokens, part), jnp.bfloat16) for part in widths],
        compiler_params=pltpu.CompilerParams(vmem_limit_bytes=VMEM_BYTES),
        cost_estimate=pl.CostEstimate(flops=flops, bytes_accessed=moved, transcendentals=0),
        name="partial_product",
    )(place, *lefts, *rights, resid)


def on_device(
    out_grad,
    gate_in,
    conv_in,
    scan_grad,
    conv_weight,
    conv_bias,
    skip_scale,
    projection,
    resid_grad,
    routes,
    gate_probs,
):
    ctx_count = lax.axis_size("ctx")
    exp_count = lax.axis_size("exp")
    chips = exp_count // 2
    ctx_at = lax.axis_index("ctx")
    exp_at = lax.axis_index("exp")
    chip_at = exp_at // 2
    core_at = exp_at % 2
    channels, length = out_grad.shape
    features = projection.shape[1]
    half = features // 2
    unit = half // UNITS
    widths = [[unit * part for part in group] for group in GROUPS]
    starts = [sum(map(sum, widths[:at])) for at in range(len(widths))]
    tok_rows = resid_grad.shape[0]
    window = tok_rows * exp_count
    tile = 2 * tok_rows

    def to_core(array):
        return lax.ppermute(array, "exp", [(place, place ^ 1) for place in range(exp_count)])

    def to_ctx(array, offset):
        return lax.ppermute(array, "ctx", [(place, place ^ offset) for place in range(ctx_count)])

    def swap_chips(array, low, inward=True, outward=True):
        pairs = set()
        for core in (0, 1):
            for near, far in ((low, low + 1), (chips - 1 - low, chips - 2 - low)):
                if inward:
                    pairs.add((2 * near + core, 2 * far + core))
                if outward:
                    pairs.add((2 * far + core, 2 * near + core))
        return lax.ppermute(array, "exp", sorted(pairs))

    def columns_of(array, core, at, width):
        return lax.dynamic_slice_in_dim(array, core * half + at, width, 1)

    def both_cores(array, at, width):
        here = columns_of(array, core_at, at, width)
        return here, to_core(columns_of(array, 1 - core_at, at, width))

    def spread(piece):
        return [piece] + [to_ctx(piece, offset) for offset in range(1, ctx_count)]

    first = sum(widths[0])
    rights = [spread(jnp.concatenate(both_cores(projection, 0, first), axis=0))]

    turned = conv_grad(
        out_grad,
        gate_in,
        conv_in,
        scan_grad,
        0.5 * conv_weight.T,
        0.5 * conv_bias[:, None],
        skip_scale[:, None],
    )
    turned, rights[0], projection, resid_grad, routes = lax.optimization_barrier(
        (turned, rights[0], projection, resid_grad, routes)
    )
    lefts = []
    for offset in range(ctx_count):
        piece = lax.dynamic_slice_in_dim(turned, (ctx_at ^ offset) * window, window, 0)
        if offset:
            piece = to_ctx(piece, offset)
        lefts += [piece, to_core(piece)]

    routed = jnp.concatenate([routes.T.astype(jnp.float32), gate_probs.T], axis=0)[None]
    offset = 1
    while offset < exp_count:
        other = lax.ppermute(routed, "exp", [(place, place ^ offset) for place in range(exp_count)])
        routed = jnp.concatenate([routed, other], axis=0)
        offset *= 2
    order = (jnp.arange(exp_count)[:, None] ^ exp_at) == jnp.arange(exp_count)[None, :]
    routed = jnp.sum(jnp.where(order[:, :, None, None], routed[None], 0.0), axis=1)

    rest_here, rest_there = both_cores(projection, first, half - first)
    for group, at in list(zip(widths, starts))[1:]:
        cut = slice(at - first, at - first + sum(group))
        rights.append(spread(jnp.concatenate([rest_here[:, cut], rest_there[:, cut]], axis=0)))
    resid_here, resid_there = both_cores(resid_grad, 0, half)
    resid = jnp.where(
        core_at == 0,
        jnp.concatenate([resid_here, resid_there], axis=0),
        jnp.concatenate([resid_there, resid_here], axis=0),
    )

    route_width = routes.shape[1]
    all_routes = routed[:, :route_width]
    all_probs = routed[:, route_width:]
    capacity = max(2, 14 * tok_rows // (4 * EXP_DEV * exp_count))
    experts = jnp.stack([exp_at, exp_at ^ 1]).astype(jnp.float32)
    named = all_routes[None] == experts[:, None, None, None]
    hit = jnp.any(named, axis=2)
    prob = jnp.sum(jnp.where(named, all_probs[None], 0.0), axis=2)
    count = hit.astype(jnp.int32)
    rank = jnp.cumsum(count, axis=2) - count
    slot = jnp.where(hit, rank + (jnp.arange(exp_count, dtype=jnp.int32) % 2)[None, :, None] * capacity, -1)
    slot = slot.reshape(2, chips, 1, tile)
    picks = slot == jnp.arange(2 * capacity, dtype=jnp.int32)[None, None, :, None]
    scale = jnp.sum(jnp.where(picks, prob.reshape(2, chips, 1, tile), 0.0), axis=3, keepdims=True)
    picks = picks.astype(jnp.bfloat16)
    picks, scale, lefts = lax.optimization_barrier((picks, scale, lefts))

    if channels < 128:
        lefts = [jnp.concatenate(lefts, axis=1)]
        rights = [[jnp.concatenate(chunk, axis=0)] for chunk in rights]
    place = chip_at.astype(jnp.int32).reshape(1)
    pieces = sum(map(len, GROUPS))

    middle = chips // 2
    distance = jnp.minimum(chip_at, chips - 1 - chip_at)
    rows_own, rows_got = [], []

    def add(one, other):
        return (one.astype(jnp.float32) + other.astype(jnp.float32)).astype(jnp.bfloat16)

    def finish(grads):
        width = grads.shape[1]
        rows = jnp.einsum("eist,itf->eisf", picks, grads.reshape(chips, tile, width), preferred_element_type=jnp.float32)
        rows = (rows * scale).astype(jnp.bfloat16).reshape(2, chips * 2 * capacity, width)
        rows_own.append(rows[0])
        rows_got.append(to_core(rows[1]))

    hops = middle - 1
    sums = [[None] * pieces for _ in range(hops + 1)]
    ready = [[None] * pieces for _ in range(hops + 1)]
    lag = DELAY - 1
    last = pieces + lag * hops + DELAY * hops
    group_at = 0
    first_of = [sum(map(len, GROUPS[:at])) for at in range(len(GROUPS))]
    for step in range(last + 1):
        if group_at < len(GROUPS) and first_of[group_at] == step:
            if step >= 2:
                sums[1][step - 2], place = lax.optimization_barrier((sums[1][step - 2], place))
            group, at = widths[group_at], starts[group_at]
            products = matmul(lefts, rights[group_at], resid[:, at : at + sum(group)], place, group)
            sums[0][step : step + len(group)] = products
            group_at += 1
        for hop in range(hops):
            inward = step - lag * hop
            outward = inward - DELAY - 2 * lag * (hops - 1 - hop)
            send_in = 0 <= inward < pieces
            send_out = 0 <= outward < pieces
            if not (send_in or send_out):
                continue
            if send_in and 0 <= inward - 2:
                sums[hop][inward], sums[hop + 1][inward - 2] = lax.optimization_barrier(
                    (sums[hop][inward], sums[hop + 1][inward - 2])
                )
            rising = sums[hop][inward] if send_in else None
            falling = ready[hop + 1][outward] if send_out else None
            if send_in and send_out:
                got = swap_chips(jnp.where(distance == hop, rising, falling), hop)
            else:
                got = swap_chips(rising if send_in else falling, hop, send_in, send_out)
            if send_in:
                sums[hop + 1][inward] = add(rising, got)
                if hop == hops - 1:
                    crossed = swap_chips(sums[hop + 1][inward], middle - 1)
                    ready[hops][inward] = add(sums[hop + 1][inward], crossed)
            if send_out:
                ready[hop][outward] = jnp.where(distance == hop, got, falling)
                if hop == 0:
                    finish(ready[0][outward])
    result = jnp.where(
        core_at == 0,
        jnp.concatenate(rows_own + rows_got, axis=1),
        jnp.concatenate(rows_got + rows_own, axis=1),
    )
    return result[None]


def solution(mesh):
    placed = (
        P(("ctx", "exp"), None),
        P(("ctx", "exp"), None),
        P(("ctx", "exp"), None),
        P(("ctx", "exp"), None),
        P(None, ("ctx", "exp")),
        P(("ctx", "exp")),
        P(("ctx", "exp")),
        P(("ctx", "exp"), None),
        P(("ctx", "exp"), None),
        P(("ctx", "exp"), None),
        P(("ctx", "exp"), None),
    )
    return jax.shard_map(
        on_device, mesh=mesh, in_specs=placed, out_specs=P("exp", "ctx", None), check_vma=False
    )
```

```python
import functools

import jax
import jax.numpy as jnp
from jax import lax
from jax.experimental import pallas as pl
from jax.experimental.pallas import tpu as pltpu
from jax.sharding import PartitionSpec as P

EXP_DEV = 1
GROUPS = ((1, 1), (1, 1), (1, 1), (1, 1))
UNITS = sum(map(sum, GROUPS))
DELAY = 3
VMEM_BYTES = 60 * 1024 * 1024


def conv_kernel(tile, at_ctx, out_grad, gate_in, conv_in, scan_grad, taps, bias, skip, *refs):
    turned, flat, columns_of = refs[:-2], refs[-2], refs[-1]
    channels, length = out_grad.shape
    window = length // len(turned)
    kernel_taps = taps.shape[0]
    rows_at_once = 16
    settings = jnp.concatenate(
        [0.5 * taps[...], 0.5 * bias[...], skip[...], jnp.zeros((8 - kernel_taps - 2, channels), jnp.float32)], axis=0
    )
    columns_of[...] = settings.T

    def row_group(group, _):
        row_at = pl.multiple_of(group * rows_at_once, rows_at_once)
        rows = pl.ds(row_at, rows_at_once)

        def spread(index):
            column = jnp.broadcast_to(columns_of[rows, index : index + 1], (rows_at_once, 128))
            return jnp.concatenate([column] * (tile // 128), axis=1)

        weights = [spread(tap) for tap in range(kernel_taps)]
        bias_half = spread(kernel_taps)
        skip_value = spread(kernel_taps + 1)
        after = jnp.zeros((rows_at_once, 128), jnp.float32)
        for at in range(length - tile, -1, -tile):
            columns = pl.ds(at, tile)
            gate = 0.5 * gate_in[rows, columns].astype(jnp.float32)
            gated = out_grad[rows, columns].astype(jnp.float32) * (gate + gate * jnp.tanh(gate))
            here = conv_in[rows, columns].astype(jnp.float32)
            if at:
                before = conv_in[rows, pl.ds(at - 128, 128)].astype(jnp.float32)
            else:
                before = jnp.zeros((rows_at_once, 128), jnp.float32)
            wide = jnp.concatenate([before, here], axis=1)
            half = bias_half + weights[kernel_taps - 1] * here
            for tap in range(kernel_taps - 1):
                back = kernel_taps - 1 - tap
                half = half + weights[tap] * pltpu.roll(wide, back, 1)[:, 128:]
            turn = jnp.tanh(half)
            scan = scan_grad[rows, columns].astype(jnp.float32)
            grad = (scan + skip_value * gated) * (1.0 + turn + half * (1.0 - turn * turn))
            wide_grad = jnp.concatenate([grad, after], axis=1)
            total = weights[kernel_taps - 1] * grad
            for tap in range(kernel_taps - 1):
                ahead = kernel_taps - 1 - tap
                total = total + weights[tap] * pltpu.roll(wide_grad, tile + 128 - ahead, 1)[:, :tile]
            flat[rows, columns] = total.astype(flat.dtype)
            after = grad[:, :128]
        return 0

    lax.fori_loop(0, channels // rows_at_once, row_group, 0)
    for offset, out in enumerate(turned):
        from_at = (at_ctx[0] ^ offset) * window
        for at in range(0, window, tile):
            out[pl.ds(at, tile), :] = flat[:, pl.ds(pl.multiple_of(from_at + at, tile), tile)].T


def conv_grad(at_ctx, ctx_count, out_grad, gate_in, conv_in, scan_grad, conv_weight, conv_bias, skip_scale):
    channels, length = out_grad.shape
    block = min(128, channels)
    window = length // ctx_count
    tile = min(512, window)
    whole = pl.BlockSpec((block, length), lambda step, at_ctx: (step, 0))
    row = pl.BlockSpec((1, block), lambda step, at_ctx: (0, step))
    return pl.pallas_call(
        functools.partial(conv_kernel, tile),
        grid_spec=pltpu.PrefetchScalarGridSpec(
            num_scalar_prefetch=1,
            grid=(channels // block,),
            in_specs=[whole] * 4
            + [pl.BlockSpec((conv_weight.shape[0], block), lambda step, at_ctx: (0, step)), row, row],
            out_specs=[pl.BlockSpec((window, block), lambda step, at_ctx: (0, step))] * ctx_count,
            scratch_shapes=[pltpu.VMEM((block, length), jnp.bfloat16), pltpu.VMEM((block, 8), jnp.float32)],
        ),
        out_shape=[jax.ShapeDtypeStruct((window, channels), jnp.bfloat16)] * ctx_count,
        compiler_params=pltpu.CompilerParams(vmem_limit_bytes=VMEM_BYTES),
        cost_estimate=pl.CostEstimate(
            flops=40 * channels * length, bytes_accessed=10 * channels * length, transcendentals=2 * channels * length
        ),
        name="conv_grad",
    )(at_ctx, out_grad, gate_in, conv_in, scan_grad, conv_weight, conv_bias[None], skip_scale[None])


def matmul_kernel(lefts, rights, place, *refs):
    left_refs = refs[:lefts]
    right_refs = refs[lefts : lefts + rights]
    resid = refs[lefts + rights]
    outs = refs[lefts + rights + 1 :]
    left = jnp.concatenate([ref[...] for ref in left_refs], axis=1)
    right = jnp.concatenate([ref[...] for ref in right_refs], axis=0)
    total = jnp.dot(left, right, preferred_element_type=jnp.float32)
    mine = pl.program_id(0) == place[0]
    total = total + jnp.where(mine, resid[...].astype(jnp.float32), 0.0)
    at = 0
    for out in outs:
        out[...] = total[:, at : at + out.shape[1]].astype(out.dtype)
        at += out.shape[1]


def matmul(lefts, rights, resid, place, widths):
    tokens, depth = lefts[0].shape
    width = rights[0].shape[1]
    tile = resid.shape[0]
    flops = 2 * tokens * depth * len(lefts) * width
    moved = 2 * (tokens * depth * len(lefts) + depth * len(lefts) * width + tokens * width)
    return pl.pallas_call(
        functools.partial(matmul_kernel, len(lefts), len(rights)),
        grid_spec=pltpu.PrefetchScalarGridSpec(
            num_scalar_prefetch=1,
            grid=(tokens // tile,),
            in_specs=[pl.BlockSpec((tile, depth), lambda step, place: (step, 0))] * len(lefts)
            + [pl.BlockSpec(right.shape, lambda step, place: (0, 0)) for right in rights]
            + [pl.BlockSpec(resid.shape, lambda step, place: (0, 0))],
            out_specs=[pl.BlockSpec((tile, part), lambda step, place: (step, 0)) for part in widths],
        ),
        out_shape=[jax.ShapeDtypeStruct((tokens, part), jnp.bfloat16) for part in widths],
        compiler_params=pltpu.CompilerParams(vmem_limit_bytes=VMEM_BYTES),
        cost_estimate=pl.CostEstimate(flops=flops, bytes_accessed=moved, transcendentals=0),
        name="partial_product",
    )(place, *lefts, *rights, resid)


def on_device(
    out_grad,
    gate_in,
    conv_in,
    scan_grad,
    conv_weight,
    conv_bias,
    skip_scale,
    projection,
    resid_grad,
    routes,
    gate_probs,
):
    ctx_count = lax.axis_size("ctx")
    exp_count = lax.axis_size("exp")
    chips = exp_count // 2
    ctx_at = lax.axis_index("ctx")
    exp_at = lax.axis_index("exp")
    chip_at = exp_at // 2
    core_at = exp_at % 2
    channels, length = out_grad.shape
    features = projection.shape[1]
    half = features // 2
    unit = half // UNITS
    widths = [[unit * part for part in group] for group in GROUPS]
    starts = [sum(map(sum, widths[:at])) for at in range(len(widths))]
    tok_rows = resid_grad.shape[0]
    window = tok_rows * exp_count
    tile = 2 * tok_rows

    def to_core(array):
        return lax.ppermute(array, "exp", [(place, place ^ 1) for place in range(exp_count)])

    def to_ctx(array, offset):
        return lax.ppermute(array, "ctx", [(place, place ^ offset) for place in range(ctx_count)])

    def swap_chips(array, low, inward=True, outward=True):
        pairs = set()
        for core in (0, 1):
            for near, far in ((low, low + 1), (chips - 1 - low, chips - 2 - low)):
                if inward:
                    pairs.add((2 * near + core, 2 * far + core))
                if outward:
                    pairs.add((2 * far + core, 2 * near + core))
        return lax.ppermute(array, "exp", sorted(pairs))

    def columns_of(array, core, at, width):
        return lax.dynamic_slice_in_dim(array, core * half + at, width, 1)

    def both_cores(array, at, width):
        here = columns_of(array, core_at, at, width)
        return here, to_core(columns_of(array, 1 - core_at, at, width))

    def spread_twice(piece, late):
        near = [to_ctx(piece, 1), to_ctx(piece, 2)]
        cut = piece.shape[0] // 2
        low, high, _ = lax.optimization_barrier((near[1][:cut], near[0][cut:], late))
        return [piece, near[0], near[1], to_ctx(low, 1), to_ctx(high, 2)]

    def spread(piece):
        return [piece] + [to_ctx(piece, offset) for offset in range(1, ctx_count)]

    first = sum(widths[0])
    rights = [spread(jnp.concatenate(both_cores(projection, 0, first), axis=0))]

    turned = conv_grad(
        ctx_at.astype(jnp.int32).reshape(1),
        ctx_count,
        out_grad,
        gate_in,
        conv_in,
        scan_grad,
        conv_weight,
        conv_bias,
        skip_scale,
    )
    turned, rights[0] = lax.optimization_barrier((turned, rights[0]))
    lefts = [turned[0], to_core(turned[0])]
    for offset in range(1, ctx_count):
        piece = to_ctx(turned[offset], offset)
        lefts += [piece, to_core(piece)]
    lefts[1], projection, resid_grad, routes = lax.optimization_barrier((lefts[1], projection, resid_grad, routes))

    routed = jnp.concatenate([routes.T.astype(jnp.float32), gate_probs.T], axis=0)[None]
    offset = 1
    while offset < exp_count:
        other = lax.ppermute(routed, "exp", [(place, place ^ offset) for place in range(exp_count)])
        routed = jnp.concatenate([routed, other], axis=0)
        offset *= 2
    order = (jnp.arange(exp_count)[:, None] ^ exp_at) == jnp.arange(exp_count)[None, :]
    routed = jnp.sum(jnp.where(order[:, :, None, None], routed[None], 0.0), axis=1)

    rest_here, rest_there = both_cores(projection, first, half - first)
    rest = []
    for group, at in list(zip(widths, starts))[1:]:
        cut = slice(at - first, at - first + sum(group))
        rest.append(jnp.concatenate([rest_here[:, cut], rest_there[:, cut]], axis=0))
    resid_here, resid_there = both_cores(resid_grad, 0, half)
    resid = jnp.where(
        core_at == 0,
        jnp.concatenate([resid_here, resid_there], axis=0),
        jnp.concatenate([resid_there, resid_here], axis=0),
    )

    route_width = routes.shape[1]
    all_routes = routed[:, :route_width]
    all_probs = routed[:, route_width:]
    capacity = max(2, 14 * tok_rows // (4 * EXP_DEV * exp_count))
    experts = jnp.stack([exp_at, exp_at ^ 1]).astype(jnp.float32)
    named = all_routes[None] == experts[:, None, None, None]
    hit = jnp.any(named, axis=2)
    prob = jnp.sum(jnp.where(named, all_probs[None], 0.0), axis=2)
    count = hit.astype(jnp.int32)
    rank = jnp.cumsum(count, axis=2) - count
    slot = jnp.where(hit, rank + (jnp.arange(exp_count, dtype=jnp.int32) % 2)[None, :, None] * capacity, -1)
    slot = slot.reshape(2, chips, 1, tile)
    picks = slot == jnp.arange(2 * capacity, dtype=jnp.int32)[None, None, :, None]
    scale = jnp.sum(jnp.where(picks, prob.reshape(2, chips, 1, tile), 0.0), axis=3, keepdims=True)
    picks = picks.astype(jnp.bfloat16)
    picks, scale, lefts = lax.optimization_barrier((picks, scale, lefts))

    if channels < 128:
        lefts = [jnp.concatenate(lefts, axis=1)]
    place = chip_at.astype(jnp.int32).reshape(1)
    pieces = sum(map(len, GROUPS))

    middle = chips // 2
    distance = jnp.minimum(chip_at, chips - 1 - chip_at)
    rows_own, rows_got, waiting = [], [], []

    def add(one, other):
        return (one.astype(jnp.float32) + other.astype(jnp.float32)).astype(jnp.bfloat16)

    def finish(grads):
        width = grads.shape[1]
        rows = jnp.einsum("eist,itf->eisf", picks, grads.reshape(chips, tile, width), preferred_element_type=jnp.float32)
        rows = (rows * scale).astype(jnp.bfloat16).reshape(2, chips * 2 * capacity, width)
        rows_own.append(rows[0])
        waiting.append(rows[1])
        if len(waiting) == 2 or len(rows_own) == pieces:
            rows_got.append(to_core(jnp.concatenate(waiting, axis=1)))
            waiting.clear()

    hops = middle - 1
    sums = [[None] * pieces for _ in range(hops + 1)]
    ready = [[None] * pieces for _ in range(hops + 1)]
    lag = DELAY - 1
    last = pieces + lag * hops + DELAY * hops
    group_at = 0
    first_of = [sum(map(len, GROUPS[:at])) for at in range(len(GROUPS))]
    for step in range(last + 1):
        if group_at < len(GROUPS) and first_of[group_at] == step:
            group, at = widths[group_at], starts[group_at]
            if group_at:
                sums[1][step - 2], place = lax.optimization_barrier((sums[1][step - 2], place))
                piece = rest[group_at - 1]
                if ctx_count == 4:
                    late = sums[1][step - 4] if step >= 4 else lefts[0]
                    rights.append(spread_twice(piece, late))
                else:
                    rights.append(spread(piece))
            right = rights[group_at]
            if channels < 128:
                right = [jnp.concatenate(right, axis=0)]
            products = matmul(lefts, right, resid[:, at : at + sum(group)], place, group)
            sums[0][step : step + len(group)] = products
            group_at += 1
        for hop in range(hops):
            inward = step - lag * hop
            outward = inward - DELAY - 2 * lag * (hops - 1 - hop)
            send_in = 0 <= inward < pieces
            send_out = 0 <= outward < pieces
            if not (send_in or send_out):
                continue
            if send_in and 0 <= inward - 2:
                sums[hop][inward], sums[hop + 1][inward - 2] = lax.optimization_barrier(
                    (sums[hop][inward], sums[hop + 1][inward - 2])
                )
            rising = sums[hop][inward] if send_in else None
            falling = ready[hop + 1][outward] if send_out else None
            if send_in and send_out:
                got = swap_chips(jnp.where(distance == hop, rising, falling), hop)
            else:
                got = swap_chips(rising if send_in else falling, hop, send_in, send_out)
            if send_in:
                sums[hop + 1][inward] = add(rising, got)
                if hop == hops - 1:
                    crossed = swap_chips(sums[hop + 1][inward], middle - 1)
                    ready[hops][inward] = add(sums[hop + 1][inward], crossed)
            if send_out:
                ready[hop][outward] = jnp.where(distance == hop, got, falling)
                if hop == 0:
                    finish(ready[0][outward])
    result = jnp.where(
        core_at == 0,
        jnp.concatenate(rows_own + rows_got, axis=1),
        jnp.concatenate(rows_got + rows_own, axis=1),
    )
    return result[None]


def solution(mesh):
    placed = (
        P(("ctx", "exp"), None),
        P(("ctx", "exp"), None),
        P(("ctx", "exp"), None),
        P(("ctx", "exp"), None),
        P(None, ("ctx", "exp")),
        P(("ctx", "exp")),
        P(("ctx", "exp")),
        P(("ctx", "exp"), None),
        P(("ctx", "exp"), None),
        P(("ctx", "exp"), None),
        P(("ctx", "exp"), None),
    )
    return jax.shard_map(
        on_device, mesh=mesh, in_specs=placed, out_specs=P("exp", "ctx", None), check_vma=False
    )
```

```python
import functools

import jax
import jax.numpy as jnp
from jax import lax
from jax.experimental import pallas as pl
from jax.experimental.pallas import tpu as pltpu
from jax.sharding import PartitionSpec as P

EXP_DEV = 1
GROUPS = ((1, 1), (1, 1), (1, 1), (1, 1))
UNITS = sum(map(sum, GROUPS))
DELAY = 3
SWAPS = (6, 8)
VMEM_BYTES = 60 * 1024 * 1024


def conv_kernel(tile, at_ctx, out_grad, gate_in, conv_in, scan_grad, taps, bias, skip, *refs):
    turned, flat, columns_of = refs[:-2], refs[-2], refs[-1]
    channels, length = out_grad.shape
    window = length // len(turned)
    kernel_taps = taps.shape[0]
    rows_at_once = 16
    settings = jnp.concatenate(
        [0.5 * taps[...], 0.5 * bias[...], skip[...], jnp.zeros((8 - kernel_taps - 2, channels), jnp.float32)], axis=0
    )
    columns_of[...] = settings.T

    def row_group(group, _):
        row_at = pl.multiple_of(group * rows_at_once, rows_at_once)
        rows = pl.ds(row_at, rows_at_once)

        def spread(index):
            column = jnp.broadcast_to(columns_of[rows, index : index + 1], (rows_at_once, 128))
            return jnp.concatenate([column] * (tile // 128), axis=1)

        weights = [spread(tap) for tap in range(kernel_taps)]
        bias_half = spread(kernel_taps)
        skip_value = spread(kernel_taps + 1)
        after = jnp.zeros((rows_at_once, 128), jnp.float32)
        for at in range(length - tile, -1, -tile):
            columns = pl.ds(at, tile)
            gate = 0.5 * gate_in[rows, columns].astype(jnp.float32)
            gated = out_grad[rows, columns].astype(jnp.float32) * (gate + gate * jnp.tanh(gate))
            here = conv_in[rows, columns].astype(jnp.float32)
            if at:
                before = conv_in[rows, pl.ds(at - 128, 128)].astype(jnp.float32)
            else:
                before = jnp.zeros((rows_at_once, 128), jnp.float32)
            wide = jnp.concatenate([before, here], axis=1)
            half = bias_half + weights[kernel_taps - 1] * here
            for tap in range(kernel_taps - 1):
                back = kernel_taps - 1 - tap
                half = half + weights[tap] * pltpu.roll(wide, back, 1)[:, 128:]
            turn = jnp.tanh(half)
            scan = scan_grad[rows, columns].astype(jnp.float32)
            grad = (scan + skip_value * gated) * (1.0 + turn + half * (1.0 - turn * turn))
            wide_grad = jnp.concatenate([grad, after], axis=1)
            total = weights[kernel_taps - 1] * grad
            for tap in range(kernel_taps - 1):
                ahead = kernel_taps - 1 - tap
                total = total + weights[tap] * pltpu.roll(wide_grad, tile + 128 - ahead, 1)[:, :tile]
            flat[rows, columns] = total.astype(flat.dtype)
            after = grad[:, :128]
        return 0

    lax.fori_loop(0, channels // rows_at_once, row_group, 0)
    for offset, out in enumerate(turned):
        from_at = (at_ctx[0] ^ offset) * window
        for at in range(0, window, tile):
            out[pl.ds(at, tile), :] = flat[:, pl.ds(pl.multiple_of(from_at + at, tile), tile)].T


def conv_grad(at_ctx, ctx_count, out_grad, gate_in, conv_in, scan_grad, conv_weight, conv_bias, skip_scale):
    channels, length = out_grad.shape
    block = min(128, channels)
    window = length // ctx_count
    tile = min(512, window)
    whole = pl.BlockSpec((block, length), lambda step, at_ctx: (step, 0))
    row = pl.BlockSpec((1, block), lambda step, at_ctx: (0, step))
    return pl.pallas_call(
        functools.partial(conv_kernel, tile),
        grid_spec=pltpu.PrefetchScalarGridSpec(
            num_scalar_prefetch=1,
            grid=(channels // block,),
            in_specs=[whole] * 4
            + [pl.BlockSpec((conv_weight.shape[0], block), lambda step, at_ctx: (0, step)), row, row],
            out_specs=[pl.BlockSpec((window, block), lambda step, at_ctx: (0, step))] * ctx_count,
            scratch_shapes=[pltpu.VMEM((block, length), jnp.bfloat16), pltpu.VMEM((block, 8), jnp.float32)],
        ),
        out_shape=[jax.ShapeDtypeStruct((window, channels), jnp.bfloat16)] * ctx_count,
        compiler_params=pltpu.CompilerParams(vmem_limit_bytes=VMEM_BYTES),
        cost_estimate=pl.CostEstimate(
            flops=40 * channels * length, bytes_accessed=10 * channels * length, transcendentals=2 * channels * length
        ),
        name="conv_grad",
    )(at_ctx, out_grad, gate_in, conv_in, scan_grad, conv_weight, conv_bias[None], skip_scale[None])


def matmul_kernel(lefts, rights, place, *refs):
    left_refs = refs[:lefts]
    right_refs = refs[lefts : lefts + rights]
    resid = refs[lefts + rights]
    outs = refs[lefts + rights + 1 :]
    left = jnp.concatenate([ref[...] for ref in left_refs], axis=1)
    right = jnp.concatenate([ref[...] for ref in right_refs], axis=0)
    total = jnp.dot(left, right, preferred_element_type=jnp.float32)
    mine = pl.program_id(0) == place[0]
    total = total + jnp.where(mine, resid[...].astype(jnp.float32), 0.0)
    at = 0
    for out in outs:
        out[...] = total[:, at : at + out.shape[1]].astype(out.dtype)
        at += out.shape[1]


def matmul(lefts, rights, resid, place, widths):
    tokens, depth = lefts[0].shape
    width = rights[0].shape[1]
    tile = resid.shape[0]
    flops = 2 * tokens * depth * len(lefts) * width
    moved = 2 * (tokens * depth * len(lefts) + depth * len(lefts) * width + tokens * width)
    return pl.pallas_call(
        functools.partial(matmul_kernel, len(lefts), len(rights)),
        grid_spec=pltpu.PrefetchScalarGridSpec(
            num_scalar_prefetch=1,
            grid=(tokens // tile,),
            in_specs=[pl.BlockSpec((tile, depth), lambda step, place: (step, 0))] * len(lefts)
            + [pl.BlockSpec(right.shape, lambda step, place: (0, 0)) for right in rights]
            + [pl.BlockSpec(resid.shape, lambda step, place: (0, 0))],
            out_specs=[pl.BlockSpec((tile, part), lambda step, place: (step, 0)) for part in widths],
        ),
        out_shape=[jax.ShapeDtypeStruct((tokens, part), jnp.bfloat16) for part in widths],
        compiler_params=pltpu.CompilerParams(vmem_limit_bytes=VMEM_BYTES),
        cost_estimate=pl.CostEstimate(flops=flops, bytes_accessed=moved, transcendentals=0),
        name="partial_product",
    )(place, *lefts, *rights, resid)


def on_device(
    out_grad,
    gate_in,
    conv_in,
    scan_grad,
    conv_weight,
    conv_bias,
    skip_scale,
    projection,
    resid_grad,
    routes,
    gate_probs,
):
    ctx_count = lax.axis_size("ctx")
    exp_count = lax.axis_size("exp")
    chips = exp_count // 2
    ctx_at = lax.axis_index("ctx")
    exp_at = lax.axis_index("exp")
    chip_at = exp_at // 2
    core_at = exp_at % 2
    channels, length = out_grad.shape
    features = projection.shape[1]
    half = features // 2
    unit = half // UNITS
    widths = [[unit * part for part in group] for group in GROUPS]
    starts = [sum(map(sum, widths[:at])) for at in range(len(widths))]
    tok_rows = resid_grad.shape[0]
    window = tok_rows * exp_count
    tile = 2 * tok_rows

    def to_core(array):
        return lax.ppermute(array, "exp", [(place, place ^ 1) for place in range(exp_count)])

    def to_ctx(array, offset):
        return lax.ppermute(array, "ctx", [(place, place ^ offset) for place in range(ctx_count)])

    def swap_chips(array, low, inward=True, outward=True):
        pairs = set()
        for core in (0, 1):
            for near, far in ((low, low + 1), (chips - 1 - low, chips - 2 - low)):
                if inward:
                    pairs.add((2 * near + core, 2 * far + core))
                if outward:
                    pairs.add((2 * far + core, 2 * near + core))
        return lax.ppermute(array, "exp", sorted(pairs))

    def columns_of(array, core, at, width):
        return lax.dynamic_slice_in_dim(array, core * half + at, width, 1)

    def both_cores(array, at, width):
        here = columns_of(array, core_at, at, width)
        return here, to_core(columns_of(array, 1 - core_at, at, width))

    def spread_near(piece):
        return [piece, to_ctx(piece, 1), to_ctx(piece, 2)]

    def spread_on(near):
        cut = near[0].shape[0] // 2
        low, high = chain(near[2][:cut], near[1][cut:])
        return near + [to_ctx(low, 1), to_ctx(high, 2)]

    def spread(piece):
        return [piece] + [to_ctx(piece, offset) for offset in range(1, ctx_count)]

    first = sum(widths[0])
    rights = [spread(jnp.concatenate(both_cores(projection, 0, first), axis=0))]

    turned = conv_grad(
        ctx_at.astype(jnp.int32).reshape(1),
        ctx_count,
        out_grad,
        gate_in,
        conv_in,
        scan_grad,
        conv_weight,
        conv_bias,
        skip_scale,
    )
    turned, rights[0] = lax.optimization_barrier((turned, rights[0]))
    lefts = [turned[0], to_core(turned[0])]
    for offset in range(1, ctx_count):
        piece = to_ctx(turned[offset], offset)
        lefts += [piece, to_core(piece)]
    lefts[1], projection, resid_grad, routes = lax.optimization_barrier((lefts[1], projection, resid_grad, routes))

    routed = jnp.concatenate([routes.T.astype(jnp.float32), gate_probs.T], axis=0)[None]
    offset = 1
    while offset < exp_count:
        other = lax.ppermute(routed, "exp", [(place, place ^ offset) for place in range(exp_count)])
        routed = jnp.concatenate([routed, other], axis=0)
        offset *= 2
    order = (jnp.arange(exp_count)[:, None] ^ exp_at) == jnp.arange(exp_count)[None, :]
    routed = jnp.sum(jnp.where(order[:, :, None, None], routed[None], 0.0), axis=1)

    rest_here, rest_there = both_cores(projection, first, half - first)
    rest = []
    for group, at in list(zip(widths, starts))[1:]:
        cut = slice(at - first, at - first + sum(group))
        rest.append(jnp.concatenate([rest_here[:, cut], rest_there[:, cut]], axis=0))
    resid_here, resid_there = both_cores(resid_grad, 0, half)
    resid = jnp.where(
        core_at == 0,
        jnp.concatenate([resid_here, resid_there], axis=0),
        jnp.concatenate([resid_there, resid_here], axis=0),
    )

    route_width = routes.shape[1]
    all_routes = routed[:, :route_width]
    all_probs = routed[:, route_width:]
    capacity = max(2, 14 * tok_rows // (4 * EXP_DEV * exp_count))
    experts = jnp.stack([exp_at, exp_at ^ 1]).astype(jnp.float32)
    named = all_routes[None] == experts[:, None, None, None]
    hit = jnp.any(named, axis=2)
    prob = jnp.sum(jnp.where(named, all_probs[None], 0.0), axis=2)
    count = hit.astype(jnp.int32)
    rank = jnp.cumsum(count, axis=2) - count
    slot = jnp.where(hit, rank + (jnp.arange(exp_count, dtype=jnp.int32) % 2)[None, :, None] * capacity, -1)
    slot = slot.reshape(2, chips, 1, tile)
    picks = slot == jnp.arange(2 * capacity, dtype=jnp.int32)[None, None, :, None]
    scale = jnp.sum(jnp.where(picks, prob.reshape(2, chips, 1, tile), 0.0), axis=3, keepdims=True)
    picks = picks.astype(jnp.bfloat16)
    picks, scale, lefts = lax.optimization_barrier((picks, scale, lefts))

    lefts, picks, scale, resid, rest = lax.optimization_barrier((lefts, picks, scale, resid, rest))
    if channels < 128:
        lefts = [jnp.concatenate(lefts, axis=1)]
    place = chip_at.astype(jnp.int32).reshape(1)
    pieces = sum(map(len, GROUPS))
    token = [place]

    def chain(*arrays):
        *arrays, token[0] = lax.optimization_barrier((*arrays, token[0]))
        token[0] = arrays[0]
        return arrays

    def products(group_at, right):
        group, at = widths[group_at], starts[group_at]
        if channels < 128:
            right = [jnp.concatenate(right, axis=0)]
        right = chain(*right)
        found = matmul(lefts, right, resid[:, at : at + sum(group)], place, group)
        token[0] = found[0]
        return found

    middle = chips // 2
    distance = jnp.minimum(chip_at, chips - 1 - chip_at)
    rows_own, rows_got, waiting = [], [], []

    def add(one, other):
        return (one.astype(jnp.float32) + other.astype(jnp.float32)).astype(jnp.bfloat16)

    def finish(grads):
        width = grads.shape[1]
        rows = jnp.einsum("eist,itf->eisf", picks, grads.reshape(chips, tile, width), preferred_element_type=jnp.float32)
        rows = (rows * scale).astype(jnp.bfloat16).reshape(2, chips * 2 * capacity, width)
        rows_own.append(rows[0])
        waiting.append(rows[1])
        if len(rows_own) in SWAPS:
            rows_got.append(to_core(jnp.concatenate(waiting, axis=1)))
            waiting.clear()

    square = ctx_count == 4
    hops = middle - 1
    lag = DELAY - 1
    sums = [[None] * pieces for _ in range(hops + 1)]
    ready = [[None] * pieces for _ in range(hops + 1)]
    outer, across = {}, {}
    first_of = [sum(map(len, GROUPS[:at])) for at in range(len(GROUPS))]
    sums[0][: len(GROUPS[0])] = products(0, rights[0])
    rights.append(spread(rest[0]))
    near = None
    for step in range(pieces + 2 * lag * hops + DELAY + 1):
        for hop in range(hops):
            if (step - 2, hop) not in outer:
                continue
            got, inward, outward = outer[step - 2, hop]
            if inward is not None:
                own, got = chain(sums[hop][inward], got)
                sums[hop + 1][inward] = token[0] = add(own, got)
                if hop == hops - 1:
                    across[step] = (swap_chips(token[0], middle - 1), inward)
            if outward is not None:
                ready[hop][outward] = jnp.where(distance == hop, got, ready[hop + 1][outward])
                if hop == 0:
                    finish(ready[0][outward])
        if step - 1 in across:
            got, index = across[step - 1]
            own, got = chain(sums[hops][index], got)
            ready[hops][index] = add(own, got)
        if step and step in first_of:
            group_at = first_of.index(step)
            if near is not None:
                rights.append(near)
            sums[0][step : step + len(GROUPS[group_at])] = products(group_at, rights[group_at])
            near = None
            if group_at + 1 < len(GROUPS):
                (piece,) = chain(rest[group_at])
                near = spread_near(piece) if square else spread(piece)
        for hop in range(hops):
            inward = step - lag * hop
            outward = inward - DELAY - 2 * lag * (hops - 1 - hop)
            inward = inward if 0 <= inward < pieces else None
            outward = outward if 0 <= outward < pieces else None
            if inward is not None and outward is not None:
                payload = jnp.where(distance == hop, sums[hop][inward], ready[hop + 1][outward])
            elif inward is not None:
                payload = sums[hop][inward]
            elif outward is not None:
                payload = ready[hop + 1][outward]
            else:
                continue
            (payload,) = chain(payload)
            outer[step, hop] = (swap_chips(payload, hop, inward is not None, outward is not None), inward, outward)
        if square and near is not None and step % 2:
            near = spread_on(near)
    result = jnp.where(
        core_at == 0,
        jnp.concatenate(rows_own + rows_got, axis=1),
        jnp.concatenate(rows_got + rows_own, axis=1),
    )
    return result[None]


def solution(mesh):
    placed = (
        P(("ctx", "exp"), None),
        P(("ctx", "exp"), None),
        P(("ctx", "exp"), None),
        P(("ctx", "exp"), None),
        P(None, ("ctx", "exp")),
        P(("ctx", "exp")),
        P(("ctx", "exp")),
        P(("ctx", "exp"), None),
        P(("ctx", "exp"), None),
        P(("ctx", "exp"), None),
        P(("ctx", "exp"), None),
    )
    return jax.shard_map(
        on_device, mesh=mesh, in_specs=placed, out_specs=P("exp", "ctx", None), check_vma=False
    )
```

```python
import functools

import jax
import jax.numpy as jnp
from jax import lax
from jax.experimental import pallas as pl
from jax.experimental.pallas import tpu as pltpu
from jax.sharding import PartitionSpec as P

EXP_DEV = 1
GROUPS = ((1, 1), (1, 1), (1, 1), (1, 1))
UNITS = sum(map(sum, GROUPS))
DELAY = 3
SWAPS = (6, 8)
CONV_VMEM = 44 * 1024 * 1024
PRODUCT_VMEM = 22 * 1024 * 1024


def conv_kernel(tile, at_ctx, out_grad, gate_in, conv_in, scan_grad, taps, bias, skip, *refs):
    turned, flat, columns_of = refs[:-2], refs[-2], refs[-1]
    channels, length = out_grad.shape
    window = length // len(turned)
    kernel_taps = taps.shape[0]
    rows_at_once = 16
    settings = jnp.concatenate(
        [0.5 * taps[...], 0.5 * bias[...], skip[...], jnp.zeros((8 - kernel_taps - 2, channels), jnp.float32)], axis=0
    )
    columns_of[...] = settings.T

    def row_group(group, _):
        row_at = pl.multiple_of(group * rows_at_once, rows_at_once)
        rows = pl.ds(row_at, rows_at_once)

        def spread(index):
            column = jnp.broadcast_to(columns_of[rows, index : index + 1], (rows_at_once, 128))
            return jnp.concatenate([column] * (tile // 128), axis=1)

        weights = [spread(tap) for tap in range(kernel_taps)]
        bias_half = spread(kernel_taps)
        skip_value = spread(kernel_taps + 1)
        after = jnp.zeros((rows_at_once, 128), jnp.float32)
        for at in range(length - tile, -1, -tile):
            columns = pl.ds(at, tile)
            gate = 0.5 * gate_in[rows, columns].astype(jnp.float32)
            gated = out_grad[rows, columns].astype(jnp.float32) * (gate + gate * jnp.tanh(gate))
            here = conv_in[rows, columns].astype(jnp.float32)
            if at:
                before = conv_in[rows, pl.ds(at - 128, 128)].astype(jnp.float32)
            else:
                before = jnp.zeros((rows_at_once, 128), jnp.float32)
            wide = jnp.concatenate([before, here], axis=1)
            half = bias_half + weights[kernel_taps - 1] * here
            for tap in range(kernel_taps - 1):
                back = kernel_taps - 1 - tap
                half = half + weights[tap] * pltpu.roll(wide, back, 1)[:, 128:]
            turn = jnp.tanh(half)
            scan = scan_grad[rows, columns].astype(jnp.float32)
            grad = (scan + skip_value * gated) * (1.0 + turn + half * (1.0 - turn * turn))
            wide_grad = jnp.concatenate([grad, after], axis=1)
            total = weights[kernel_taps - 1] * grad
            for tap in range(kernel_taps - 1):
                ahead = kernel_taps - 1 - tap
                total = total + weights[tap] * pltpu.roll(wide_grad, tile + 128 - ahead, 1)[:, :tile]
            flat[rows, columns] = total.astype(flat.dtype)
            after = grad[:, :128]
        return 0

    lax.fori_loop(0, channels // rows_at_once, row_group, 0)
    for offset, out in enumerate(turned):
        from_at = (at_ctx[0] ^ offset) * window
        for at in range(0, window, tile):
            out[pl.ds(at, tile), :] = flat[:, pl.ds(pl.multiple_of(from_at + at, tile), tile)].T


def conv_grad(at_ctx, ctx_count, out_grad, gate_in, conv_in, scan_grad, conv_weight, conv_bias, skip_scale):
    channels, length = out_grad.shape
    block = min(128, channels)
    window = length // ctx_count
    tile = min(512, window)
    whole = pl.BlockSpec((block, length), lambda step, at_ctx: (step, 0))
    row = pl.BlockSpec((1, block), lambda step, at_ctx: (0, step))
    return pl.pallas_call(
        functools.partial(conv_kernel, tile),
        grid_spec=pltpu.PrefetchScalarGridSpec(
            num_scalar_prefetch=1,
            grid=(channels // block,),
            in_specs=[whole] * 4
            + [pl.BlockSpec((conv_weight.shape[0], block), lambda step, at_ctx: (0, step)), row, row],
            out_specs=[pl.BlockSpec((window, block), lambda step, at_ctx: (0, step))] * ctx_count,
            scratch_shapes=[pltpu.VMEM((block, length), jnp.bfloat16), pltpu.VMEM((block, 8), jnp.float32)],
        ),
        out_shape=[jax.ShapeDtypeStruct((window, channels), jnp.bfloat16)] * ctx_count,
        compiler_params=pltpu.CompilerParams(vmem_limit_bytes=CONV_VMEM),
        cost_estimate=pl.CostEstimate(
            flops=40 * channels * length, bytes_accessed=10 * channels * length, transcendentals=2 * channels * length
        ),
        name="conv_grad",
    )(at_ctx, out_grad, gate_in, conv_in, scan_grad, conv_weight, conv_bias[None], skip_scale[None])


def matmul_kernel(lefts, rights, place, *refs):
    left_refs = refs[:lefts]
    right_refs = refs[lefts : lefts + rights]
    resid = refs[lefts + rights]
    outs = refs[lefts + rights + 1 :]
    left = jnp.concatenate([ref[...] for ref in left_refs], axis=1)
    right = jnp.concatenate([ref[...] for ref in right_refs], axis=0)
    total = jnp.dot(left, right, preferred_element_type=jnp.float32)
    many = left.shape[0] // resid.shape[0]
    parts = []
    for part in range(many):
        mine = pl.program_id(0) * many + part == place[0]
        rows = total[part * resid.shape[0] : (part + 1) * resid.shape[0]]
        parts.append(rows + jnp.where(mine, resid[...].astype(jnp.float32), 0.0))
    total = jnp.concatenate(parts, axis=0)
    at = 0
    for out in outs:
        out[...] = total[:, at : at + out.shape[1]].astype(out.dtype)
        at += out.shape[1]


def matmul(lefts, rights, resid, place, widths):
    tokens, depth = lefts[0].shape
    width = rights[0].shape[1]
    tile = 2 * resid.shape[0]
    flops = 2 * tokens * depth * len(lefts) * width
    moved = 2 * (tokens * depth * len(lefts) + depth * len(lefts) * width + tokens * width)
    return pl.pallas_call(
        functools.partial(matmul_kernel, len(lefts), len(rights)),
        grid_spec=pltpu.PrefetchScalarGridSpec(
            num_scalar_prefetch=1,
            grid=(tokens // tile,),
            in_specs=[pl.BlockSpec((tile, depth), lambda step, place: (step, 0))] * len(lefts)
            + [pl.BlockSpec(right.shape, lambda step, place: (0, 0)) for right in rights]
            + [pl.BlockSpec(resid.shape, lambda step, place: (0, 0))],
            out_specs=[pl.BlockSpec((tile, part), lambda step, place: (step, 0)) for part in widths],
        ),
        out_shape=[jax.ShapeDtypeStruct((tokens, part), jnp.bfloat16) for part in widths],
        compiler_params=pltpu.CompilerParams(vmem_limit_bytes=PRODUCT_VMEM),
        cost_estimate=pl.CostEstimate(flops=flops, bytes_accessed=moved, transcendentals=0),
        name="partial_product",
    )(place, *lefts, *rights, resid)


def on_device(
    out_grad,
    gate_in,
    conv_in,
    scan_grad,
    conv_weight,
    conv_bias,
    skip_scale,
    projection,
    resid_grad,
    routes,
    gate_probs,
):
    ctx_count = lax.axis_size("ctx")
    exp_count = lax.axis_size("exp")
    chips = exp_count // 2
    ctx_at = lax.axis_index("ctx")
    exp_at = lax.axis_index("exp")
    chip_at = exp_at // 2
    core_at = exp_at % 2
    channels, length = out_grad.shape
    features = projection.shape[1]
    half = features // 2
    unit = half // UNITS
    widths = [[unit * part for part in group] for group in GROUPS]
    starts = [sum(map(sum, widths[:at])) for at in range(len(widths))]
    tok_rows = resid_grad.shape[0]
    window = tok_rows * exp_count
    tile = 2 * tok_rows

    def to_core(array):
        return lax.ppermute(array, "exp", [(place, place ^ 1) for place in range(exp_count)])

    def to_ctx(array, offset):
        return lax.ppermute(array, "ctx", [(place, place ^ offset) for place in range(ctx_count)])

    def swap_chips(array, low, inward=True, outward=True):
        pairs = set()
        for core in (0, 1):
            for near, far in ((low, low + 1), (chips - 1 - low, chips - 2 - low)):
                if inward:
                    pairs.add((2 * near + core, 2 * far + core))
                if outward:
                    pairs.add((2 * far + core, 2 * near + core))
        return lax.ppermute(array, "exp", sorted(pairs))

    def columns_of(array, core, at, width):
        return lax.dynamic_slice_in_dim(array, core * half + at, width, 1)

    def both_cores(array, at, width):
        here = columns_of(array, core_at, at, width)
        return here, to_core(columns_of(array, 1 - core_at, at, width))

    def spread_near(piece):
        return [piece, to_ctx(piece, 1), to_ctx(piece, 2)]

    def spread_on(near):
        cut = near[0].shape[0] // 2
        low, high = chain(near[2][:cut], near[1][cut:])
        return near + [to_ctx(low, 1), to_ctx(high, 2)]

    def spread(piece):
        return [piece] + [to_ctx(piece, offset) for offset in range(1, ctx_count)]

    first = sum(widths[0])
    rights = [spread(jnp.concatenate(both_cores(projection, 0, first), axis=0))]

    turned = conv_grad(
        ctx_at.astype(jnp.int32).reshape(1),
        ctx_count,
        out_grad,
        gate_in,
        conv_in,
        scan_grad,
        conv_weight,
        conv_bias,
        skip_scale,
    )
    turned, rights[0] = lax.optimization_barrier((turned, rights[0]))
    lefts = [turned[0], to_core(turned[0])]
    received = [to_ctx(turned[offset], offset) for offset in range(1, ctx_count)]
    lefts[1], projection, resid_grad, routes = lax.optimization_barrier((lefts[1], projection, resid_grad, routes))

    routed = jnp.concatenate([routes.T.astype(jnp.float32), gate_probs.T], axis=0)[None]
    offset = 1
    while offset < exp_count:
        other = lax.ppermute(routed, "exp", [(place, place ^ offset) for place in range(exp_count)])
        routed = jnp.concatenate([routed, other], axis=0)
        offset *= 2
    order = (jnp.arange(exp_count)[:, None] ^ exp_at) == jnp.arange(exp_count)[None, :]
    routed = jnp.sum(jnp.where(order[:, :, None, None], routed[None], 0.0), axis=1)

    rest_here, rest_there = both_cores(projection, first, half - first)
    rest = []
    for group, at in list(zip(widths, starts))[1:]:
        cut = slice(at - first, at - first + sum(group))
        rest.append(jnp.concatenate([rest_here[:, cut], rest_there[:, cut]], axis=0))
    received[-2], rest = lax.optimization_barrier((received[-2], rest))
    rights.append(spread(rest[0]))
    for piece in received:
        lefts += [piece, to_core(piece)]
    resid_here, resid_there = both_cores(resid_grad, 0, half)
    resid = jnp.where(
        core_at == 0,
        jnp.concatenate([resid_here, resid_there], axis=0),
        jnp.concatenate([resid_there, resid_here], axis=0),
    )

    route_width = routes.shape[1]
    all_routes = routed[:, :route_width]
    all_probs = routed[:, route_width:]
    capacity = max(2, 14 * tok_rows // (4 * EXP_DEV * exp_count))
    experts = jnp.stack([exp_at, exp_at ^ 1]).astype(jnp.float32)
    named = all_routes[None] == experts[:, None, None, None]
    hit = jnp.any(named, axis=2)
    prob = jnp.sum(jnp.where(named, all_probs[None], 0.0), axis=2)
    count = hit.astype(jnp.int32)
    rank = jnp.cumsum(count, axis=2) - count
    slot = jnp.where(hit, rank + (jnp.arange(exp_count, dtype=jnp.int32) % 2)[None, :, None] * capacity, -1)
    slot = slot.reshape(2, chips, 1, tile)
    picks = slot == jnp.arange(2 * capacity, dtype=jnp.int32)[None, None, :, None]
    scale = jnp.sum(jnp.where(picks, prob.reshape(2, chips, 1, tile), 0.0), axis=3, keepdims=True)
    picks = picks.astype(jnp.bfloat16)
    picks, scale, lefts = lax.optimization_barrier((picks, scale, lefts))

    lefts, picks, scale, resid, rest = lax.optimization_barrier((lefts, picks, scale, resid, rest))
    if channels < 128:
        lefts = [jnp.concatenate(lefts, axis=1)]
    place = chip_at.astype(jnp.int32).reshape(1)
    pieces = sum(map(len, GROUPS))
    token = [place]

    def chain(*arrays):
        *arrays, token[0] = lax.optimization_barrier((*arrays, token[0]))
        token[0] = arrays[0]
        return arrays

    def products(group_at, right):
        group, at = widths[group_at], starts[group_at]
        if channels < 128:
            right = [jnp.concatenate(right, axis=0)]
        right = chain(*right)
        found = matmul(lefts, right, resid[:, at : at + sum(group)], place, group)
        token[0] = found[0]
        return found

    middle = chips // 2
    distance = jnp.minimum(chip_at, chips - 1 - chip_at)
    rows_own, rows_got, waiting = [], [], []

    def add(one, other):
        return (one.astype(jnp.float32) + other.astype(jnp.float32)).astype(jnp.bfloat16)

    def finish(grads):
        width = grads.shape[1]
        rows = jnp.einsum("eist,itf->eisf", picks, grads.reshape(chips, tile, width), preferred_element_type=jnp.float32)
        rows = (rows * scale).astype(jnp.bfloat16).reshape(2, chips * 2 * capacity, width)
        rows_own.append(rows[0])
        waiting.append(rows[1])
        if len(rows_own) in SWAPS:
            rows_got.append(to_core(jnp.concatenate(waiting, axis=1)))
            waiting.clear()

    square = ctx_count == 4
    hops = middle - 1
    lag = DELAY - 1
    sums = [[None] * pieces for _ in range(hops + 1)]
    ready = [[None] * pieces for _ in range(hops + 1)]
    outer, across = {}, {}
    first_of = [sum(map(len, GROUPS[:at])) for at in range(len(GROUPS))]
    sums[0][: len(GROUPS[0])] = products(0, rights[0])
    near = None
    for step in range(pieces + 2 * lag * hops + DELAY + 1):
        for hop in range(hops):
            if (step - 2, hop) not in outer:
                continue
            got, inward, outward = outer[step - 2, hop]
            if inward is not None:
                own, got = chain(sums[hop][inward], got)
                sums[hop + 1][inward] = token[0] = add(own, got)
                if hop == hops - 1:
                    across[step] = (swap_chips(token[0], middle - 1), inward)
            if outward is not None:
                ready[hop][outward] = jnp.where(distance == hop, got, ready[hop + 1][outward])
                if hop == 0:
                    finish(ready[0][outward])
        if step - 1 in across:
            got, index = across[step - 1]
            own, got = chain(sums[hops][index], got)
            ready[hops][index] = add(own, got)
        if square and near is not None and step % 2:
            near = spread_on(near)
        if step and step in first_of:
            group_at = first_of.index(step)
            if near is not None:
                rights.append(near)
            near = None
            if group_at + 1 < len(GROUPS):
                piece, *rights[group_at] = chain(rest[group_at], *rights[group_at])
                near = spread_near(piece) if square else spread(piece)
            sums[0][step : step + len(GROUPS[group_at])] = products(group_at, rights[group_at])
        for hop in range(hops):
            inward = step - lag * hop
            outward = inward - DELAY - 2 * lag * (hops - 1 - hop)
            inward = inward if 0 <= inward < pieces else None
            outward = outward if 0 <= outward < pieces else None
            if inward is not None and outward is not None:
                payload = jnp.where(distance == hop, sums[hop][inward], ready[hop + 1][outward])
            elif inward is not None:
                payload = sums[hop][inward]
            elif outward is not None:
                payload = ready[hop + 1][outward]
            else:
                continue
            (payload,) = chain(payload)
            outer[step, hop] = (swap_chips(payload, hop, inward is not None, outward is not None), inward, outward)
    result = jnp.where(
        core_at == 0,
        jnp.concatenate(rows_own + rows_got, axis=1),
        jnp.concatenate(rows_got + rows_own, axis=1),
    )
    return result[None]


def solution(mesh):
    placed = (
        P(("ctx", "exp"), None),
        P(("ctx", "exp"), None),
        P(("ctx", "exp"), None),
        P(("ctx", "exp"), None),
        P(None, ("ctx", "exp")),
        P(("ctx", "exp")),
        P(("ctx", "exp")),
        P(("ctx", "exp"), None),
        P(("ctx", "exp"), None),
        P(("ctx", "exp"), None),
        P(("ctx", "exp"), None),
    )
    return jax.shard_map(
        on_device, mesh=mesh, in_specs=placed, out_specs=P("exp", "ctx", None), check_vma=False
    )
```

```python
import functools

import jax
import jax.numpy as jnp
from jax import lax
from jax.experimental import pallas as pl
from jax.experimental.pallas import tpu as pltpu
from jax.sharding import PartitionSpec as P

EXP_DEV = 1
GROUPS = ((1,), (1,), (1, 1), (1, 1), (1, 1))
FIRST_PHASE = {1: 2, 2: 3, 4: 4}
SECOND_PHASE = {2: 2, 3: 3, 5: 4}
UNITS = sum(map(sum, GROUPS))
DELAY = 3
SWAPS = (6, 8)
VMEM_BYTES = 60 * 1024 * 1024


def conv_kernel(tile, at_ctx, out_grad, gate_in, conv_in, scan_grad, taps, bias, skip, *refs):
    turned, flat, columns_of = refs[:-2], refs[-2], refs[-1]
    channels, length = out_grad.shape
    window = length // len(turned)
    rows_at_once = 16
    groups = channels // rows_at_once
    chunk = window // groups
    settings = jnp.concatenate(
        [0.5 * taps[...], 0.5 * bias[...], skip[...], jnp.zeros((2, channels), jnp.float32)], axis=0
    )
    columns_of[...] = settings.T

    def turn(offset, at):
        at = pl.multiple_of(at, chunk)
        turned[offset][pl.ds(at, chunk), :] = flat[offset % 2, :, pl.ds(at, chunk)].T

    for offset in range(len(turned)):
        from_at = (at_ctx[0] ^ offset) * window

        def row_group(group, _):
            if offset:
                turn(offset - 1, group * chunk)
            rows = pl.ds(pl.multiple_of(group * rows_at_once, rows_at_once), rows_at_once)
            setting = [jnp.broadcast_to(columns_of[rows, at : at + 1], (rows_at_once, 128)) for at in range(6)]

            def spread(index, width):
                return jnp.concatenate([setting[index]] * (width // 128), axis=1)

            def columns(ref, at, width):
                return ref[rows, pl.ds(pl.multiple_of(at, 128), width)].astype(jnp.float32)

            def grad_of(at, width):
                gate = 0.5 * columns(gate_in, at, width)
                gated = columns(out_grad, at, width) * (gate + gate * jnp.tanh(gate))
                here = columns(conv_in, at, width)
                before = jnp.where(at > 0, columns(conv_in, jnp.maximum(at - 128, 0), 128), 0.0)
                wide = jnp.concatenate([before, here], axis=1)
                one_back = pltpu.roll(wide, 1, 1)
                older = spread(1, width + 128) * wide + spread(0, width + 128) * one_back
                half = spread(4, width) + spread(3, width) * here + spread(2, width) * one_back[:, 128:]
                half = half + pltpu.roll(older, 2, 1)[:, 128:]
                turn_value = jnp.tanh(half)
                slope = 1.0 + turn_value + half * (1.0 - turn_value * turn_value)
                return (columns(scan_grad, at, width) + spread(5, width) * gated) * slope

            end = from_at + window
            after = grad_of(jnp.minimum(end, length - 128), 128)
            after = jnp.where(end < length, after, 0.0)
            for at in range(window - tile, -1, -tile):
                grad = grad_of(from_at + at, tile)
                wide = jnp.concatenate([grad, after], axis=1)
                one_on = pltpu.roll(wide, tile + 127, 1)
                later = spread(1, tile + 128) * wide + spread(0, tile + 128) * one_on
                total = spread(3, tile) * grad + spread(2, tile) * one_on[:, :tile]
                total = total + pltpu.roll(later, tile + 126, 1)[:, :tile]
                flat[offset % 2, rows, pl.ds(at, tile)] = total.astype(flat.dtype)
                after = grad[:, :128]
            return 0

        lax.fori_loop(0, groups, row_group, 0)
    lax.fori_loop(0, groups, lambda group, _: (turn(len(turned) - 1, group * chunk), 0)[1], 0)


def conv_grad(at_ctx, ctx_count, out_grad, gate_in, conv_in, scan_grad, conv_weight, conv_bias, skip_scale):
    channels, length = out_grad.shape
    block = min(128, channels)
    window = length // ctx_count
    tile = min(512, window)
    whole = pl.BlockSpec((block, length), lambda step, at_ctx: (step, 0))
    row = pl.BlockSpec((1, block), lambda step, at_ctx: (0, step))
    return pl.pallas_call(
        functools.partial(conv_kernel, tile),
        grid_spec=pltpu.PrefetchScalarGridSpec(
            num_scalar_prefetch=1,
            grid=(channels // block,),
            in_specs=[whole] * 4
            + [pl.BlockSpec((conv_weight.shape[0], block), lambda step, at_ctx: (0, step)), row, row],
            out_specs=[pl.BlockSpec((window, block), lambda step, at_ctx: (0, step))] * ctx_count,
            scratch_shapes=[pltpu.VMEM((2, block, window), jnp.bfloat16), pltpu.VMEM((block, 8), jnp.float32)],
        ),
        out_shape=[jax.ShapeDtypeStruct((window, channels), jnp.bfloat16)] * ctx_count,
        compiler_params=pltpu.CompilerParams(vmem_limit_bytes=VMEM_BYTES),
        cost_estimate=pl.CostEstimate(
            flops=40 * channels * length, bytes_accessed=10 * channels * length, transcendentals=2 * channels * length
        ),
        name="conv_grad",
    )(at_ctx, out_grad, gate_in, conv_in, scan_grad, conv_weight, conv_bias[None], skip_scale[None])


def matmul_kernel(lefts, rights, place, *refs):
    left_refs = refs[:lefts]
    right_refs = refs[lefts : lefts + rights]
    resid = refs[lefts + rights]
    outs = refs[lefts + rights + 1 :]
    left = jnp.concatenate([ref[...] for ref in left_refs], axis=1)
    right = jnp.concatenate([ref[...] for ref in right_refs], axis=0)
    total = jnp.dot(left, right, preferred_element_type=jnp.float32)
    many = left.shape[0] // resid.shape[0]
    parts = []
    for part in range(many):
        mine = pl.program_id(0) * many + part == place[0]
        rows = total[part * resid.shape[0] : (part + 1) * resid.shape[0]]
        parts.append(rows + jnp.where(mine, resid[...].astype(jnp.float32), 0.0))
    total = jnp.concatenate(parts, axis=0)
    at = 0
    for out in outs:
        out[...] = total[:, at : at + out.shape[1]].astype(out.dtype)
        at += out.shape[1]


def matmul(lefts, rights, resid, place, widths):
    tokens, depth = lefts[0].shape
    width = rights[0].shape[1]
    tile = 2 * resid.shape[0]
    flops = 2 * tokens * depth * len(lefts) * width
    moved = 2 * (tokens * depth * len(lefts) + depth * len(lefts) * width + tokens * width)
    return pl.pallas_call(
        functools.partial(matmul_kernel, len(lefts), len(rights)),
        grid_spec=pltpu.PrefetchScalarGridSpec(
            num_scalar_prefetch=1,
            grid=(tokens // tile,),
            in_specs=[pl.BlockSpec((tile, depth), lambda step, place: (step, 0))] * len(lefts)
            + [pl.BlockSpec(right.shape, lambda step, place: (0, 0)) for right in rights]
            + [pl.BlockSpec(resid.shape, lambda step, place: (0, 0))],
            out_specs=[pl.BlockSpec((tile, part), lambda step, place: (step, 0)) for part in widths],
        ),
        out_shape=[jax.ShapeDtypeStruct((tokens, part), jnp.bfloat16) for part in widths],
        compiler_params=pltpu.CompilerParams(vmem_limit_bytes=VMEM_BYTES),
        cost_estimate=pl.CostEstimate(flops=flops, bytes_accessed=moved, transcendentals=0),
        name="partial_product",
    )(place, *lefts, *rights, resid)


def on_device(
    out_grad,
    gate_in,
    conv_in,
    scan_grad,
    conv_weight,
    conv_bias,
    skip_scale,
    projection,
    resid_grad,
    routes,
    gate_probs,
):
    ctx_count = lax.axis_size("ctx")
    exp_count = lax.axis_size("exp")
    chips = exp_count // 2
    ctx_at = lax.axis_index("ctx")
    exp_at = lax.axis_index("exp")
    chip_at = exp_at // 2
    core_at = exp_at % 2
    channels, length = out_grad.shape
    features = projection.shape[1]
    half = features // 2
    unit = half // UNITS
    widths = [[unit * part for part in group] for group in GROUPS]
    starts = [sum(map(sum, widths[:at])) for at in range(len(widths))]
    tok_rows = resid_grad.shape[0]
    window = tok_rows * exp_count
    tile = 2 * tok_rows

    def to_core(array):
        return lax.ppermute(array, "exp", [(place, place ^ 1) for place in range(exp_count)])

    def to_ctx(array, offset):
        return lax.ppermute(array, "ctx", [(place, place ^ offset) for place in range(ctx_count)])

    def swap_chips(array, low, inward=True, outward=True):
        pairs = set()
        for core in (0, 1):
            for near, far in ((low, low + 1), (chips - 1 - low, chips - 2 - low)):
                if inward:
                    pairs.add((2 * near + core, 2 * far + core))
                if outward:
                    pairs.add((2 * far + core, 2 * near + core))
        return lax.ppermute(array, "exp", sorted(pairs))

    def columns_of(array, core, at, width):
        return lax.dynamic_slice_in_dim(array, core * half + at, width, 1)

    def both_cores(array, at, width):
        here = columns_of(array, core_at, at, width)
        return here, to_core(columns_of(array, 1 - core_at, at, width))

    def spread_near(piece):
        return [piece, to_ctx(piece, 1), to_ctx(piece, 2)]

    def spread_on(near):
        cut = near[0].shape[0] // 2
        low, high = chain(near[2][:cut], near[1][cut:])
        return near + [to_ctx(low, 1), to_ctx(high, 2)]

    def spread(piece):
        return [piece] + [to_ctx(piece, offset) for offset in range(1, ctx_count)]

    first = sum(widths[0])
    rights = [spread(jnp.concatenate(both_cores(projection, 0, first), axis=0))]

    turned = conv_grad(
        ctx_at.astype(jnp.int32).reshape(1),
        ctx_count,
        out_grad,
        gate_in,
        conv_in,
        scan_grad,
        conv_weight,
        conv_bias,
        skip_scale,
    )
    turned, rights[0] = lax.optimization_barrier((turned, rights[0]))
    lefts = [turned[0], to_core(turned[0])]
    received = [to_ctx(turned[offset], offset) for offset in range(1, ctx_count)]
    lefts[1], projection, resid_grad, routes = lax.optimization_barrier((lefts[1], projection, resid_grad, routes))

    routed = jnp.concatenate([routes.T.astype(jnp.float32), gate_probs.T], axis=0)[None]
    offset = 1
    while offset < exp_count:
        other = lax.ppermute(routed, "exp", [(place, place ^ offset) for place in range(exp_count)])
        routed = jnp.concatenate([routed, other], axis=0)
        offset *= 2
    order = (jnp.arange(exp_count)[:, None] ^ exp_at) == jnp.arange(exp_count)[None, :]
    routed = jnp.sum(jnp.where(order[:, :, None, None], routed[None], 0.0), axis=1)

    rest_here, rest_there = both_cores(projection, first, half - first)
    rest = []
    for group, at in list(zip(widths, starts))[1:]:
        cut = slice(at - first, at - first + sum(group))
        rest.append(jnp.concatenate([rest_here[:, cut], rest_there[:, cut]], axis=0))
    received[-2], rest = lax.optimization_barrier((received[-2], rest))
    rights.append(spread(rest[0]))
    for piece in received:
        lefts += [piece, to_core(piece)]
    resid_here, resid_there = both_cores(resid_grad, 0, half)
    resid = jnp.where(
        core_at == 0,
        jnp.concatenate([resid_here, resid_there], axis=0),
        jnp.concatenate([resid_there, resid_here], axis=0),
    )

    route_width = routes.shape[1]
    all_routes = routed[:, :route_width]
    all_probs = routed[:, route_width:]
    capacity = max(2, 14 * tok_rows // (4 * EXP_DEV * exp_count))
    experts = jnp.stack([exp_at, exp_at ^ 1]).astype(jnp.float32)
    named = all_routes[None] == experts[:, None, None, None]
    hit = jnp.any(named, axis=2)
    prob = jnp.sum(jnp.where(named, all_probs[None], 0.0), axis=2)
    count = hit.astype(jnp.int32)
    rank = jnp.cumsum(count, axis=2) - count
    slot = jnp.where(hit, rank + (jnp.arange(exp_count, dtype=jnp.int32) % 2)[None, :, None] * capacity, -1)
    slot = slot.reshape(2, chips, 1, tile)
    picks = slot == jnp.arange(2 * capacity, dtype=jnp.int32)[None, None, :, None]
    scale = jnp.sum(jnp.where(picks, prob.reshape(2, chips, 1, tile), 0.0), axis=3, keepdims=True)
    picks = picks.astype(jnp.bfloat16)
    picks, scale, lefts = lax.optimization_barrier((picks, scale, lefts))

    lefts, picks, scale, resid, rest = lax.optimization_barrier((lefts, picks, scale, resid, rest))
    if channels < 128:
        lefts = [jnp.concatenate(lefts, axis=1)]
    place = chip_at.astype(jnp.int32).reshape(1)
    pieces = sum(map(len, GROUPS))
    token = [place]

    def chain(*arrays):
        *arrays, token[0] = lax.optimization_barrier((*arrays, token[0]))
        token[0] = arrays[0]
        return arrays

    def products(group_at, right):
        group, at = widths[group_at], starts[group_at]
        if channels < 128:
            right = [jnp.concatenate(right, axis=0)]
        right = chain(*right)
        found = matmul(lefts, right, resid[:, at : at + sum(group)], place, group)
        token[0] = found[0]
        return found

    middle = chips // 2
    distance = jnp.minimum(chip_at, chips - 1 - chip_at)
    rows_own, rows_got, waiting = [], [], []

    def add(one, other):
        return (one.astype(jnp.float32) + other.astype(jnp.float32)).astype(jnp.bfloat16)

    def finish(grads):
        width = grads.shape[1]
        rows = jnp.einsum("eist,itf->eisf", picks, grads.reshape(chips, tile, width), preferred_element_type=jnp.float32)
        rows = (rows * scale).astype(jnp.bfloat16).reshape(2, chips * 2 * capacity, width)
        rows_own.append(rows[0])
        waiting.append(rows[1])
        if len(rows_own) in SWAPS:
            rows_got.append(to_core(jnp.concatenate(waiting, axis=1)))
            waiting.clear()

    square = ctx_count == 4
    hops = middle - 1
    lag = DELAY - 1
    sums = [[None] * pieces for _ in range(hops + 1)]
    ready = [[None] * pieces for _ in range(hops + 1)]
    outer, across = {}, {}
    first_of = [sum(map(len, GROUPS[:at])) for at in range(len(GROUPS))]
    sums[0][: len(GROUPS[0])] = products(0, rights[0])
    rights += [None] * (len(GROUPS) - len(rights))
    for step in range(pieces + 2 * lag * hops + DELAY + 1):
        for hop in range(hops):
            if (step - 2, hop) not in outer:
                continue
            got, inward, outward = outer[step - 2, hop]
            if inward is not None:
                own, got = chain(sums[hop][inward], got)
                sums[hop + 1][inward] = token[0] = add(own, got)
                if hop == hops - 1:
                    across[step] = (swap_chips(token[0], middle - 1), inward)
            if outward is not None:
                ready[hop][outward] = jnp.where(distance == hop, got, ready[hop + 1][outward])
                if hop == 0:
                    finish(ready[0][outward])
        if step - 1 in across:
            got, index = across[step - 1]
            own, got = chain(sums[hops][index], got)
            ready[hops][index] = add(own, got)
        if step in SECOND_PHASE and square:
            rights[SECOND_PHASE[step]] = spread_on(rights[SECOND_PHASE[step]])
        group_at = first_of.index(step) if step and step in first_of else None
        if step in FIRST_PHASE:
            coming = FIRST_PHASE[step]
            piece, *rights[group_at] = chain(rest[coming - 1], *rights[group_at])
            rights[coming] = spread_near(piece) if square else spread(piece)
        if group_at:
            sums[0][step : step + len(GROUPS[group_at])] = products(group_at, rights[group_at])
        for hop in range(hops):
            inward = step - lag * hop
            outward = inward - DELAY - 2 * lag * (hops - 1 - hop)
            inward = inward if 0 <= inward < pieces else None
            outward = outward if 0 <= outward < pieces else None
            if inward is not None and outward is not None:
                payload = jnp.where(distance == hop, sums[hop][inward], ready[hop + 1][outward])
            elif inward is not None:
                payload = sums[hop][inward]
            elif outward is not None:
                payload = ready[hop + 1][outward]
            else:
                continue
            (payload,) = chain(payload)
            outer[step, hop] = (swap_chips(payload, hop, inward is not None, outward is not None), inward, outward)
    result = jnp.where(
        core_at == 0,
        jnp.concatenate(rows_own + rows_got, axis=1),
        jnp.concatenate(rows_got + rows_own, axis=1),
    )
    return result[None]


def solution(mesh):
    placed = (
        P(("ctx", "exp"), None),
        P(("ctx", "exp"), None),
        P(("ctx", "exp"), None),
        P(("ctx", "exp"), None),
        P(None, ("ctx", "exp")),
        P(("ctx", "exp")),
        P(("ctx", "exp")),
        P(("ctx", "exp"), None),
        P(("ctx", "exp"), None),
        P(("ctx", "exp"), None),
        P(("ctx", "exp"), None),
    )
    return jax.shard_map(
        on_device, mesh=mesh, in_specs=placed, out_specs=P("exp", "ctx", None), check_vma=False
    )
```

```python
import functools

import jax
import jax.numpy as jnp
from jax import lax
from jax.experimental import pallas as pl
from jax.experimental.pallas import tpu as pltpu
from jax.sharding import PartitionSpec as P

EXP_DEV = 1
GROUPS = ((1,), (1,), (1, 1), (1, 1), (1, 1))
FIRST_PHASE = {2: 3, 4: 4}
SECOND_PHASE = {3: 3, 5: 4}
UNITS = sum(map(sum, GROUPS))
DELAY = 3
SWAPS = (6, 8)
VMEM_BYTES = 60 * 1024 * 1024


def conv_kernel(tile, at_ctx, out_grad, gate_in, conv_in, scan_grad, taps, bias, skip, *refs):
    turned, flat, columns_of = refs[:-2], refs[-2], refs[-1]
    channels, length = out_grad.shape
    window = length // len(turned)
    kernel_taps = taps.shape[0]
    rows_at_once = 16
    settings = jnp.concatenate(
        [0.5 * taps[...], 0.5 * bias[...], skip[...], jnp.zeros((8 - kernel_taps - 2, channels), jnp.float32)], axis=0
    )
    columns_of[...] = settings.T

    def row_group(group, _):
        row_at = pl.multiple_of(group * rows_at_once, rows_at_once)
        rows = pl.ds(row_at, rows_at_once)

        def spread(index, width=tile):
            column = jnp.broadcast_to(columns_of[rows, index : index + 1], (rows_at_once, 128))
            return jnp.concatenate([column] * (width // 128), axis=1)

        weights = [spread(tap) for tap in range(kernel_taps)]
        wider = [spread(tap, tile + 128) for tap in (0, 1)]
        bias_half = spread(kernel_taps)
        skip_value = spread(kernel_taps + 1)
        after = jnp.zeros((rows_at_once, 128), jnp.float32)
        for at in range(length - tile, -1, -tile):
            columns = pl.ds(at, tile)
            gate = 0.5 * gate_in[rows, columns].astype(jnp.float32)
            gated = out_grad[rows, columns].astype(jnp.float32) * (gate + gate * jnp.tanh(gate))
            here = conv_in[rows, columns].astype(jnp.float32)
            if at:
                before = conv_in[rows, pl.ds(at - 128, 128)].astype(jnp.float32)
            else:
                before = jnp.zeros((rows_at_once, 128), jnp.float32)
            wide = jnp.concatenate([before, here], axis=1)
            one_back = pltpu.roll(wide, 1, 1)
            older = wider[1] * wide + wider[0] * one_back
            half = bias_half + weights[3] * here + weights[2] * one_back[:, 128:]
            half = half + pltpu.roll(older, 2, 1)[:, 128:]
            turn = jnp.tanh(half)
            scan = scan_grad[rows, columns].astype(jnp.float32)
            grad = (scan + skip_value * gated) * (1.0 + turn + half * (1.0 - turn * turn))
            wide_grad = jnp.concatenate([grad, after], axis=1)
            one_on = pltpu.roll(wide_grad, tile + 127, 1)
            later = wider[1] * wide_grad + wider[0] * one_on
            total = weights[3] * grad + weights[2] * one_on[:, :tile]
            total = total + pltpu.roll(later, tile + 126, 1)[:, :tile]
            flat[rows, columns] = total.astype(flat.dtype)
            after = grad[:, :128]
        return 0

    lax.fori_loop(0, channels // rows_at_once, row_group, 0)
    for offset, out in enumerate(turned):
        from_at = (at_ctx[0] ^ offset) * window
        for at in range(0, window, tile):
            out[pl.ds(at, tile), :] = flat[:, pl.ds(pl.multiple_of(from_at + at, tile), tile)].T


def conv_grad(at_ctx, ctx_count, out_grad, gate_in, conv_in, scan_grad, conv_weight, conv_bias, skip_scale):
    channels, length = out_grad.shape
    block = min(128, channels)
    window = length // ctx_count
    tile = min(512, window)
    whole = pl.BlockSpec((block, length), lambda step, at_ctx: (step, 0))
    row = pl.BlockSpec((1, block), lambda step, at_ctx: (0, step))
    return pl.pallas_call(
        functools.partial(conv_kernel, tile),
        grid_spec=pltpu.PrefetchScalarGridSpec(
            num_scalar_prefetch=1,
            grid=(channels // block,),
            in_specs=[whole] * 4
            + [pl.BlockSpec((conv_weight.shape[0], block), lambda step, at_ctx: (0, step)), row, row],
            out_specs=[pl.BlockSpec((window, block), lambda step, at_ctx: (0, step))] * ctx_count,
            scratch_shapes=[pltpu.VMEM((block, length), jnp.bfloat16), pltpu.VMEM((block, 8), jnp.float32)],
        ),
        out_shape=[jax.ShapeDtypeStruct((window, channels), jnp.bfloat16)] * ctx_count,
        compiler_params=pltpu.CompilerParams(vmem_limit_bytes=VMEM_BYTES),
        cost_estimate=pl.CostEstimate(
            flops=40 * channels * length, bytes_accessed=10 * channels * length, transcendentals=2 * channels * length
        ),
        name="conv_grad",
    )(at_ctx, out_grad, gate_in, conv_in, scan_grad, conv_weight, conv_bias[None], skip_scale[None])


def matmul_kernel(lefts, rights, place, *refs):
    left_refs = refs[:lefts]
    right_refs = refs[lefts : lefts + rights]
    resid = refs[lefts + rights]
    outs = refs[lefts + rights + 1 :]
    left = jnp.concatenate([ref[...] for ref in left_refs], axis=1)
    right = jnp.concatenate([ref[...] for ref in right_refs], axis=0)
    total = jnp.dot(left, right, preferred_element_type=jnp.float32)
    many = left.shape[0] // resid.shape[0]
    parts = []
    for part in range(many):
        mine = pl.program_id(0) * many + part == place[0]
        rows = total[part * resid.shape[0] : (part + 1) * resid.shape[0]]
        parts.append(rows + jnp.where(mine, resid[...].astype(jnp.float32), 0.0))
    total = jnp.concatenate(parts, axis=0)
    at = 0
    for out in outs:
        out[...] = total[:, at : at + out.shape[1]].astype(out.dtype)
        at += out.shape[1]


def matmul(lefts, rights, resid, place, widths):
    tokens, depth = lefts[0].shape
    width = rights[0].shape[1]
    tile = 2 * resid.shape[0]
    flops = 2 * tokens * depth * len(lefts) * width
    moved = 2 * (tokens * depth * len(lefts) + depth * len(lefts) * width + tokens * width)
    return pl.pallas_call(
        functools.partial(matmul_kernel, len(lefts), len(rights)),
        grid_spec=pltpu.PrefetchScalarGridSpec(
            num_scalar_prefetch=1,
            grid=(tokens // tile,),
            in_specs=[pl.BlockSpec((tile, depth), lambda step, place: (step, 0))] * len(lefts)
            + [pl.BlockSpec(right.shape, lambda step, place: (0, 0)) for right in rights]
            + [pl.BlockSpec(resid.shape, lambda step, place: (0, 0))],
            out_specs=[pl.BlockSpec((tile, part), lambda step, place: (step, 0)) for part in widths],
        ),
        out_shape=[jax.ShapeDtypeStruct((tokens, part), jnp.bfloat16) for part in widths],
        compiler_params=pltpu.CompilerParams(vmem_limit_bytes=VMEM_BYTES),
        cost_estimate=pl.CostEstimate(flops=flops, bytes_accessed=moved, transcendentals=0),
        name="partial_product",
    )(place, *lefts, *rights, resid)


def on_device(
    out_grad,
    gate_in,
    conv_in,
    scan_grad,
    conv_weight,
    conv_bias,
    skip_scale,
    projection,
    resid_grad,
    routes,
    gate_probs,
):
    ctx_count = lax.axis_size("ctx")
    exp_count = lax.axis_size("exp")
    chips = exp_count // 2
    ctx_at = lax.axis_index("ctx")
    exp_at = lax.axis_index("exp")
    chip_at = exp_at // 2
    core_at = exp_at % 2
    channels, length = out_grad.shape
    features = projection.shape[1]
    half = features // 2
    unit = half // UNITS
    widths = [[unit * part for part in group] for group in GROUPS]
    starts = [sum(map(sum, widths[:at])) for at in range(len(widths))]
    tok_rows = resid_grad.shape[0]
    window = tok_rows * exp_count
    tile = 2 * tok_rows

    def to_core(array):
        return lax.ppermute(array, "exp", [(place, place ^ 1) for place in range(exp_count)])

    def to_ctx(array, offset):
        return lax.ppermute(array, "ctx", [(place, place ^ offset) for place in range(ctx_count)])

    def swap_chips(array, low, inward=True, outward=True):
        pairs = set()
        for core in (0, 1):
            for near, far in ((low, low + 1), (chips - 1 - low, chips - 2 - low)):
                if inward:
                    pairs.add((2 * near + core, 2 * far + core))
                if outward:
                    pairs.add((2 * far + core, 2 * near + core))
        return lax.ppermute(array, "exp", sorted(pairs))

    def columns_of(array, core, at, width):
        return lax.dynamic_slice_in_dim(array, core * half + at, width, 1)

    def both_cores(array, at, width):
        here = columns_of(array, core_at, at, width)
        return here, to_core(columns_of(array, 1 - core_at, at, width))

    def spread_near(piece):
        return [piece, to_ctx(piece, 1), to_ctx(piece, 2)]

    def spread_on(near):
        cut = near[0].shape[0] // 2
        low, high = chain(near[2][:cut], near[1][cut:])
        return near + [to_ctx(low, 1), to_ctx(high, 2)]

    def spread(piece):
        return [piece] + [to_ctx(piece, offset) for offset in range(1, ctx_count)]

    first = sum(widths[0])
    rights = [spread(jnp.concatenate(both_cores(projection, 0, first), axis=0))]

    turned = conv_grad(
        ctx_at.astype(jnp.int32).reshape(1),
        ctx_count,
        out_grad,
        gate_in,
        conv_in,
        scan_grad,
        conv_weight,
        conv_bias,
        skip_scale,
    )
    turned, rights[0] = lax.optimization_barrier((turned, rights[0]))
    lefts = [turned[0], to_core(turned[0])]
    received = [to_ctx(turned[offset], offset) for offset in range(1, ctx_count)]
    lefts[1], projection, resid_grad, routes = lax.optimization_barrier((lefts[1], projection, resid_grad, routes))

    routed = jnp.concatenate([routes.T.astype(jnp.float32), gate_probs.T], axis=0)[None]
    offset = 1
    while offset < exp_count:
        other = lax.ppermute(routed, "exp", [(place, place ^ offset) for place in range(exp_count)])
        routed = jnp.concatenate([routed, other], axis=0)
        offset *= 2
    order = (jnp.arange(exp_count)[:, None] ^ exp_at) == jnp.arange(exp_count)[None, :]
    routed = jnp.sum(jnp.where(order[:, :, None, None], routed[None], 0.0), axis=1)

    rest_here, rest_there = both_cores(projection, first, half - first)
    rest = []
    for group, at in list(zip(widths, starts))[1:]:
        cut = slice(at - first, at - first + sum(group))
        rest.append(jnp.concatenate([rest_here[:, cut], rest_there[:, cut]], axis=0))
    resid_here, resid_there = both_cores(resid_grad, 0, half)
    resid = jnp.where(
        core_at == 0,
        jnp.concatenate([resid_here, resid_there], axis=0),
        jnp.concatenate([resid_there, resid_here], axis=0),
    )

    route_width = routes.shape[1]
    all_routes = routed[:, :route_width]
    all_probs = routed[:, route_width:]
    capacity = max(2, 14 * tok_rows // (4 * EXP_DEV * exp_count))
    experts = jnp.stack([exp_at, exp_at ^ 1]).astype(jnp.float32)
    named = all_routes[None] == experts[:, None, None, None]
    hit = jnp.any(named, axis=2)
    prob = jnp.sum(jnp.where(named, all_probs[None], 0.0), axis=2)
    count = hit.astype(jnp.int32)
    rank = jnp.cumsum(count, axis=2) - count
    slot = jnp.where(hit, rank + (jnp.arange(exp_count, dtype=jnp.int32) % 2)[None, :, None] * capacity, -1)
    slot = slot.reshape(2, chips, 1, tile)
    picks = slot == jnp.arange(2 * capacity, dtype=jnp.int32)[None, None, :, None]
    scale = jnp.sum(jnp.where(picks, prob.reshape(2, chips, 1, tile), 0.0), axis=3, keepdims=True)
    picks = picks.astype(jnp.bfloat16)

    rights.append(spread(rest[0]))
    received, rest, rights[1], resid, picks, scale = lax.optimization_barrier(
        (received, rest, rights[1], resid, picks, scale)
    )
    for piece in received:
        lefts += [piece, to_core(piece)]

    if channels < 128:
        lefts = [jnp.concatenate(lefts, axis=1)]
    place = chip_at.astype(jnp.int32).reshape(1)
    pieces = sum(map(len, GROUPS))
    token = [place]

    def chain(*arrays):
        *arrays, token[0] = lax.optimization_barrier((*arrays, token[0]))
        token[0] = arrays[0]
        return arrays

    def products(group_at, right):
        group, at = widths[group_at], starts[group_at]
        if channels < 128:
            right = [jnp.concatenate(right, axis=0)]
        right = chain(*right)
        found = matmul(lefts, right, resid[:, at : at + sum(group)], place, group)
        token[0] = found[0]
        return found

    middle = chips // 2
    distance = jnp.minimum(chip_at, chips - 1 - chip_at)
    rows_own, rows_got, waiting = [], [], []

    def add(one, other):
        return (one.astype(jnp.float32) + other.astype(jnp.float32)).astype(jnp.bfloat16)

    def finish(grads):
        width = grads.shape[1]
        rows = jnp.einsum("eist,itf->eisf", picks, grads.reshape(chips, tile, width), preferred_element_type=jnp.float32)
        rows = (rows * scale).astype(jnp.bfloat16).reshape(2, chips * 2 * capacity, width)
        rows_own.append(rows[0])
        waiting.append(rows[1])
        if len(rows_own) in SWAPS:
            rows_got.append(to_core(jnp.concatenate(waiting, axis=1)))
            waiting.clear()

    square = ctx_count == 4
    hops = middle - 1
    lag = DELAY - 1
    sums = [[None] * pieces for _ in range(hops + 1)]
    ready = [[None] * pieces for _ in range(hops + 1)]
    outer, across = {}, {}
    first_of = [sum(map(len, GROUPS[:at])) for at in range(len(GROUPS))]
    lefts, rest[1] = lax.optimization_barrier((lefts, rest[1]))
    rights.append(spread_near(rest[1]) if square else spread(rest[1]))
    sums[0][: len(GROUPS[0])] = products(0, rights[0])
    rights += [None] * (len(GROUPS) - len(rights))
    for step in range(pieces + 2 * lag * hops + DELAY + 1):
        for hop in range(hops):
            if (step - 2, hop) not in outer:
                continue
            got, inward, outward = outer[step - 2, hop]
            if inward is not None:
                own, got = chain(sums[hop][inward], got)
                sums[hop + 1][inward] = token[0] = add(own, got)
                if hop == hops - 1:
                    across[step] = (swap_chips(token[0], middle - 1), inward)
            if outward is not None:
                ready[hop][outward] = jnp.where(distance == hop, got, ready[hop + 1][outward])
                if hop == 0:
                    finish(ready[0][outward])
        if step - 1 in across:
            got, index = across[step - 1]
            own, got = chain(sums[hops][index], got)
            ready[hops][index] = add(own, got)
        if step in SECOND_PHASE and square:
            rights[SECOND_PHASE[step]] = spread_on(rights[SECOND_PHASE[step]])
        group_at = first_of.index(step) if step and step in first_of else None
        if step in FIRST_PHASE:
            coming = FIRST_PHASE[step]
            piece, *rights[group_at] = chain(rest[coming - 1], *rights[group_at])
            rights[coming] = spread_near(piece) if square else spread(piece)
        if group_at:
            sums[0][step : step + len(GROUPS[group_at])] = products(group_at, rights[group_at])
        for hop in range(hops):
            inward = step - lag * hop
            outward = inward - DELAY - 2 * lag * (hops - 1 - hop)
            inward = inward if 0 <= inward < pieces else None
            outward = outward if 0 <= outward < pieces else None
            if inward is not None and outward is not None:
                payload = jnp.where(distance == hop, sums[hop][inward], ready[hop + 1][outward])
            elif inward is not None:
                payload = sums[hop][inward]
            elif outward is not None:
                payload = ready[hop + 1][outward]
            else:
                continue
            (payload,) = chain(payload)
            outer[step, hop] = (swap_chips(payload, hop, inward is not None, outward is not None), inward, outward)
        if step == 1 and square:
            rights[2] = spread_on(rights[2])
    result = jnp.where(
        core_at == 0,
        jnp.concatenate(rows_own + rows_got, axis=1),
        jnp.concatenate(rows_got + rows_own, axis=1),
    )
    return result[None]


def solution(mesh):
    placed = (
        P(("ctx", "exp"), None),
        P(("ctx", "exp"), None),
        P(("ctx", "exp"), None),
        P(("ctx", "exp"), None),
        P(None, ("ctx", "exp")),
        P(("ctx", "exp")),
        P(("ctx", "exp")),
        P(("ctx", "exp"), None),
        P(("ctx", "exp"), None),
        P(("ctx", "exp"), None),
        P(("ctx", "exp"), None),
    )
    return jax.shard_map(
        on_device, mesh=mesh, in_specs=placed, out_specs=P("exp", "ctx", None), check_vma=False
    )
```

```python
import functools

import jax
import jax.numpy as jnp
from jax import lax
from jax.experimental import pallas as pl
from jax.experimental.pallas import tpu as pltpu
from jax.sharding import PartitionSpec as P

EXP_DEV = 1
GROUPS = ((1, 1), (1, 1), (1, 1), (1, 1))
FIRST_PHASE = {2: 2, 4: 3}
SECOND_PHASE = {3: 2, 5: 3}
UNITS = sum(map(sum, GROUPS))
DELAY = 3
SWAPS = (6, 8)
VMEM_BYTES = 60 * 1024 * 1024


def conv_kernel(tile, at_ctx, out_grad, gate_in, conv_in, scan_grad, taps, bias, skip, *refs):
    turned, flat, columns_of = refs[:-2], refs[-2], refs[-1]
    channels, length = out_grad.shape
    window = length // len(turned)
    kernel_taps = taps.shape[0]
    rows_at_once = 16
    settings = jnp.concatenate(
        [0.5 * taps[...], 0.5 * bias[...], skip[...], jnp.zeros((8 - kernel_taps - 2, channels), jnp.float32)], axis=0
    )
    columns_of[...] = settings.T

    def row_group(group, _):
        row_at = pl.multiple_of(group * rows_at_once, rows_at_once)
        rows = pl.ds(row_at, rows_at_once)

        def spread(index, width=tile):
            column = jnp.broadcast_to(columns_of[rows, index : index + 1], (rows_at_once, 128))
            return jnp.concatenate([column] * (width // 128), axis=1)

        weights = [spread(tap) for tap in range(kernel_taps)]
        wider = [spread(tap, tile + 128) for tap in (0, 1)]
        bias_half = spread(kernel_taps)
        skip_value = spread(kernel_taps + 1)
        after = jnp.zeros((rows_at_once, 128), jnp.float32)
        for at in range(length - tile, -1, -tile):
            columns = pl.ds(at, tile)
            gate = 0.5 * gate_in[rows, columns].astype(jnp.float32)
            gated = out_grad[rows, columns].astype(jnp.float32) * (gate + gate * jnp.tanh(gate))
            here = conv_in[rows, columns].astype(jnp.float32)
            if at:
                before = conv_in[rows, pl.ds(at - 128, 128)].astype(jnp.float32)
            else:
                before = jnp.zeros((rows_at_once, 128), jnp.float32)
            wide = jnp.concatenate([before, here], axis=1)
            one_back = pltpu.roll(wide, 1, 1)
            older = wider[1] * wide + wider[0] * one_back
            half = bias_half + weights[3] * here + weights[2] * one_back[:, 128:]
            half = half + pltpu.roll(older, 2, 1)[:, 128:]
            turn = jnp.tanh(half)
            scan = scan_grad[rows, columns].astype(jnp.float32)
            grad = (scan + skip_value * gated) * (1.0 + turn + half * (1.0 - turn * turn))
            wide_grad = jnp.concatenate([grad, after], axis=1)
            one_on = pltpu.roll(wide_grad, tile + 127, 1)
            later = wider[1] * wide_grad + wider[0] * one_on
            total = weights[3] * grad + weights[2] * one_on[:, :tile]
            total = total + pltpu.roll(later, tile + 126, 1)[:, :tile]
            flat[rows, columns] = total.astype(flat.dtype)
            after = grad[:, :128]
        return 0

    lax.fori_loop(0, channels // rows_at_once, row_group, 0)
    for offset, out in enumerate(turned):
        from_at = (at_ctx[0] ^ offset) * window
        for at in range(0, window, tile):
            out[pl.ds(at, tile), :] = flat[:, pl.ds(pl.multiple_of(from_at + at, tile), tile)].T


def conv_grad(at_ctx, ctx_count, out_grad, gate_in, conv_in, scan_grad, conv_weight, conv_bias, skip_scale):
    channels, length = out_grad.shape
    block = min(128, channels)
    window = length // ctx_count
    tile = min(512, window)
    whole = pl.BlockSpec((block, length), lambda step, at_ctx: (step, 0))
    row = pl.BlockSpec((1, block), lambda step, at_ctx: (0, step))
    return pl.pallas_call(
        functools.partial(conv_kernel, tile),
        grid_spec=pltpu.PrefetchScalarGridSpec(
            num_scalar_prefetch=1,
            grid=(channels // block,),
            in_specs=[whole] * 4
            + [pl.BlockSpec((conv_weight.shape[0], block), lambda step, at_ctx: (0, step)), row, row],
            out_specs=[pl.BlockSpec((window, block), lambda step, at_ctx: (0, step))] * ctx_count,
            scratch_shapes=[pltpu.VMEM((block, length), jnp.bfloat16), pltpu.VMEM((block, 8), jnp.float32)],
        ),
        out_shape=[jax.ShapeDtypeStruct((window, channels), jnp.bfloat16)] * ctx_count,
        compiler_params=pltpu.CompilerParams(vmem_limit_bytes=VMEM_BYTES),
        cost_estimate=pl.CostEstimate(
            flops=40 * channels * length, bytes_accessed=10 * channels * length, transcendentals=2 * channels * length
        ),
        name="conv_grad",
    )(at_ctx, out_grad, gate_in, conv_in, scan_grad, conv_weight, conv_bias[None], skip_scale[None])


def matmul_kernel(lefts, rights, place, *refs):
    left_refs = refs[:lefts]
    right_refs = refs[lefts : lefts + rights]
    resid = refs[lefts + rights]
    outs = refs[lefts + rights + 1 :]
    left = jnp.concatenate([ref[...] for ref in left_refs], axis=1)
    right = jnp.concatenate([ref[...] for ref in right_refs], axis=0)
    total = jnp.dot(left, right, preferred_element_type=jnp.float32)
    many = left.shape[0] // resid.shape[0]
    parts = []
    for part in range(many):
        mine = pl.program_id(0) * many + part == place[0]
        rows = total[part * resid.shape[0] : (part + 1) * resid.shape[0]]
        parts.append(rows + jnp.where(mine, resid[...].astype(jnp.float32), 0.0))
    total = jnp.concatenate(parts, axis=0)
    at = 0
    for out in outs:
        out[...] = total[:, at : at + out.shape[1]].astype(out.dtype)
        at += out.shape[1]


def matmul(lefts, rights, resid, place, widths, only=None):
    tokens, depth = lefts[0].shape
    block = 0
    width = rights[0].shape[1]
    if only is not None:
        block, width = only, widths[only]
        widths = (width,)
    tile = 2 * resid.shape[0]
    flops = 2 * tokens * depth * len(lefts) * width
    moved = 2 * (tokens * depth * len(lefts) + depth * len(lefts) * width + tokens * width)
    return pl.pallas_call(
        functools.partial(matmul_kernel, len(lefts), len(rights)),
        grid_spec=pltpu.PrefetchScalarGridSpec(
            num_scalar_prefetch=1,
            grid=(tokens // tile,),
            in_specs=[pl.BlockSpec((tile, depth), lambda step, place: (step, 0))] * len(lefts)
            + [pl.BlockSpec((right.shape[0], width), lambda step, place: (0, block)) for right in rights]
            + [pl.BlockSpec((resid.shape[0], width), lambda step, place: (0, block))],
            out_specs=[pl.BlockSpec((tile, part), lambda step, place: (step, 0)) for part in widths],
        ),
        out_shape=[jax.ShapeDtypeStruct((tokens, part), jnp.bfloat16) for part in widths],
        compiler_params=pltpu.CompilerParams(vmem_limit_bytes=VMEM_BYTES),
        cost_estimate=pl.CostEstimate(flops=flops, bytes_accessed=moved, transcendentals=0),
        name="partial_product",
    )(place, *lefts, *rights, resid)


def on_device(
    out_grad,
    gate_in,
    conv_in,
    scan_grad,
    conv_weight,
    conv_bias,
    skip_scale,
    projection,
    resid_grad,
    routes,
    gate_probs,
):
    ctx_count = lax.axis_size("ctx")
    exp_count = lax.axis_size("exp")
    chips = exp_count // 2
    ctx_at = lax.axis_index("ctx")
    exp_at = lax.axis_index("exp")
    chip_at = exp_at // 2
    core_at = exp_at % 2
    channels, length = out_grad.shape
    features = projection.shape[1]
    half = features // 2
    unit = half // UNITS
    widths = [[unit * part for part in group] for group in GROUPS]
    starts = [sum(map(sum, widths[:at])) for at in range(len(widths))]
    tok_rows = resid_grad.shape[0]
    window = tok_rows * exp_count
    tile = 2 * tok_rows

    def to_core(array):
        return lax.ppermute(array, "exp", [(place, place ^ 1) for place in range(exp_count)])

    def to_ctx(array, offset):
        return lax.ppermute(array, "ctx", [(place, place ^ offset) for place in range(ctx_count)])

    def swap_chips(array, low, inward=True, outward=True):
        pairs = set()
        for core in (0, 1):
            for near, far in ((low, low + 1), (chips - 1 - low, chips - 2 - low)):
                if inward:
                    pairs.add((2 * near + core, 2 * far + core))
                if outward:
                    pairs.add((2 * far + core, 2 * near + core))
        return lax.ppermute(array, "exp", sorted(pairs))

    def columns_of(array, core, at, width):
        return lax.dynamic_slice_in_dim(array, core * half + at, width, 1)

    def both_cores(array, at, width):
        here = columns_of(array, core_at, at, width)
        return here, to_core(columns_of(array, 1 - core_at, at, width))

    def spread_near(piece):
        return [piece, to_ctx(piece, 1), to_ctx(piece, 2)]

    def spread_on(near):
        cut = near[0].shape[0] // 2
        low, high = chain(near[2][:cut], near[1][cut:])
        return near + [to_ctx(low, 1), to_ctx(high, 2)]

    def spread(piece):
        return [piece] + [to_ctx(piece, offset) for offset in range(1, ctx_count)]

    first = sum(widths[0])
    rights = [spread(jnp.concatenate(both_cores(projection, 0, first), axis=0))]

    turned = conv_grad(
        ctx_at.astype(jnp.int32).reshape(1),
        ctx_count,
        out_grad,
        gate_in,
        conv_in,
        scan_grad,
        conv_weight,
        conv_bias,
        skip_scale,
    )
    turned, rights[0] = lax.optimization_barrier((turned, rights[0]))
    lefts = [turned[0], to_core(turned[0])]
    received = [to_ctx(turned[offset], offset) for offset in range(1, ctx_count)]
    lefts[1], projection, resid_grad, routes = lax.optimization_barrier((lefts[1], projection, resid_grad, routes))

    routed = jnp.concatenate([routes.T.astype(jnp.float32), gate_probs.T], axis=0)[None]
    offset = 1
    while offset < exp_count:
        other = lax.ppermute(routed, "exp", [(place, place ^ offset) for place in range(exp_count)])
        routed = jnp.concatenate([routed, other], axis=0)
        offset *= 2
    order = (jnp.arange(exp_count)[:, None] ^ exp_at) == jnp.arange(exp_count)[None, :]
    routed = jnp.sum(jnp.where(order[:, :, None, None], routed[None], 0.0), axis=1)

    rest_here, rest_there = both_cores(projection, first, half - first)
    rest = []
    for group, at in list(zip(widths, starts))[1:]:
        cut = slice(at - first, at - first + sum(group))
        rest.append(jnp.concatenate([rest_here[:, cut], rest_there[:, cut]], axis=0))
    resid_here, resid_there = both_cores(resid_grad, 0, half)
    resid = jnp.where(
        core_at == 0,
        jnp.concatenate([resid_here, resid_there], axis=0),
        jnp.concatenate([resid_there, resid_here], axis=0),
    )

    route_width = routes.shape[1]
    all_routes = routed[:, :route_width]
    all_probs = routed[:, route_width:]
    capacity = max(2, 14 * tok_rows // (4 * EXP_DEV * exp_count))
    experts = jnp.stack([exp_at, exp_at ^ 1]).astype(jnp.float32)
    named = all_routes[None] == experts[:, None, None, None]
    hit = jnp.any(named, axis=2)
    prob = jnp.sum(jnp.where(named, all_probs[None], 0.0), axis=2)
    count = hit.astype(jnp.int32)
    rank = jnp.cumsum(count, axis=2) - count
    slot = jnp.where(hit, rank + (jnp.arange(exp_count, dtype=jnp.int32) % 2)[None, :, None] * capacity, -1)
    slot = slot.reshape(2, chips, 1, tile)
    picks = slot == jnp.arange(2 * capacity, dtype=jnp.int32)[None, None, :, None]
    scale = jnp.sum(jnp.where(picks, prob.reshape(2, chips, 1, tile), 0.0), axis=3, keepdims=True)
    picks = picks.astype(jnp.bfloat16)

    square = ctx_count == 4
    rights.append(spread_near(rest[0]) if square else spread(rest[0]))
    received, rest, rights[1], resid, picks, scale = lax.optimization_barrier(
        (received, rest, rights[1], resid, picks, scale)
    )
    for piece in received:
        lefts += [piece, to_core(piece)]

    if channels < 128:
        lefts = [jnp.concatenate(lefts, axis=1)]
    place = chip_at.astype(jnp.int32).reshape(1)
    pieces = sum(map(len, GROUPS))
    token = [place]

    def chain(*arrays):
        *arrays, token[0] = lax.optimization_barrier((*arrays, token[0]))
        token[0] = arrays[0]
        return arrays

    def products(group_at, right, only=None):
        group, at = widths[group_at], starts[group_at]
        if channels < 128:
            right = [jnp.concatenate(right, axis=0)]
        right = chain(*right)
        found = matmul(lefts, right, resid[:, at : at + sum(group)], place, group, only)
        token[0] = found[0]
        return found if only is None else found[0]

    middle = chips // 2
    distance = jnp.minimum(chip_at, chips - 1 - chip_at)
    rows_own, rows_got, waiting = [], [], []

    def add(one, other):
        return (one.astype(jnp.float32) + other.astype(jnp.float32)).astype(jnp.bfloat16)

    def finish(grads):
        width = grads.shape[1]
        rows = jnp.einsum("eist,itf->eisf", picks, grads.reshape(chips, tile, width), preferred_element_type=jnp.float32)
        rows = (rows * scale).astype(jnp.bfloat16).reshape(2, chips * 2 * capacity, width)
        rows_own.append(rows[0])
        waiting.append(rows[1])
        if len(rows_own) in SWAPS:
            rows_got.append(to_core(jnp.concatenate(waiting, axis=1)))
            waiting.clear()

    hops = middle - 1
    lag = DELAY - 1
    sums = [[None] * pieces for _ in range(hops + 1)]
    ready = [[None] * pieces for _ in range(hops + 1)]
    outer, across = {}, {}
    first_of = [sum(map(len, GROUPS[:at])) for at in range(len(GROUPS))]
    sums[0][0] = products(0, rights[0], 0)
    rights += [None] * (len(GROUPS) - len(rights))
    for step in range(pieces + 2 * lag * hops + DELAY + 1):
        for hop in range(hops):
            if (step - 2, hop) not in outer:
                continue
            got, inward, outward = outer[step - 2, hop]
            if inward is not None:
                own, got = chain(sums[hop][inward], got)
                sums[hop + 1][inward] = token[0] = add(own, got)
                if hop == hops - 1:
                    across[step] = (swap_chips(token[0], middle - 1), inward)
            if outward is not None:
                ready[hop][outward] = jnp.where(distance == hop, got, ready[hop + 1][outward])
                if hop == 0:
                    finish(ready[0][outward])
        if step - 1 in across:
            got, index = across[step - 1]
            own, got = chain(sums[hops][index], got)
            ready[hops][index] = add(own, got)
        if step in SECOND_PHASE and square:
            rights[SECOND_PHASE[step]] = spread_on(rights[SECOND_PHASE[step]])
        group_at = first_of.index(step) if step and step in first_of else None
        if step in FIRST_PHASE:
            coming = FIRST_PHASE[step]
            piece, *rights[group_at] = chain(rest[coming - 1], *rights[group_at])
            rights[coming] = spread_near(piece) if square else spread(piece)
        if group_at:
            sums[0][step : step + len(GROUPS[group_at])] = products(group_at, rights[group_at])
        for hop in range(hops):
            inward = step - lag * hop
            outward = inward - DELAY - 2 * lag * (hops - 1 - hop)
            inward = inward if 0 <= inward < pieces else None
            outward = outward if 0 <= outward < pieces else None
            if inward is not None and outward is not None:
                payload = jnp.where(distance == hop, sums[hop][inward], ready[hop + 1][outward])
            elif inward is not None:
                payload = sums[hop][inward]
            elif outward is not None:
                payload = ready[hop + 1][outward]
            else:
                continue
            (payload,) = chain(payload)
            outer[step, hop] = (swap_chips(payload, hop, inward is not None, outward is not None), inward, outward)
        if step == 0:
            if square:
                rights[1] = spread_on(rights[1])
            sums[0][1] = products(0, rights[0], 1)
    result = jnp.where(
        core_at == 0,
        jnp.concatenate(rows_own + rows_got, axis=1),
        jnp.concatenate(rows_got + rows_own, axis=1),
    )
    return result[None]


def solution(mesh):
    placed = (
        P(("ctx", "exp"), None),
        P(("ctx", "exp"), None),
        P(("ctx", "exp"), None),
        P(("ctx", "exp"), None),
        P(None, ("ctx", "exp")),
        P(("ctx", "exp")),
        P(("ctx", "exp")),
        P(("ctx", "exp"), None),
        P(("ctx", "exp"), None),
        P(("ctx", "exp"), None),
        P(("ctx", "exp"), None),
    )
    return jax.shard_map(
        on_device, mesh=mesh, in_specs=placed, out_specs=P("exp", "ctx", None), check_vma=False
    )
```

```python
import functools

import jax
import jax.numpy as jnp
from jax import lax
from jax.experimental import pallas as pl
from jax.experimental.pallas import tpu as pltpu
from jax.sharding import PartitionSpec as P

EXP_DEV = 1
GROUPS = ((1,), (1,), (1, 1), (1, 1), (1, 1))
GATHERED = (3, 4)
GATHER_AT = {2: 4}
UNITS = sum(map(sum, GROUPS))
DELAY = 3
SWAPS = (6, 8)
VMEM_BYTES = 60 * 1024 * 1024


def conv_kernel(tile, at_ctx, out_grad, gate_in, conv_in, scan_grad, taps, bias, skip, *refs):
    turned, flat, columns_of = refs[:-2], refs[-2], refs[-1]
    channels, length = out_grad.shape
    window = length // len(turned)
    kernel_taps = taps.shape[0]
    rows_at_once = 16
    settings = jnp.concatenate(
        [0.5 * taps[...], 0.5 * bias[...], skip[...], jnp.zeros((8 - kernel_taps - 2, channels), jnp.float32)], axis=0
    )
    columns_of[...] = settings.T

    def row_group(group, _):
        row_at = pl.multiple_of(group * rows_at_once, rows_at_once)
        rows = pl.ds(row_at, rows_at_once)

        def spread(index, width=tile):
            column = jnp.broadcast_to(columns_of[rows, index : index + 1], (rows_at_once, 128))
            return jnp.concatenate([column] * (width // 128), axis=1)

        weights = [spread(tap) for tap in range(kernel_taps)]
        wider = [spread(tap, tile + 128) for tap in (0, 1)]
        bias_half = spread(kernel_taps)
        skip_value = spread(kernel_taps + 1)
        after = jnp.zeros((rows_at_once, 128), jnp.float32)
        for at in range(length - tile, -1, -tile):
            columns = pl.ds(at, tile)
            gate = 0.5 * gate_in[rows, columns].astype(jnp.float32)
            gated = out_grad[rows, columns].astype(jnp.float32) * (gate + gate * jnp.tanh(gate))
            here = conv_in[rows, columns].astype(jnp.float32)
            if at:
                before = conv_in[rows, pl.ds(at - 128, 128)].astype(jnp.float32)
            else:
                before = jnp.zeros((rows_at_once, 128), jnp.float32)
            wide = jnp.concatenate([before, here], axis=1)
            one_back = pltpu.roll(wide, 1, 1)
            older = wider[1] * wide + wider[0] * one_back
            half = bias_half + weights[3] * here + weights[2] * one_back[:, 128:]
            half = half + pltpu.roll(older, 2, 1)[:, 128:]
            turn = jnp.tanh(half)
            scan = scan_grad[rows, columns].astype(jnp.float32)
            grad = (scan + skip_value * gated) * (1.0 + turn + half * (1.0 - turn * turn))
            wide_grad = jnp.concatenate([grad, after], axis=1)
            one_on = pltpu.roll(wide_grad, tile + 127, 1)
            later = wider[1] * wide_grad + wider[0] * one_on
            total = weights[3] * grad + weights[2] * one_on[:, :tile]
            total = total + pltpu.roll(later, tile + 126, 1)[:, :tile]
            flat[rows, columns] = total.astype(flat.dtype)
            after = grad[:, :128]
        return 0

    lax.fori_loop(0, channels // rows_at_once, row_group, 0)
    for offset, out in enumerate(turned):
        from_at = (at_ctx[0] ^ offset) * window
        for at in range(0, window, tile):
            out[pl.ds(at, tile), :] = flat[:, pl.ds(pl.multiple_of(from_at + at, tile), tile)].T


def conv_grad(at_ctx, ctx_count, out_grad, gate_in, conv_in, scan_grad, conv_weight, conv_bias, skip_scale):
    channels, length = out_grad.shape
    block = min(128, channels)
    window = length // ctx_count
    tile = min(512, window)
    whole = pl.BlockSpec((block, length), lambda step, at_ctx: (step, 0))
    row = pl.BlockSpec((1, block), lambda step, at_ctx: (0, step))
    return pl.pallas_call(
        functools.partial(conv_kernel, tile),
        grid_spec=pltpu.PrefetchScalarGridSpec(
            num_scalar_prefetch=1,
            grid=(channels // block,),
            in_specs=[whole] * 4
            + [pl.BlockSpec((conv_weight.shape[0], block), lambda step, at_ctx: (0, step)), row, row],
            out_specs=[pl.BlockSpec((window, block), lambda step, at_ctx: (0, step))] * ctx_count,
            scratch_shapes=[pltpu.VMEM((block, length), jnp.bfloat16), pltpu.VMEM((block, 8), jnp.float32)],
        ),
        out_shape=[jax.ShapeDtypeStruct((window, channels), jnp.bfloat16)] * ctx_count,
        compiler_params=pltpu.CompilerParams(vmem_limit_bytes=VMEM_BYTES),
        cost_estimate=pl.CostEstimate(
            flops=40 * channels * length, bytes_accessed=10 * channels * length, transcendentals=2 * channels * length
        ),
        name="conv_grad",
    )(at_ctx, out_grad, gate_in, conv_in, scan_grad, conv_weight, conv_bias[None], skip_scale[None])


def matmul_kernel(lefts, rights, place, *refs):
    left_refs = refs[:lefts]
    right_refs = refs[lefts : lefts + rights]
    resid = refs[lefts + rights]
    outs = refs[lefts + rights + 1 :]
    left = jnp.concatenate([ref[...] for ref in left_refs], axis=1)
    right = jnp.concatenate([ref[...] for ref in right_refs], axis=0)
    total = jnp.dot(left, right, preferred_element_type=jnp.float32)
    many = left.shape[0] // resid.shape[0]
    parts = []
    for part in range(many):
        mine = pl.program_id(0) * many + part == place[0]
        rows = total[part * resid.shape[0] : (part + 1) * resid.shape[0]]
        parts.append(rows + jnp.where(mine, resid[...].astype(jnp.float32), 0.0))
    total = jnp.concatenate(parts, axis=0)
    at = 0
    for out in outs:
        out[...] = total[:, at : at + out.shape[1]].astype(out.dtype)
        at += out.shape[1]


def matmul(lefts, rights, resid, place, widths, gathered=0):
    tokens, depth = lefts[0].shape
    width = rights[0].shape[1]
    tile = 2 * resid.shape[0]
    right_specs = [pl.BlockSpec(right.shape, lambda step, place: (0, 0)) for right in rights]
    if gathered:
        rows = rights[0].shape[0] // gathered
        rights = rights * gathered
        right_specs = [
            pl.BlockSpec((rows, width), functools.partial(lambda offset, step, place: (place[1] ^ offset, 0), offset))
            for offset in range(gathered)
        ]
    flops = 2 * tokens * depth * len(lefts) * width
    moved = 2 * (tokens * depth * len(lefts) + depth * len(lefts) * width + tokens * width)
    return pl.pallas_call(
        functools.partial(matmul_kernel, len(lefts), len(rights)),
        grid_spec=pltpu.PrefetchScalarGridSpec(
            num_scalar_prefetch=1,
            grid=(tokens // tile,),
            in_specs=[pl.BlockSpec((tile, depth), lambda step, place: (step, 0))] * len(lefts)
            + right_specs
            + [pl.BlockSpec(resid.shape, lambda step, place: (0, 0))],
            out_specs=[pl.BlockSpec((tile, part), lambda step, place: (step, 0)) for part in widths],
        ),
        out_shape=[jax.ShapeDtypeStruct((tokens, part), jnp.bfloat16) for part in widths],
        compiler_params=pltpu.CompilerParams(vmem_limit_bytes=VMEM_BYTES),
        cost_estimate=pl.CostEstimate(flops=flops, bytes_accessed=moved, transcendentals=0),
        name="partial_product",
    )(place, *lefts, *rights, resid)


def on_device(
    out_grad,
    gate_in,
    conv_in,
    scan_grad,
    conv_weight,
    conv_bias,
    skip_scale,
    projection,
    resid_grad,
    routes,
    gate_probs,
):
    ctx_count = lax.axis_size("ctx")
    exp_count = lax.axis_size("exp")
    chips = exp_count // 2
    ctx_at = lax.axis_index("ctx")
    exp_at = lax.axis_index("exp")
    chip_at = exp_at // 2
    core_at = exp_at % 2
    channels, length = out_grad.shape
    features = projection.shape[1]
    half = features // 2
    unit = half // UNITS
    widths = [[unit * part for part in group] for group in GROUPS]
    starts = [sum(map(sum, widths[:at])) for at in range(len(widths))]
    tok_rows = resid_grad.shape[0]
    window = tok_rows * exp_count
    tile = 2 * tok_rows

    def to_core(array):
        return lax.ppermute(array, "exp", [(place, place ^ 1) for place in range(exp_count)])

    def to_ctx(array, offset):
        return lax.ppermute(array, "ctx", [(place, place ^ offset) for place in range(ctx_count)])

    def swap_chips(array, low, inward=True, outward=True):
        pairs = set()
        for core in (0, 1):
            for near, far in ((low, low + 1), (chips - 1 - low, chips - 2 - low)):
                if inward:
                    pairs.add((2 * near + core, 2 * far + core))
                if outward:
                    pairs.add((2 * far + core, 2 * near + core))
        return lax.ppermute(array, "exp", sorted(pairs))

    def columns_of(array, core, at, width):
        return lax.dynamic_slice_in_dim(array, core * half + at, width, 1)

    def both_cores(array, at, width):
        here = columns_of(array, core_at, at, width)
        return here, to_core(columns_of(array, 1 - core_at, at, width))

    def spread_near(piece):
        return [piece, to_ctx(piece, 1), to_ctx(piece, 2)]

    def spread_on(near):
        cut = near[0].shape[0] // 2
        low, high = chain(near[2][:cut], near[1][cut:])
        return near + [to_ctx(low, 1), to_ctx(high, 2)]

    def spread(piece):
        return [piece] + [to_ctx(piece, offset) for offset in range(1, ctx_count)]

    first = sum(widths[0])
    rights = [spread(jnp.concatenate(both_cores(projection, 0, first), axis=0))]

    turned = conv_grad(
        ctx_at.astype(jnp.int32).reshape(1),
        ctx_count,
        out_grad,
        gate_in,
        conv_in,
        scan_grad,
        conv_weight,
        conv_bias,
        skip_scale,
    )
    turned, rights[0] = lax.optimization_barrier((turned, rights[0]))
    lefts = [turned[0], to_core(turned[0])]
    received = [to_ctx(turned[offset], offset) for offset in range(1, ctx_count)]
    lefts[1], projection, resid_grad, routes = lax.optimization_barrier((lefts[1], projection, resid_grad, routes))

    routed = jnp.concatenate([routes.T.astype(jnp.float32), gate_probs.T], axis=0)[None]
    offset = 1
    while offset < exp_count:
        other = lax.ppermute(routed, "exp", [(place, place ^ offset) for place in range(exp_count)])
        routed = jnp.concatenate([routed, other], axis=0)
        offset *= 2
    order = (jnp.arange(exp_count)[:, None] ^ exp_at) == jnp.arange(exp_count)[None, :]
    routed = jnp.sum(jnp.where(order[:, :, None, None], routed[None], 0.0), axis=1)

    rest_here, rest_there = both_cores(projection, first, half - first)
    rest = []
    for group, at in list(zip(widths, starts))[1:]:
        cut = slice(at - first, at - first + sum(group))
        rest.append(jnp.concatenate([rest_here[:, cut], rest_there[:, cut]], axis=0))
    resid_here, resid_there = both_cores(resid_grad, 0, half)
    resid = jnp.where(
        core_at == 0,
        jnp.concatenate([resid_here, resid_there], axis=0),
        jnp.concatenate([resid_there, resid_here], axis=0),
    )

    route_width = routes.shape[1]
    all_routes = routed[:, :route_width]
    all_probs = routed[:, route_width:]
    capacity = max(2, 14 * tok_rows // (4 * EXP_DEV * exp_count))
    experts = jnp.stack([exp_at, exp_at ^ 1]).astype(jnp.float32)
    named = all_routes[None] == experts[:, None, None, None]
    hit = jnp.any(named, axis=2)
    prob = jnp.sum(jnp.where(named, all_probs[None], 0.0), axis=2)
    count = hit.astype(jnp.int32)
    rank = jnp.cumsum(count, axis=2) - count
    slot = jnp.where(hit, rank + (jnp.arange(exp_count, dtype=jnp.int32) % 2)[None, :, None] * capacity, -1)
    slot = slot.reshape(2, chips, 1, tile)
    picks = slot == jnp.arange(2 * capacity, dtype=jnp.int32)[None, None, :, None]
    scale = jnp.sum(jnp.where(picks, prob.reshape(2, chips, 1, tile), 0.0), axis=3, keepdims=True)
    picks = picks.astype(jnp.bfloat16)

    rights.append(spread(rest[0]))
    received, rest, rights[1], resid, picks, scale = lax.optimization_barrier(
        (received, rest, rights[1], resid, picks, scale)
    )
    for piece in received:
        lefts += [piece, to_core(piece)]

    if channels < 128:
        lefts = [jnp.concatenate(lefts, axis=1)]
    place = jnp.stack([chip_at, ctx_at]).astype(jnp.int32)
    pieces = sum(map(len, GROUPS))
    token = [place]

    def chain(*arrays):
        *arrays, token[0] = lax.optimization_barrier((*arrays, token[0]))
        token[0] = arrays[0]
        return arrays

    def products(group_at):
        group, at = widths[group_at], starts[group_at]
        right = chain(*rights[group_at])
        gathered = ctx_count if group_at in GATHERED else 0
        if channels < 128:
            right = [jnp.concatenate(right, axis=0)]
            if gathered:
                right = right[0].reshape(ctx_count, -1, sum(group))[ctx_at ^ jnp.arange(ctx_count)]
                right, gathered = [right.reshape(-1, sum(group))], 0
        found = matmul(lefts, right, resid[:, at : at + sum(group)], place, group, gathered)
        token[0] = found[0]
        return found

    def gather(group_at):
        return [lax.all_gather(rest[group_at - 1], "ctx", axis=0, tiled=True)]

    middle = chips // 2
    distance = jnp.minimum(chip_at, chips - 1 - chip_at)
    rows_own, rows_got, waiting = [], [], []

    def add(one, other):
        return (one.astype(jnp.float32) + other.astype(jnp.float32)).astype(jnp.bfloat16)

    def finish(grads):
        width = grads.shape[1]
        rows = jnp.einsum("eist,itf->eisf", picks, grads.reshape(chips, tile, width), preferred_element_type=jnp.float32)
        rows = (rows * scale).astype(jnp.bfloat16).reshape(2, chips * 2 * capacity, width)
        rows_own.append(rows[0])
        waiting.append(rows[1])
        if len(rows_own) in SWAPS:
            rows_got.append(to_core(jnp.concatenate(waiting, axis=1)))
            waiting.clear()

    square = ctx_count == 4
    hops = middle - 1
    lag = DELAY - 1
    sums = [[None] * pieces for _ in range(hops + 1)]
    ready = [[None] * pieces for _ in range(hops + 1)]
    outer, across = {}, {}
    first_of = [sum(map(len, GROUPS[:at])) for at in range(len(GROUPS))]
    lefts, rest[1] = lax.optimization_barrier((lefts, rest[1]))
    rights.append(spread_near(rest[1]) if square else spread(rest[1]))
    rights += [None] * (len(GROUPS) - len(rights))
    rights[3] = gather(3)
    sums[0][: len(GROUPS[0])] = products(0)
    for step in range(pieces + 2 * lag * hops + DELAY + 1):
        for hop in range(hops):
            if (step - 2, hop) not in outer:
                continue
            got, inward, outward = outer[step - 2, hop]
            if inward is not None:
                own, got = chain(sums[hop][inward], got)
                sums[hop + 1][inward] = token[0] = add(own, got)
                if hop == hops - 1:
                    across[step] = (swap_chips(token[0], middle - 1), inward)
            if outward is not None:
                ready[hop][outward] = jnp.where(distance == hop, got, ready[hop + 1][outward])
                if hop == 0:
                    finish(ready[0][outward])
        if step - 1 in across:
            got, index = across[step - 1]
            own, got = chain(sums[hops][index], got)
            ready[hops][index] = add(own, got)
        if step in GATHER_AT:
            (rest[GATHER_AT[step] - 1],) = chain(rest[GATHER_AT[step] - 1])
            rights[GATHER_AT[step]] = gather(GATHER_AT[step])
        if step and step in first_of:
            group_at = first_of.index(step)
            sums[0][step : step + len(GROUPS[group_at])] = products(group_at)
        for hop in range(hops):
            inward = step - lag * hop
            outward = inward - DELAY - 2 * lag * (hops - 1 - hop)
            inward = inward if 0 <= inward < pieces else None
            outward = outward if 0 <= outward < pieces else None
            if inward is not None and outward is not None:
                payload = jnp.where(distance == hop, sums[hop][inward], ready[hop + 1][outward])
            elif inward is not None:
                payload = sums[hop][inward]
            elif outward is not None:
                payload = ready[hop + 1][outward]
            else:
                continue
            (payload,) = chain(payload)
            outer[step, hop] = (swap_chips(payload, hop, inward is not None, outward is not None), inward, outward)
        if step == 1 and square:
            rights[2] = spread_on(rights[2])
    result = jnp.where(
        core_at == 0,
        jnp.concatenate(rows_own + rows_got, axis=1),
        jnp.concatenate(rows_got + rows_own, axis=1),
    )
    return result[None]


def solution(mesh):
    placed = (
        P(("ctx", "exp"), None),
        P(("ctx", "exp"), None),
        P(("ctx", "exp"), None),
        P(("ctx", "exp"), None),
        P(None, ("ctx", "exp")),
        P(("ctx", "exp")),
        P(("ctx", "exp")),
        P(("ctx", "exp"), None),
        P(("ctx", "exp"), None),
        P(("ctx", "exp"), None),
        P(("ctx", "exp"), None),
    )
    return jax.shard_map(
        on_device, mesh=mesh, in_specs=placed, out_specs=P("exp", "ctx", None), check_vma=False
    )
```

```python
import functools

import jax
import jax.numpy as jnp
from jax import lax
from jax.experimental import pallas as pl
from jax.experimental.pallas import tpu as pltpu
from jax.sharding import PartitionSpec as P

EXP_DEV = 1
GROUPS = ((1,), (1,), (1, 1), (1, 1), (1, 1))
FIRST_PHASE = {2: 3, 4: 4}
SECOND_PHASE = {3: 3, 5: 4}
UNITS = sum(map(sum, GROUPS))
DELAY = 3
SWAPS = (6, 8)
VMEM_BYTES = 60 * 1024 * 1024


def conv_kernel(tile, at_ctx, out_grad, gate_in, conv_in, scan_grad, taps, bias, skip, *refs):
    turned, flat, columns_of = refs[:-2], refs[-2], refs[-1]
    channels, length = out_grad.shape
    window = length // len(turned)
    kernel_taps = taps.shape[0]
    rows_at_once = 16
    settings = jnp.concatenate(
        [0.5 * taps[...], 0.5 * bias[...], skip[...], jnp.zeros((8 - kernel_taps - 2, channels), jnp.float32)], axis=0
    )
    columns_of[...] = settings.T

    def row_group(group, _):
        row_at = pl.multiple_of(group * rows_at_once, rows_at_once)
        rows = pl.ds(row_at, rows_at_once)

        def spread(index, width=tile):
            column = jnp.broadcast_to(columns_of[rows, index : index + 1], (rows_at_once, 128))
            return jnp.concatenate([column] * (width // 128), axis=1)

        weights = [spread(tap) for tap in range(kernel_taps)]
        wider = [spread(tap, tile + 128) for tap in (0, 1)]
        bias_half = spread(kernel_taps)
        skip_value = spread(kernel_taps + 1)
        after = jnp.zeros((rows_at_once, 128), jnp.float32)
        for at in range(length - tile, -1, -tile):
            columns = pl.ds(at, tile)
            gate = 0.5 * gate_in[rows, columns].astype(jnp.float32)
            gated = out_grad[rows, columns].astype(jnp.float32) * (gate + gate * jnp.tanh(gate))
            here = conv_in[rows, columns].astype(jnp.float32)
            if at:
                before = conv_in[rows, pl.ds(at - 128, 128)].astype(jnp.float32)
            else:
                before = jnp.zeros((rows_at_once, 128), jnp.float32)
            wide = jnp.concatenate([before, here], axis=1)
            one_back = pltpu.roll(wide, 1, 1)
            older = wider[1] * wide + wider[0] * one_back
            half = bias_half + weights[3] * here + weights[2] * one_back[:, 128:]
            half = half + pltpu.roll(older, 2, 1)[:, 128:]
            turn = jnp.tanh(half)
            scan = scan_grad[rows, columns].astype(jnp.float32)
            grad = (scan + skip_value * gated) * (1.0 + turn + half * (1.0 - turn * turn))
            wide_grad = jnp.concatenate([grad, after], axis=1)
            one_on = pltpu.roll(wide_grad, tile + 127, 1)
            later = wider[1] * wide_grad + wider[0] * one_on
            total = weights[3] * grad + weights[2] * one_on[:, :tile]
            total = total + pltpu.roll(later, tile + 126, 1)[:, :tile]
            flat[rows, columns] = total.astype(flat.dtype)
            after = grad[:, :128]
        return 0

    lax.fori_loop(0, channels // rows_at_once, row_group, 0)
    for offset, out in enumerate(turned):
        from_at = (at_ctx[0] ^ offset) * window
        for at in range(0, window, tile):
            out[pl.ds(at, tile), :] = flat[:, pl.ds(pl.multiple_of(from_at + at, tile), tile)].T


def conv_grad(at_ctx, ctx_count, out_grad, gate_in, conv_in, scan_grad, conv_weight, conv_bias, skip_scale):
    channels, length = out_grad.shape
    block = min(128, channels)
    window = length // ctx_count
    tile = min(512, window)
    whole = pl.BlockSpec((block, length), lambda step, at_ctx: (step, 0))
    row = pl.BlockSpec((1, block), lambda step, at_ctx: (0, step))
    return pl.pallas_call(
        functools.partial(conv_kernel, tile),
        grid_spec=pltpu.PrefetchScalarGridSpec(
            num_scalar_prefetch=1,
            grid=(channels // block,),
            in_specs=[whole] * 4
            + [pl.BlockSpec((conv_weight.shape[0], block), lambda step, at_ctx: (0, step)), row, row],
            out_specs=[pl.BlockSpec((window, block), lambda step, at_ctx: (0, step))] * ctx_count,
            scratch_shapes=[pltpu.VMEM((block, length), jnp.bfloat16), pltpu.VMEM((block, 8), jnp.float32)],
        ),
        out_shape=[jax.ShapeDtypeStruct((window, channels), jnp.bfloat16)] * ctx_count,
        compiler_params=pltpu.CompilerParams(vmem_limit_bytes=VMEM_BYTES),
        cost_estimate=pl.CostEstimate(
            flops=40 * channels * length, bytes_accessed=10 * channels * length, transcendentals=2 * channels * length
        ),
        name="conv_grad",
    )(at_ctx, out_grad, gate_in, conv_in, scan_grad, conv_weight, conv_bias[None], skip_scale[None])


def matmul_kernel(lefts, rights, place, *refs):
    left_refs = refs[:lefts]
    right_refs = refs[lefts : lefts + rights]
    resid = refs[lefts + rights]
    outs = refs[lefts + rights + 1 :]
    left = jnp.concatenate([ref[...] for ref in left_refs], axis=1)
    right = jnp.concatenate([ref[...] for ref in right_refs], axis=0)
    total = jnp.dot(left, right, preferred_element_type=jnp.float32)
    many = left.shape[0] // resid.shape[0]
    parts = []
    for part in range(many):
        mine = pl.program_id(0) * many + part == place[0]
        rows = total[part * resid.shape[0] : (part + 1) * resid.shape[0]]
        parts.append(rows + jnp.where(mine, resid[...].astype(jnp.float32), 0.0))
    total = jnp.concatenate(parts, axis=0)
    at = 0
    for out in outs:
        out[...] = total[:, at : at + out.shape[1]].astype(out.dtype)
        at += out.shape[1]


def matmul(lefts, rights, resid, place, widths):
    tokens, depth = lefts[0].shape
    width = rights[0].shape[1]
    tile = 2 * resid.shape[0]
    flops = 2 * tokens * depth * len(lefts) * width
    moved = 2 * (tokens * depth * len(lefts) + depth * len(lefts) * width + tokens * width)
    return pl.pallas_call(
        functools.partial(matmul_kernel, len(lefts), len(rights)),
        grid_spec=pltpu.PrefetchScalarGridSpec(
            num_scalar_prefetch=1,
            grid=(tokens // tile,),
            in_specs=[pl.BlockSpec((tile, depth), lambda step, place: (step, 0))] * len(lefts)
            + [pl.BlockSpec(right.shape, lambda step, place: (0, 0)) for right in rights]
            + [pl.BlockSpec(resid.shape, lambda step, place: (0, 0))],
            out_specs=[pl.BlockSpec((tile, part), lambda step, place: (step, 0)) for part in widths],
        ),
        out_shape=[jax.ShapeDtypeStruct((tokens, part), jnp.bfloat16) for part in widths],
        compiler_params=pltpu.CompilerParams(vmem_limit_bytes=VMEM_BYTES),
        cost_estimate=pl.CostEstimate(flops=flops, bytes_accessed=moved, transcendentals=0),
        name="partial_product",
    )(place, *lefts, *rights, resid)


def on_device(
    out_grad,
    gate_in,
    conv_in,
    scan_grad,
    conv_weight,
    conv_bias,
    skip_scale,
    projection,
    resid_grad,
    routes,
    gate_probs,
):
    ctx_count = lax.axis_size("ctx")
    exp_count = lax.axis_size("exp")
    chips = exp_count // 2
    ctx_at = lax.axis_index("ctx")
    exp_at = lax.axis_index("exp")
    chip_at = exp_at // 2
    core_at = exp_at % 2
    channels, length = out_grad.shape
    features = projection.shape[1]
    half = features // 2
    unit = half // UNITS
    widths = [[unit * part for part in group] for group in GROUPS]
    starts = [sum(map(sum, widths[:at])) for at in range(len(widths))]
    tok_rows = resid_grad.shape[0]
    window = tok_rows * exp_count
    tile = 2 * tok_rows

    def to_core(array):
        return lax.ppermute(array, "exp", [(place, place ^ 1) for place in range(exp_count)])

    def to_ctx(array, offset):
        return lax.ppermute(array, "ctx", [(place, place ^ offset) for place in range(ctx_count)])

    def swap_chips(array, low, inward=True, outward=True):
        pairs = set()
        for core in (0, 1):
            for near, far in ((low, low + 1), (chips - 1 - low, chips - 2 - low)):
                if inward:
                    pairs.add((2 * near + core, 2 * far + core))
                if outward:
                    pairs.add((2 * far + core, 2 * near + core))
        return lax.ppermute(array, "exp", sorted(pairs))

    def columns_of(array, core, at, width):
        return lax.dynamic_slice_in_dim(array, core * half + at, width, 1)

    def both_cores(array, at, width):
        here = columns_of(array, core_at, at, width)
        return here, to_core(columns_of(array, 1 - core_at, at, width))

    def spread_near(piece):
        return [piece, to_ctx(piece, 1), to_ctx(piece, 2)]

    def spread_far(near):
        (piece,) = chain(near[0])
        return near + [to_ctx(piece, 3)]

    def spread(piece):
        return [piece] + [to_ctx(piece, offset) for offset in range(1, ctx_count)]

    first = sum(widths[0])
    rights = [spread(jnp.concatenate(both_cores(projection, 0, first), axis=0))]

    turned = conv_grad(
        ctx_at.astype(jnp.int32).reshape(1),
        ctx_count,
        out_grad,
        gate_in,
        conv_in,
        scan_grad,
        conv_weight,
        conv_bias,
        skip_scale,
    )
    turned, rights[0] = lax.optimization_barrier((turned, rights[0]))
    lefts = [turned[0], to_core(turned[0])]
    received = [to_ctx(turned[offset], offset) for offset in range(1, ctx_count)]
    lefts[1], projection, resid_grad, routes = lax.optimization_barrier((lefts[1], projection, resid_grad, routes))

    routed = jnp.concatenate([routes.T.astype(jnp.float32), gate_probs.T], axis=0)[None]
    offset = 1
    while offset < exp_count:
        other = lax.ppermute(routed, "exp", [(place, place ^ offset) for place in range(exp_count)])
        routed = jnp.concatenate([routed, other], axis=0)
        offset *= 2
    order = (jnp.arange(exp_count)[:, None] ^ exp_at) == jnp.arange(exp_count)[None, :]
    routed = jnp.sum(jnp.where(order[:, :, None, None], routed[None], 0.0), axis=1)

    rest_here, rest_there = both_cores(projection, first, half - first)
    rest = []
    for group, at in list(zip(widths, starts))[1:]:
        cut = slice(at - first, at - first + sum(group))
        rest.append(jnp.concatenate([rest_here[:, cut], rest_there[:, cut]], axis=0))
    resid_here, resid_there = both_cores(resid_grad, 0, half)
    resid = jnp.where(
        core_at == 0,
        jnp.concatenate([resid_here, resid_there], axis=0),
        jnp.concatenate([resid_there, resid_here], axis=0),
    )

    route_width = routes.shape[1]
    all_routes = routed[:, :route_width]
    all_probs = routed[:, route_width:]
    capacity = max(2, 14 * tok_rows // (4 * EXP_DEV * exp_count))
    experts = jnp.stack([exp_at, exp_at ^ 1]).astype(jnp.float32)
    named = all_routes[None] == experts[:, None, None, None]
    hit = jnp.any(named, axis=2)
    prob = jnp.sum(jnp.where(named, all_probs[None], 0.0), axis=2)
    count = hit.astype(jnp.int32)
    rank = jnp.cumsum(count, axis=2) - count
    slot = jnp.where(hit, rank + (jnp.arange(exp_count, dtype=jnp.int32) % 2)[None, :, None] * capacity, -1)
    slot = slot.reshape(2, chips, 1, tile)
    picks = slot == jnp.arange(2 * capacity, dtype=jnp.int32)[None, None, :, None]
    scale = jnp.sum(jnp.where(picks, prob.reshape(2, chips, 1, tile), 0.0), axis=3, keepdims=True)
    picks = picks.astype(jnp.bfloat16)

    rights.append(spread(rest[0]))
    received, rest, rights[1], resid, picks, scale = lax.optimization_barrier(
        (received, rest, rights[1], resid, picks, scale)
    )
    for piece in received:
        lefts += [piece, to_core(piece)]

    if channels < 128:
        lefts = [jnp.concatenate(lefts, axis=1)]
    place = chip_at.astype(jnp.int32).reshape(1)
    pieces = sum(map(len, GROUPS))
    token = [place]

    def chain(*arrays):
        *arrays, token[0] = lax.optimization_barrier((*arrays, token[0]))
        token[0] = arrays[0]
        return arrays

    def products(group_at, right):
        group, at = widths[group_at], starts[group_at]
        if channels < 128:
            right = [jnp.concatenate(right, axis=0)]
        right = chain(*right)
        found = matmul(lefts, right, resid[:, at : at + sum(group)], place, group)
        token[0] = found[0]
        return found

    middle = chips // 2
    distance = jnp.minimum(chip_at, chips - 1 - chip_at)
    rows_own, rows_got, waiting = [], [], []

    def add(one, other):
        return (one.astype(jnp.float32) + other.astype(jnp.float32)).astype(jnp.bfloat16)

    def finish(grads):
        width = grads.shape[1]
        rows = jnp.einsum("eist,itf->eisf", picks, grads.reshape(chips, tile, width), preferred_element_type=jnp.float32)
        rows = (rows * scale).astype(jnp.bfloat16).reshape(2, chips * 2 * capacity, width)
        rows_own.append(rows[0])
        waiting.append(rows[1])
        if len(rows_own) in SWAPS:
            rows_got.append(to_core(jnp.concatenate(waiting, axis=1)))
            waiting.clear()

    square = ctx_count == 4
    hops = middle - 1
    lag = DELAY - 1
    sums = [[None] * pieces for _ in range(hops + 1)]
    ready = [[None] * pieces for _ in range(hops + 1)]
    outer, across = {}, {}
    first_of = [sum(map(len, GROUPS[:at])) for at in range(len(GROUPS))]
    lefts, rest[1] = lax.optimization_barrier((lefts, rest[1]))
    rights.append(spread_near(rest[1]) if square else spread(rest[1]))
    sums[0][: len(GROUPS[0])] = products(0, rights[0])
    rights += [None] * (len(GROUPS) - len(rights))
    for step in range(pieces + 2 * lag * hops + DELAY + 1):
        for hop in range(hops):
            if (step - 2, hop) not in outer:
                continue
            got, inward, outward = outer[step - 2, hop]
            if inward is not None:
                own, got = chain(sums[hop][inward], got)
                sums[hop + 1][inward] = token[0] = add(own, got)
                if hop == hops - 1:
                    across[step] = (swap_chips(token[0], middle - 1), inward)
            if outward is not None:
                ready[hop][outward] = jnp.where(distance == hop, got, ready[hop + 1][outward])
                if hop == 0:
                    finish(ready[0][outward])
        if step - 1 in across:
            got, index = across[step - 1]
            own, got = chain(sums[hops][index], got)
            ready[hops][index] = add(own, got)
        if step in SECOND_PHASE and square:
            rights[SECOND_PHASE[step]] = spread_far(rights[SECOND_PHASE[step]])
        group_at = first_of.index(step) if step and step in first_of else None
        if step in FIRST_PHASE:
            coming = FIRST_PHASE[step]
            piece, *rights[group_at] = chain(rest[coming - 1], *rights[group_at])
            rights[coming] = spread_near(piece) if square else spread(piece)
        if group_at:
            sums[0][step : step + len(GROUPS[group_at])] = products(group_at, rights[group_at])
        for hop in range(hops):
            inward = step - lag * hop
            outward = inward - DELAY - 2 * lag * (hops - 1 - hop)
            inward = inward if 0 <= inward < pieces else None
            outward = outward if 0 <= outward < pieces else None
            if inward is not None and outward is not None:
                payload = jnp.where(distance == hop, sums[hop][inward], ready[hop + 1][outward])
            elif inward is not None:
                payload = sums[hop][inward]
            elif outward is not None:
                payload = ready[hop + 1][outward]
            else:
                continue
            (payload,) = chain(payload)
            outer[step, hop] = (swap_chips(payload, hop, inward is not None, outward is not None), inward, outward)
        if step == 0 and square:
            rights[2] = spread_far(rights[2])
    result = jnp.where(
        core_at == 0,
        jnp.concatenate(rows_own + rows_got, axis=1),
        jnp.concatenate(rows_got + rows_own, axis=1),
    )
    return result[None]


def solution(mesh):
    placed = (
        P(("ctx", "exp"), None),
        P(("ctx", "exp"), None),
        P(("ctx", "exp"), None),
        P(("ctx", "exp"), None),
        P(None, ("ctx", "exp")),
        P(("ctx", "exp")),
        P(("ctx", "exp")),
        P(("ctx", "exp"), None),
        P(("ctx", "exp"), None),
        P(("ctx", "exp"), None),
        P(("ctx", "exp"), None),
    )
    return jax.shard_map(
        on_device, mesh=mesh, in_specs=placed, out_specs=P("exp", "ctx", None), check_vma=False
    )
```

```python
import functools

import jax
import jax.numpy as jnp
from jax import lax
from jax.experimental import pallas as pl
from jax.experimental.pallas import tpu as pltpu
from jax.sharding import PartitionSpec as P

EXP_DEV = 1
GROUPS = ((1,), (1,), (1, 1), (1, 1), (1, 1))
FIRST_PHASE = {2: 3, 4: 4}
SECOND_PHASE = {3: 3, 5: 4}
UNITS = sum(map(sum, GROUPS))
DELAY = 3
SWAPS = (6, 8)
VMEM_BYTES = 60 * 1024 * 1024


def conv_kernel(tile, at_ctx, out_grad, gate_in, conv_in, scan_grad, taps, bias, skip, *refs):
    turned, flat, columns_of = refs[:-2], refs[-2], refs[-1]
    channels, length = out_grad.shape
    window = length // len(turned)
    kernel_taps = taps.shape[0]
    rows_at_once = 16
    settings = jnp.concatenate(
        [0.5 * taps[...], 0.5 * bias[...], skip[...], jnp.zeros((8 - kernel_taps - 2, channels), jnp.float32)], axis=0
    )
    columns_of[...] = settings.T

    def row_group(group, _):
        row_at = pl.multiple_of(group * rows_at_once, rows_at_once)
        rows = pl.ds(row_at, rows_at_once)

        def spread(index, width=tile):
            column = jnp.broadcast_to(columns_of[rows, index : index + 1], (rows_at_once, 128))
            return jnp.concatenate([column] * (width // 128), axis=1)

        weights = [spread(tap) for tap in range(kernel_taps)]
        wider = [spread(tap, tile + 128) for tap in (0, 1)]
        bias_half = spread(kernel_taps)
        skip_value = spread(kernel_taps + 1)
        after = jnp.zeros((rows_at_once, 128), jnp.float32)
        for at in range(length - tile, -1, -tile):
            columns = pl.ds(at, tile)
            gate = 0.5 * gate_in[rows, columns].astype(jnp.float32)
            gated = out_grad[rows, columns].astype(jnp.float32) * (gate + gate * jnp.tanh(gate))
            here = conv_in[rows, columns].astype(jnp.float32)
            if at:
                before = conv_in[rows, pl.ds(at - 128, 128)].astype(jnp.float32)
            else:
                before = jnp.zeros((rows_at_once, 128), jnp.float32)
            wide = jnp.concatenate([before, here], axis=1)
            one_back = pltpu.roll(wide, 1, 1)
            older = wider[1] * wide + wider[0] * one_back
            half = bias_half + weights[3] * here + weights[2] * one_back[:, 128:]
            half = half + pltpu.roll(older, 2, 1)[:, 128:]
            turn = jnp.tanh(half)
            scan = scan_grad[rows, columns].astype(jnp.float32)
            grad = (scan + skip_value * gated) * (1.0 + turn + half * (1.0 - turn * turn))
            wide_grad = jnp.concatenate([grad, after], axis=1)
            one_on = pltpu.roll(wide_grad, tile + 127, 1)
            later = wider[1] * wide_grad + wider[0] * one_on
            total = weights[3] * grad + weights[2] * one_on[:, :tile]
            total = total + pltpu.roll(later, tile + 126, 1)[:, :tile]
            flat[rows, columns] = total.astype(flat.dtype)
            after = grad[:, :128]
        return 0

    lax.fori_loop(0, channels // rows_at_once, row_group, 0)
    for offset, out in enumerate(turned):
        from_at = (at_ctx[0] ^ offset) * window
        for at in range(0, window, tile):
            out[pl.ds(at, tile), :] = flat[:, pl.ds(pl.multiple_of(from_at + at, tile), tile)].T


def conv_grad(at_ctx, ctx_count, out_grad, gate_in, conv_in, scan_grad, conv_weight, conv_bias, skip_scale):
    channels, length = out_grad.shape
    block = min(128, channels)
    window = length // ctx_count
    tile = min(512, window)
    whole = pl.BlockSpec((block, length), lambda step, at_ctx: (step, 0))
    row = pl.BlockSpec((1, block), lambda step, at_ctx: (0, step))
    return pl.pallas_call(
        functools.partial(conv_kernel, tile),
        grid_spec=pltpu.PrefetchScalarGridSpec(
            num_scalar_prefetch=1,
            grid=(channels // block,),
            in_specs=[whole] * 4
            + [pl.BlockSpec((conv_weight.shape[0], block), lambda step, at_ctx: (0, step)), row, row],
            out_specs=[pl.BlockSpec((window, block), lambda step, at_ctx: (0, step))] * ctx_count,
            scratch_shapes=[pltpu.VMEM((block, length), jnp.bfloat16), pltpu.VMEM((block, 8), jnp.float32)],
        ),
        out_shape=[jax.ShapeDtypeStruct((window, channels), jnp.bfloat16)] * ctx_count,
        compiler_params=pltpu.CompilerParams(vmem_limit_bytes=VMEM_BYTES),
        cost_estimate=pl.CostEstimate(
            flops=40 * channels * length, bytes_accessed=10 * channels * length, transcendentals=2 * channels * length
        ),
        name="conv_grad",
    )(at_ctx, out_grad, gate_in, conv_in, scan_grad, conv_weight, conv_bias[None], skip_scale[None])


def matmul_kernel(lefts, rights, place, *refs):
    left_refs = refs[:lefts]
    right_refs = refs[lefts : lefts + rights]
    resid = refs[lefts + rights]
    outs = refs[lefts + rights + 1 :]
    left = jnp.concatenate([ref[...] for ref in left_refs], axis=1)
    right = jnp.concatenate([ref[...] for ref in right_refs], axis=0)
    total = jnp.dot(left, right, preferred_element_type=jnp.float32)
    many = left.shape[0] // resid.shape[0]
    parts = []
    for part in range(many):
        mine = pl.program_id(0) * many + part == place[0]
        rows = total[part * resid.shape[0] : (part + 1) * resid.shape[0]]
        parts.append(rows + jnp.where(mine, resid[...].astype(jnp.float32), 0.0))
    total = jnp.concatenate(parts, axis=0)
    at = 0
    for out in outs:
        out[...] = total[:, at : at + out.shape[1]].astype(out.dtype)
        at += out.shape[1]


def matmul(lefts, rights, resid, place, widths):
    tokens, depth = lefts[0].shape
    width = rights[0].shape[1]
    tile = 2 * resid.shape[0]
    flops = 2 * tokens * depth * len(lefts) * width
    moved = 2 * (tokens * depth * len(lefts) + depth * len(lefts) * width + tokens * width)
    return pl.pallas_call(
        functools.partial(matmul_kernel, len(lefts), len(rights)),
        grid_spec=pltpu.PrefetchScalarGridSpec(
            num_scalar_prefetch=1,
            grid=(tokens // tile,),
            in_specs=[pl.BlockSpec((tile, depth), lambda step, place: (step, 0))] * len(lefts)
            + [pl.BlockSpec(right.shape, lambda step, place: (0, 0)) for right in rights]
            + [pl.BlockSpec(resid.shape, lambda step, place: (0, 0))],
            out_specs=[pl.BlockSpec((tile, part), lambda step, place: (step, 0)) for part in widths],
        ),
        out_shape=[jax.ShapeDtypeStruct((tokens, part), jnp.bfloat16) for part in widths],
        compiler_params=pltpu.CompilerParams(vmem_limit_bytes=VMEM_BYTES),
        cost_estimate=pl.CostEstimate(flops=flops, bytes_accessed=moved, transcendentals=0),
        name="partial_product",
    )(place, *lefts, *rights, resid)


def on_device(
    out_grad,
    gate_in,
    conv_in,
    scan_grad,
    conv_weight,
    conv_bias,
    skip_scale,
    projection,
    resid_grad,
    routes,
    gate_probs,
):
    ctx_count = lax.axis_size("ctx")
    exp_count = lax.axis_size("exp")
    chips = exp_count // 2
    ctx_at = lax.axis_index("ctx")
    exp_at = lax.axis_index("exp")
    chip_at = exp_at // 2
    core_at = exp_at % 2
    channels, length = out_grad.shape
    features = projection.shape[1]
    half = features // 2
    unit = half // UNITS
    widths = [[unit * part for part in group] for group in GROUPS]
    starts = [sum(map(sum, widths[:at])) for at in range(len(widths))]
    tok_rows = resid_grad.shape[0]
    window = tok_rows * exp_count
    tile = 2 * tok_rows

    def to_core(array):
        return lax.ppermute(array, "exp", [(place, place ^ 1) for place in range(exp_count)])

    def to_ctx(array, offset):
        return lax.ppermute(array, "ctx", [(place, place ^ offset) for place in range(ctx_count)])

    def swap_chips(array, low, inward=True, outward=True):
        pairs = set()
        for core in (0, 1):
            for near, far in ((low, low + 1), (chips - 1 - low, chips - 2 - low)):
                if inward:
                    pairs.add((2 * near + core, 2 * far + core))
                if outward:
                    pairs.add((2 * far + core, 2 * near + core))
        return lax.ppermute(array, "exp", sorted(pairs))

    def columns_of(array, core, at, width):
        return lax.dynamic_slice_in_dim(array, core * half + at, width, 1)

    def both_cores(array, at, width):
        here = columns_of(array, core_at, at, width)
        return here, to_core(columns_of(array, 1 - core_at, at, width))

    def spread_near(piece):
        return [piece, to_ctx(piece, 1), to_ctx(piece, 2)]

    def spread_far(near):
        near = list(chain(*near))
        return near + [to_ctx(near[0], 3)]

    def spread(piece):
        return [piece] + [to_ctx(piece, offset) for offset in range(1, ctx_count)]

    first = sum(widths[0])
    rights = [spread(jnp.concatenate(both_cores(projection, 0, first), axis=0))]

    turned = conv_grad(
        ctx_at.astype(jnp.int32).reshape(1),
        ctx_count,
        out_grad,
        gate_in,
        conv_in,
        scan_grad,
        conv_weight,
        conv_bias,
        skip_scale,
    )
    turned, rights[0] = lax.optimization_barrier((turned, rights[0]))
    lefts = [turned[0], to_core(turned[0])]
    received = [to_ctx(turned[offset], offset) for offset in range(1, ctx_count)]
    lefts[1], projection, resid_grad, routes = lax.optimization_barrier((lefts[1], projection, resid_grad, routes))

    routed = jnp.concatenate([routes.T.astype(jnp.float32), gate_probs.T], axis=0)[None]
    offset = 1
    while offset < exp_count:
        other = lax.ppermute(routed, "exp", [(place, place ^ offset) for place in range(exp_count)])
        routed = jnp.concatenate([routed, other], axis=0)
        offset *= 2
    order = (jnp.arange(exp_count)[:, None] ^ exp_at) == jnp.arange(exp_count)[None, :]
    routed = jnp.sum(jnp.where(order[:, :, None, None], routed[None], 0.0), axis=1)

    rest_here, rest_there = both_cores(projection, first, half - first)
    rest = []
    for group, at in list(zip(widths, starts))[1:]:
        cut = slice(at - first, at - first + sum(group))
        rest.append(jnp.concatenate([rest_here[:, cut], rest_there[:, cut]], axis=0))
    resid_here, resid_there = both_cores(resid_grad, 0, half)
    resid = jnp.where(
        core_at == 0,
        jnp.concatenate([resid_here, resid_there], axis=0),
        jnp.concatenate([resid_there, resid_here], axis=0),
    )

    route_width = routes.shape[1]
    all_routes = routed[:, :route_width]
    all_probs = routed[:, route_width:]
    capacity = max(2, 14 * tok_rows // (4 * EXP_DEV * exp_count))
    experts = jnp.stack([exp_at, exp_at ^ 1]).astype(jnp.float32)
    named = all_routes[None] == experts[:, None, None, None]
    hit = jnp.any(named, axis=2)
    prob = jnp.sum(jnp.where(named, all_probs[None], 0.0), axis=2)
    count = hit.astype(jnp.int32)
    rank = jnp.cumsum(count, axis=2) - count
    slot = jnp.where(hit, rank + (jnp.arange(exp_count, dtype=jnp.int32) % 2)[None, :, None] * capacity, -1)
    slot = slot.reshape(2, chips, 1, tile)
    picks = slot == jnp.arange(2 * capacity, dtype=jnp.int32)[None, None, :, None]
    scale = jnp.sum(jnp.where(picks, prob.reshape(2, chips, 1, tile), 0.0), axis=3, keepdims=True)
    picks = picks.astype(jnp.bfloat16)

    rights.append(spread(rest[0]))
    received, rest, rights[1], resid, picks, scale = lax.optimization_barrier(
        (received, rest, rights[1], resid, picks, scale)
    )
    for piece in received:
        lefts += [piece, to_core(piece)]

    if channels < 128:
        lefts = [jnp.concatenate(lefts, axis=1)]
    place = chip_at.astype(jnp.int32).reshape(1)
    pieces = sum(map(len, GROUPS))
    token = [place]

    def chain(*arrays):
        *arrays, token[0] = lax.optimization_barrier((*arrays, token[0]))
        token[0] = arrays[0]
        return arrays

    def products(group_at, right):
        group, at = widths[group_at], starts[group_at]
        if channels < 128:
            right = [jnp.concatenate(right, axis=0)]
        right = chain(*right)
        found = matmul(lefts, right, resid[:, at : at + sum(group)], place, group)
        token[0] = found[0]
        return found

    middle = chips // 2
    distance = jnp.minimum(chip_at, chips - 1 - chip_at)
    rows_own, rows_got, waiting = [], [], []

    def add(one, other):
        return (one.astype(jnp.float32) + other.astype(jnp.float32)).astype(jnp.bfloat16)

    def finish(grads):
        width = grads.shape[1]
        rows = jnp.einsum("eist,itf->eisf", picks, grads.reshape(chips, tile, width), preferred_element_type=jnp.float32)
        rows = (rows * scale).astype(jnp.bfloat16).reshape(2, chips * 2 * capacity, width)
        rows_own.append(rows[0])
        waiting.append(rows[1])
        if len(rows_own) in SWAPS:
            rows_got.append(to_core(jnp.concatenate(waiting, axis=1)))
            waiting.clear()

    square = ctx_count == 4
    hops = middle - 1
    lag = DELAY - 1
    sums = [[None] * pieces for _ in range(hops + 1)]
    ready = [[None] * pieces for _ in range(hops + 1)]
    outer, across = {}, {}
    first_of = [sum(map(len, GROUPS[:at])) for at in range(len(GROUPS))]
    lefts, rest[1] = lax.optimization_barrier((lefts, rest[1]))
    rights.append(spread_near(rest[1]) if square else spread(rest[1]))
    sums[0][: len(GROUPS[0])] = products(0, rights[0])
    rights += [None] * (len(GROUPS) - len(rights))
    for step in range(pieces + 2 * lag * hops + DELAY + 1):
        for hop in range(hops):
            if (step - 2, hop) not in outer:
                continue
            got, inward, outward = outer[step - 2, hop]
            if inward is not None:
                own, got = chain(sums[hop][inward], got)
                sums[hop + 1][inward] = token[0] = add(own, got)
                if hop == hops - 1:
                    across[step] = (swap_chips(token[0], middle - 1), inward)
            if outward is not None:
                ready[hop][outward] = jnp.where(distance == hop, got, ready[hop + 1][outward])
                if hop == 0:
                    finish(ready[0][outward])
        if step - 1 in across:
            got, index = across[step - 1]
            own, got = chain(sums[hops][index], got)
            ready[hops][index] = add(own, got)
        if step in SECOND_PHASE and square:
            rights[SECOND_PHASE[step]] = spread_far(rights[SECOND_PHASE[step]])
        group_at = first_of.index(step) if step and step in first_of else None
        if step in FIRST_PHASE:
            coming = FIRST_PHASE[step]
            piece, *rights[group_at] = chain(rest[coming - 1], *rights[group_at])
            rights[coming] = spread_near(piece) if square else spread(piece)
        if group_at:
            sums[0][step : step + len(GROUPS[group_at])] = products(group_at, rights[group_at])
        for hop in range(hops):
            inward = step - lag * hop
            outward = inward - DELAY - 2 * lag * (hops - 1 - hop)
            inward = inward if 0 <= inward < pieces else None
            outward = outward if 0 <= outward < pieces else None
            if inward is not None and outward is not None:
                payload = jnp.where(distance == hop, sums[hop][inward], ready[hop + 1][outward])
            elif inward is not None:
                payload = sums[hop][inward]
            elif outward is not None:
                payload = ready[hop + 1][outward]
            else:
                continue
            (payload,) = chain(payload)
            outer[step, hop] = (swap_chips(payload, hop, inward is not None, outward is not None), inward, outward)
        if step == 0 and square:
            (piece,) = chain(rights[2][0])
            rights[2].append(to_ctx(piece, 3))
        if step == 1 and square:
            rights[2][1:3] = chain(*rights[2][1:3])
    result = jnp.where(
        core_at == 0,
        jnp.concatenate(rows_own + rows_got, axis=1),
        jnp.concatenate(rows_got + rows_own, axis=1),
    )
    return result[None]


def solution(mesh):
    placed = (
        P(("ctx", "exp"), None),
        P(("ctx", "exp"), None),
        P(("ctx", "exp"), None),
        P(("ctx", "exp"), None),
        P(None, ("ctx", "exp")),
        P(("ctx", "exp")),
        P(("ctx", "exp")),
        P(("ctx", "exp"), None),
        P(("ctx", "exp"), None),
        P(("ctx", "exp"), None),
        P(("ctx", "exp"), None),
    )
    return jax.shard_map(
        on_device, mesh=mesh, in_specs=placed, out_specs=P("exp", "ctx", None), check_vma=False
    )
```

```python
import functools

import jax
import jax.numpy as jnp
from jax import lax
from jax.experimental import pallas as pl
from jax.experimental.pallas import tpu as pltpu
from jax.sharding import PartitionSpec as P

EXP_DEV = 1
GROUPS = ((1,), (1,), (1, 1), (1, 1), (1, 1))
NEAR_AFTER = {1: 3, 3: 4}
FAR_AFTER = {2: 3, 4: 4}
PRODUCT_AFTER = {3: 3, 5: 4}
UNITS = sum(map(sum, GROUPS))
DELAY = 3
SWAPS = (6, 8)
VMEM_BYTES = 60 * 1024 * 1024


def conv_kernel(tile, at_ctx, out_grad, gate_in, conv_in, scan_grad, taps, bias, skip, *refs):
    turned, flat, columns_of = refs[:-2], refs[-2], refs[-1]
    channels, length = out_grad.shape
    window = length // len(turned)
    kernel_taps = taps.shape[0]
    rows_at_once = 16
    settings = jnp.concatenate(
        [0.5 * taps[...], 0.5 * bias[...], skip[...], jnp.zeros((8 - kernel_taps - 2, channels), jnp.float32)], axis=0
    )
    columns_of[...] = settings.T

    def row_group(group, _):
        row_at = pl.multiple_of(group * rows_at_once, rows_at_once)
        rows = pl.ds(row_at, rows_at_once)

        def spread(index, width=tile):
            column = jnp.broadcast_to(columns_of[rows, index : index + 1], (rows_at_once, 128))
            return jnp.concatenate([column] * (width // 128), axis=1)

        weights = [spread(tap) for tap in range(kernel_taps)]
        wider = [spread(tap, tile + 128) for tap in (0, 1)]
        bias_half = spread(kernel_taps)
        skip_value = spread(kernel_taps + 1)
        after = jnp.zeros((rows_at_once, 128), jnp.float32)
        for at in range(length - tile, -1, -tile):
            columns = pl.ds(at, tile)
            gate = 0.5 * gate_in[rows, columns].astype(jnp.float32)
            gated = out_grad[rows, columns].astype(jnp.float32) * (gate + gate * jnp.tanh(gate))
            here = conv_in[rows, columns].astype(jnp.float32)
            if at:
                before = conv_in[rows, pl.ds(at - 128, 128)].astype(jnp.float32)
            else:
                before = jnp.zeros((rows_at_once, 128), jnp.float32)
            wide = jnp.concatenate([before, here], axis=1)
            one_back = pltpu.roll(wide, 1, 1)
            older = wider[1] * wide + wider[0] * one_back
            half = bias_half + weights[3] * here + weights[2] * one_back[:, 128:]
            half = half + pltpu.roll(older, 2, 1)[:, 128:]
            turn = jnp.tanh(half)
            scan = scan_grad[rows, columns].astype(jnp.float32)
            grad = (scan + skip_value * gated) * (1.0 + turn + half * (1.0 - turn * turn))
            wide_grad = jnp.concatenate([grad, after], axis=1)
            one_on = pltpu.roll(wide_grad, tile + 127, 1)
            later = wider[1] * wide_grad + wider[0] * one_on
            total = weights[3] * grad + weights[2] * one_on[:, :tile]
            total = total + pltpu.roll(later, tile + 126, 1)[:, :tile]
            flat[rows, columns] = total.astype(flat.dtype)
            after = grad[:, :128]
        return 0

    lax.fori_loop(0, channels // rows_at_once, row_group, 0)
    for offset, out in enumerate(turned):
        from_at = (at_ctx[0] ^ offset) * window
        for at in range(0, window, tile):
            out[pl.ds(at, tile), :] = flat[:, pl.ds(pl.multiple_of(from_at + at, tile), tile)].T


def conv_grad(at_ctx, ctx_count, out_grad, gate_in, conv_in, scan_grad, conv_weight, conv_bias, skip_scale):
    channels, length = out_grad.shape
    block = min(128, channels)
    window = length // ctx_count
    tile = min(512, window)
    whole = pl.BlockSpec((block, length), lambda step, at_ctx: (step, 0))
    row = pl.BlockSpec((1, block), lambda step, at_ctx: (0, step))
    return pl.pallas_call(
        functools.partial(conv_kernel, tile),
        grid_spec=pltpu.PrefetchScalarGridSpec(
            num_scalar_prefetch=1,
            grid=(channels // block,),
            in_specs=[whole] * 4
            + [pl.BlockSpec((conv_weight.shape[0], block), lambda step, at_ctx: (0, step)), row, row],
            out_specs=[pl.BlockSpec((window, block), lambda step, at_ctx: (0, step))] * ctx_count,
            scratch_shapes=[pltpu.VMEM((block, length), jnp.bfloat16), pltpu.VMEM((block, 8), jnp.float32)],
        ),
        out_shape=[jax.ShapeDtypeStruct((window, channels), jnp.bfloat16)] * ctx_count,
        compiler_params=pltpu.CompilerParams(vmem_limit_bytes=VMEM_BYTES),
        cost_estimate=pl.CostEstimate(
            flops=40 * channels * length, bytes_accessed=10 * channels * length, transcendentals=2 * channels * length
        ),
        name="conv_grad",
    )(at_ctx, out_grad, gate_in, conv_in, scan_grad, conv_weight, conv_bias[None], skip_scale[None])


def matmul_kernel(lefts, rights, place, *refs):
    left_refs = refs[:lefts]
    right_refs = refs[lefts : lefts + rights]
    resid = refs[lefts + rights]
    outs = refs[lefts + rights + 1 :]
    left = jnp.concatenate([ref[...] for ref in left_refs], axis=1)
    right = jnp.concatenate([ref[...] for ref in right_refs], axis=0)
    total = jnp.dot(left, right, preferred_element_type=jnp.float32)
    many = left.shape[0] // resid.shape[0]
    parts = []
    for part in range(many):
        mine = pl.program_id(0) * many + part == place[0]
        rows = total[part * resid.shape[0] : (part + 1) * resid.shape[0]]
        parts.append(rows + jnp.where(mine, resid[...].astype(jnp.float32), 0.0))
    total = jnp.concatenate(parts, axis=0)
    at = 0
    for out in outs:
        out[...] = total[:, at : at + out.shape[1]].astype(out.dtype)
        at += out.shape[1]


def matmul(lefts, rights, resid, place, widths):
    tokens, depth = lefts[0].shape
    width = rights[0].shape[1]
    tile = 2 * resid.shape[0]
    flops = 2 * tokens * depth * len(lefts) * width
    moved = 2 * (tokens * depth * len(lefts) + depth * len(lefts) * width + tokens * width)
    return pl.pallas_call(
        functools.partial(matmul_kernel, len(lefts), len(rights)),
        grid_spec=pltpu.PrefetchScalarGridSpec(
            num_scalar_prefetch=1,
            grid=(tokens // tile,),
            in_specs=[pl.BlockSpec((tile, depth), lambda step, place: (step, 0))] * len(lefts)
            + [pl.BlockSpec(right.shape, lambda step, place: (0, 0)) for right in rights]
            + [pl.BlockSpec(resid.shape, lambda step, place: (0, 0))],
            out_specs=[pl.BlockSpec((tile, part), lambda step, place: (step, 0)) for part in widths],
        ),
        out_shape=[jax.ShapeDtypeStruct((tokens, part), jnp.bfloat16) for part in widths],
        compiler_params=pltpu.CompilerParams(vmem_limit_bytes=VMEM_BYTES),
        cost_estimate=pl.CostEstimate(flops=flops, bytes_accessed=moved, transcendentals=0),
        name="partial_product",
    )(place, *lefts, *rights, resid)


def on_device(
    out_grad,
    gate_in,
    conv_in,
    scan_grad,
    conv_weight,
    conv_bias,
    skip_scale,
    projection,
    resid_grad,
    routes,
    gate_probs,
):
    ctx_count = lax.axis_size("ctx")
    exp_count = lax.axis_size("exp")
    chips = exp_count // 2
    ctx_at = lax.axis_index("ctx")
    exp_at = lax.axis_index("exp")
    chip_at = exp_at // 2
    core_at = exp_at % 2
    channels, length = out_grad.shape
    features = projection.shape[1]
    half = features // 2
    unit = half // UNITS
    widths = [[unit * part for part in group] for group in GROUPS]
    starts = [sum(map(sum, widths[:at])) for at in range(len(widths))]
    tok_rows = resid_grad.shape[0]
    window = tok_rows * exp_count
    tile = 2 * tok_rows

    def to_core(array):
        return lax.ppermute(array, "exp", [(place, place ^ 1) for place in range(exp_count)])

    def to_ctx(array, offset):
        return lax.ppermute(array, "ctx", [(place, place ^ offset) for place in range(ctx_count)])

    def swap_chips(array, low, inward=True, outward=True):
        pairs = set()
        for core in (0, 1):
            for near, far in ((low, low + 1), (chips - 1 - low, chips - 2 - low)):
                if inward:
                    pairs.add((2 * near + core, 2 * far + core))
                if outward:
                    pairs.add((2 * far + core, 2 * near + core))
        return lax.ppermute(array, "exp", sorted(pairs))

    def columns_of(array, core, at, width):
        return lax.dynamic_slice_in_dim(array, core * half + at, width, 1)

    def both_cores(array, at, width):
        here = columns_of(array, core_at, at, width)
        return here, to_core(columns_of(array, 1 - core_at, at, width))

    def spread_near(piece):
        return [piece, to_ctx(piece, 1), to_ctx(piece, 2)]

    def spread_far(near):
        near = list(chain(*near))
        return near + [to_ctx(near[0], 3)]

    def spread(piece):
        return [piece] + [to_ctx(piece, offset) for offset in range(1, ctx_count)]

    first = sum(widths[0])
    rights = [spread(jnp.concatenate(both_cores(projection, 0, first), axis=0))]

    turned = conv_grad(
        ctx_at.astype(jnp.int32).reshape(1),
        ctx_count,
        out_grad,
        gate_in,
        conv_in,
        scan_grad,
        conv_weight,
        conv_bias,
        skip_scale,
    )
    turned, rights[0] = lax.optimization_barrier((turned, rights[0]))
    lefts = [turned[0], to_core(turned[0])]
    received = [to_ctx(turned[offset], offset) for offset in range(1, ctx_count)]
    lefts[1], projection, resid_grad, routes = lax.optimization_barrier((lefts[1], projection, resid_grad, routes))

    routed = jnp.concatenate([routes.T.astype(jnp.float32), gate_probs.T], axis=0)[None]
    offset = 1
    while offset < exp_count:
        other = lax.ppermute(routed, "exp", [(place, place ^ offset) for place in range(exp_count)])
        routed = jnp.concatenate([routed, other], axis=0)
        offset *= 2
    order = (jnp.arange(exp_count)[:, None] ^ exp_at) == jnp.arange(exp_count)[None, :]
    routed = jnp.sum(jnp.where(order[:, :, None, None], routed[None], 0.0), axis=1)

    rest_here, rest_there = both_cores(projection, first, half - first)
    rest = []
    for group, at in list(zip(widths, starts))[1:]:
        cut = slice(at - first, at - first + sum(group))
        rest.append(jnp.concatenate([rest_here[:, cut], rest_there[:, cut]], axis=0))
    resid_here, resid_there = both_cores(resid_grad, 0, half)
    resid = jnp.where(
        core_at == 0,
        jnp.concatenate([resid_here, resid_there], axis=0),
        jnp.concatenate([resid_there, resid_here], axis=0),
    )

    route_width = routes.shape[1]
    all_routes = routed[:, :route_width]
    all_probs = routed[:, route_width:]
    capacity = max(2, 14 * tok_rows // (4 * EXP_DEV * exp_count))
    experts = jnp.stack([exp_at, exp_at ^ 1]).astype(jnp.float32)
    named = all_routes[None] == experts[:, None, None, None]
    hit = jnp.any(named, axis=2)
    prob = jnp.sum(jnp.where(named, all_probs[None], 0.0), axis=2)
    count = hit.astype(jnp.int32)
    rank = jnp.cumsum(count, axis=2) - count
    slot = jnp.where(hit, rank + (jnp.arange(exp_count, dtype=jnp.int32) % 2)[None, :, None] * capacity, -1)
    slot = slot.reshape(2, chips, 1, tile)
    picks = slot == jnp.arange(2 * capacity, dtype=jnp.int32)[None, None, :, None]
    scale = jnp.sum(jnp.where(picks, prob.reshape(2, chips, 1, tile), 0.0), axis=3, keepdims=True)
    picks = picks.astype(jnp.bfloat16)

    rights.append(spread(rest[0]))
    received, rest, rights[1], resid, picks, scale = lax.optimization_barrier(
        (received, rest, rights[1], resid, picks, scale)
    )
    for piece in received:
        lefts += [piece, to_core(piece)]

    if channels < 128:
        lefts = [jnp.concatenate(lefts, axis=1)]
    place = chip_at.astype(jnp.int32).reshape(1)
    pieces = sum(map(len, GROUPS))
    token = [place]

    def chain(*arrays):
        *arrays, token[0] = lax.optimization_barrier((*arrays, token[0]))
        token[0] = arrays[0]
        return arrays

    def products(group_at, right):
        group, at = widths[group_at], starts[group_at]
        if channels < 128:
            right = [jnp.concatenate(right, axis=0)]
        right = chain(*right)
        found = matmul(lefts, right, resid[:, at : at + sum(group)], place, group)
        token[0] = found[0]
        return found

    middle = chips // 2
    distance = jnp.minimum(chip_at, chips - 1 - chip_at)
    rows_own, rows_got, waiting = [], [], []

    def add(one, other):
        return (one.astype(jnp.float32) + other.astype(jnp.float32)).astype(jnp.bfloat16)

    def finish(grads):
        width = grads.shape[1]
        rows = jnp.einsum("eist,itf->eisf", picks, grads.reshape(chips, tile, width), preferred_element_type=jnp.float32)
        rows = (rows * scale).astype(jnp.bfloat16).reshape(2, chips * 2 * capacity, width)
        rows_own.append(rows[0])
        waiting.append(rows[1])
        if len(rows_own) in SWAPS:
            rows_got.append(to_core(jnp.concatenate(waiting, axis=1)))
            waiting.clear()

    square = ctx_count == 4
    hops = middle - 1
    lag = DELAY - 1
    sums = [[None] * pieces for _ in range(hops + 1)]
    ready = [[None] * pieces for _ in range(hops + 1)]
    outer, across = {}, {}
    first_of = [sum(map(len, GROUPS[:at])) for at in range(len(GROUPS))]
    lefts, rest[1] = lax.optimization_barrier((lefts, rest[1]))
    rights.append(spread_near(rest[1]) if square else spread(rest[1]))
    sums[0][: len(GROUPS[0])] = products(0, rights[0])
    rights += [None] * (len(GROUPS) - len(rights))
    for step in range(pieces + 2 * lag * hops + DELAY + 1):
        for hop in range(hops):
            if (step - 2, hop) not in outer:
                continue
            got, inward, outward = outer[step - 2, hop]
            if inward is not None:
                own, got = chain(sums[hop][inward], got)
                sums[hop + 1][inward] = token[0] = add(own, got)
                if hop == hops - 1:
                    across[step] = (swap_chips(token[0], middle - 1), inward)
            if outward is not None:
                ready[hop][outward] = jnp.where(distance == hop, got, ready[hop + 1][outward])
                if hop == 0:
                    finish(ready[0][outward])
        if step - 1 in across:
            got, index = across[step - 1]
            own, got = chain(sums[hops][index], got)
            ready[hops][index] = add(own, got)
        group_at = first_of.index(step) if step and step in first_of else None
        if group_at and group_at not in PRODUCT_AFTER.values():
            sums[0][step : step + len(GROUPS[group_at])] = products(group_at, rights[group_at])
        for hop in range(hops):
            inward = step - lag * hop
            outward = inward - DELAY - 2 * lag * (hops - 1 - hop)
            inward = inward if 0 <= inward < pieces else None
            outward = outward if 0 <= outward < pieces else None
            if inward is not None and outward is not None:
                payload = jnp.where(distance == hop, sums[hop][inward], ready[hop + 1][outward])
            elif inward is not None:
                payload = sums[hop][inward]
            elif outward is not None:
                payload = ready[hop + 1][outward]
            else:
                continue
            (payload,) = chain(payload)
            outer[step, hop] = (swap_chips(payload, hop, inward is not None, outward is not None), inward, outward)
        if step == 0 and square:
            (piece,) = chain(rights[2][0])
            rights[2].append(to_ctx(piece, 3))
        if step == 1 and square:
            rights[2][1:3] = chain(*rights[2][1:3])
        group_at = PRODUCT_AFTER.get(step)
        if step in NEAR_AFTER:
            coming = NEAR_AFTER[step]
            piece, *arrived = chain(rest[coming - 1], *(rights[group_at] if group_at else []))
            rights[coming] = spread_near(piece) if square else spread(piece)
            if group_at:
                rights[group_at] = arrived
        if step in FAR_AFTER and square:
            rights[FAR_AFTER[step]] = spread_far(rights[FAR_AFTER[step]])
        if group_at:
            first_piece = first_of[group_at]
            sums[0][first_piece : first_piece + len(GROUPS[group_at])] = products(group_at, rights[group_at])
    result = jnp.where(
        core_at == 0,
        jnp.concatenate(rows_own + rows_got, axis=1),
        jnp.concatenate(rows_got + rows_own, axis=1),
    )
    return result[None]


def solution(mesh):
    placed = (
        P(("ctx", "exp"), None),
        P(("ctx", "exp"), None),
        P(("ctx", "exp"), None),
        P(("ctx", "exp"), None),
        P(None, ("ctx", "exp")),
        P(("ctx", "exp")),
        P(("ctx", "exp")),
        P(("ctx", "exp"), None),
        P(("ctx", "exp"), None),
        P(("ctx", "exp"), None),
        P(("ctx", "exp"), None),
    )
    return jax.shard_map(
        on_device, mesh=mesh, in_specs=placed, out_specs=P("exp", "ctx", None), check_vma=False
    )
```

```python
import functools

import jax
import jax.numpy as jnp
from jax import lax
from jax.experimental import pallas as pl
from jax.experimental.pallas import tpu as pltpu
from jax.sharding import PartitionSpec as P

EXP_DEV = 1
GROUPS = ((1,), (1,), (1, 1), (1, 1), (1, 1))
FIRST_PHASE = {2: 3, 4: 4}
SECOND_PHASE = {3: 3, 5: 4}
UNITS = sum(map(sum, GROUPS))
DELAY = 3
SWAPS = (6, 8)
VMEM_BYTES = 60 * 1024 * 1024


def conv_kernel(tile, at_ctx, out_grad, gate_in, conv_in, scan_grad, taps, bias, skip, *refs):
    turned, flat, columns_of = refs[:-2], refs[-2], refs[-1]
    channels, length = out_grad.shape
    window = length // len(turned)
    kernel_taps = taps.shape[0]
    rows_at_once = 16
    settings = jnp.concatenate(
        [0.5 * taps[...], 0.5 * bias[...], skip[...], jnp.zeros((8 - kernel_taps - 2, channels), jnp.float32)], axis=0
    )
    columns_of[...] = settings.T

    def row_group(group, _):
        row_at = pl.multiple_of(group * rows_at_once, rows_at_once)
        rows = pl.ds(row_at, rows_at_once)

        def spread(index, width=tile):
            column = jnp.broadcast_to(columns_of[rows, index : index + 1], (rows_at_once, 128))
            return jnp.concatenate([column] * (width // 128), axis=1)

        weights = [spread(tap) for tap in range(kernel_taps)]
        wider = [spread(tap, tile + 128) for tap in (0, 1)]
        bias_half = spread(kernel_taps)
        skip_value = spread(kernel_taps + 1)
        after = jnp.zeros((rows_at_once, 128), jnp.float32)
        for at in range(length - tile, -1, -tile):
            columns = pl.ds(at, tile)
            gate = 0.5 * gate_in[rows, columns].astype(jnp.float32)
            gated = out_grad[rows, columns].astype(jnp.float32) * (gate + gate * jnp.tanh(gate))
            here = conv_in[rows, columns].astype(jnp.float32)
            if at:
                before = conv_in[rows, pl.ds(at - 128, 128)].astype(jnp.float32)
            else:
                before = jnp.zeros((rows_at_once, 128), jnp.float32)
            wide = jnp.concatenate([before, here], axis=1)
            one_back = pltpu.roll(wide, 1, 1)
            older = wider[1] * wide + wider[0] * one_back
            half = bias_half + weights[3] * here + weights[2] * one_back[:, 128:]
            half = half + pltpu.roll(older, 2, 1)[:, 128:]
            turn = jnp.tanh(half)
            scan = scan_grad[rows, columns].astype(jnp.float32)
            grad = (scan + skip_value * gated) * (1.0 + turn + half * (1.0 - turn * turn))
            wide_grad = jnp.concatenate([grad, after], axis=1)
            one_on = pltpu.roll(wide_grad, tile + 127, 1)
            later = wider[1] * wide_grad + wider[0] * one_on
            total = weights[3] * grad + weights[2] * one_on[:, :tile]
            total = total + pltpu.roll(later, tile + 126, 1)[:, :tile]
            flat[rows, columns] = total.astype(flat.dtype)
            after = grad[:, :128]
        return 0

    lax.fori_loop(0, channels // rows_at_once, row_group, 0)
    for offset, out in enumerate(turned):
        from_at = (at_ctx[0] ^ offset) * window
        for at in range(0, window, tile):
            out[pl.ds(at, tile), :] = flat[:, pl.ds(pl.multiple_of(from_at + at, tile), tile)].T


def conv_grad(at_ctx, ctx_count, out_grad, gate_in, conv_in, scan_grad, conv_weight, conv_bias, skip_scale):
    channels, length = out_grad.shape
    block = min(128, channels)
    window = length // ctx_count
    tile = min(512, window)
    whole = pl.BlockSpec((block, length), lambda step, at_ctx: (step, 0))
    row = pl.BlockSpec((1, block), lambda step, at_ctx: (0, step))
    return pl.pallas_call(
        functools.partial(conv_kernel, tile),
        grid_spec=pltpu.PrefetchScalarGridSpec(
            num_scalar_prefetch=1,
            grid=(channels // block,),
            in_specs=[whole] * 4
            + [pl.BlockSpec((conv_weight.shape[0], block), lambda step, at_ctx: (0, step)), row, row],
            out_specs=[pl.BlockSpec((window, block), lambda step, at_ctx: (0, step))] * ctx_count,
            scratch_shapes=[pltpu.VMEM((block, length), jnp.bfloat16), pltpu.VMEM((block, 8), jnp.float32)],
        ),
        out_shape=[jax.ShapeDtypeStruct((window, channels), jnp.bfloat16)] * ctx_count,
        compiler_params=pltpu.CompilerParams(vmem_limit_bytes=VMEM_BYTES),
        cost_estimate=pl.CostEstimate(
            flops=40 * channels * length, bytes_accessed=10 * channels * length, transcendentals=2 * channels * length
        ),
        name="conv_grad",
    )(at_ctx, out_grad, gate_in, conv_in, scan_grad, conv_weight, conv_bias[None], skip_scale[None])


def matmul_kernel(lefts, rights, place, *refs):
    left_refs = refs[:lefts]
    right_refs = refs[lefts : lefts + rights]
    resid = refs[lefts + rights]
    outs = refs[lefts + rights + 1 :]
    left = jnp.concatenate([ref[...] for ref in left_refs], axis=1)
    right = jnp.concatenate([ref[...] for ref in right_refs], axis=0)
    total = jnp.dot(left, right, preferred_element_type=jnp.float32)
    many = left.shape[0] // resid.shape[0]
    parts = []
    for part in range(many):
        mine = pl.program_id(0) * many + part == place[0]
        rows = total[part * resid.shape[0] : (part + 1) * resid.shape[0]]
        parts.append(rows + jnp.where(mine, resid[...].astype(jnp.float32), 0.0))
    total = jnp.concatenate(parts, axis=0)
    at = 0
    for out in outs:
        out[...] = total[:, at : at + out.shape[1]].astype(out.dtype)
        at += out.shape[1]


def matmul(lefts, rights, resid, place, widths, only=None):
    tokens, depth = lefts[0].shape
    block = 0
    width = rights[0].shape[1]
    if only is not None:
        block, width = only, widths[only]
        widths = (width,)
    tile = 2 * resid.shape[0]
    flops = 2 * tokens * depth * len(lefts) * width
    moved = 2 * (tokens * depth * len(lefts) + depth * len(lefts) * width + tokens * width)
    return pl.pallas_call(
        functools.partial(matmul_kernel, len(lefts), len(rights)),
        grid_spec=pltpu.PrefetchScalarGridSpec(
            num_scalar_prefetch=1,
            grid=(tokens // tile,),
            in_specs=[pl.BlockSpec((tile, depth), lambda step, place: (step, 0))] * len(lefts)
            + [pl.BlockSpec((right.shape[0], width), lambda step, place: (0, block)) for right in rights]
            + [pl.BlockSpec((resid.shape[0], width), lambda step, place: (0, block))],
            out_specs=[pl.BlockSpec((tile, part), lambda step, place: (step, 0)) for part in widths],
        ),
        out_shape=[jax.ShapeDtypeStruct((tokens, part), jnp.bfloat16) for part in widths],
        compiler_params=pltpu.CompilerParams(vmem_limit_bytes=VMEM_BYTES),
        cost_estimate=pl.CostEstimate(flops=flops, bytes_accessed=moved, transcendentals=0),
        name="partial_product",
    )(place, *lefts, *rights, resid)


def on_device(
    out_grad,
    gate_in,
    conv_in,
    scan_grad,
    conv_weight,
    conv_bias,
    skip_scale,
    projection,
    resid_grad,
    routes,
    gate_probs,
):
    ctx_count = lax.axis_size("ctx")
    exp_count = lax.axis_size("exp")
    chips = exp_count // 2
    ctx_at = lax.axis_index("ctx")
    exp_at = lax.axis_index("exp")
    chip_at = exp_at // 2
    core_at = exp_at % 2
    channels, length = out_grad.shape
    features = projection.shape[1]
    half = features // 2
    unit = half // UNITS
    widths = [[unit * part for part in group] for group in GROUPS]
    starts = [sum(map(sum, widths[:at])) for at in range(len(widths))]
    tok_rows = resid_grad.shape[0]
    window = tok_rows * exp_count
    tile = 2 * tok_rows

    def to_core(array):
        return lax.ppermute(array, "exp", [(place, place ^ 1) for place in range(exp_count)])

    def to_ctx(array, offset):
        return lax.ppermute(array, "ctx", [(place, place ^ offset) for place in range(ctx_count)])

    def swap_chips(array, low, inward=True, outward=True):
        pairs = set()
        for core in (0, 1):
            for near, far in ((low, low + 1), (chips - 1 - low, chips - 2 - low)):
                if inward:
                    pairs.add((2 * near + core, 2 * far + core))
                if outward:
                    pairs.add((2 * far + core, 2 * near + core))
        return lax.ppermute(array, "exp", sorted(pairs))

    def columns_of(array, core, at, width):
        return lax.dynamic_slice_in_dim(array, core * half + at, width, 1)

    def both_cores(array, at, width):
        here = columns_of(array, core_at, at, width)
        return here, to_core(columns_of(array, 1 - core_at, at, width))

    def spread_near(piece):
        return [piece, to_ctx(piece, 1), to_ctx(piece, 2)]

    def spread_far(near):
        near = list(chain(*near))
        return near + [to_ctx(near[0], 3)]

    def spread(piece):
        return [piece] + [to_ctx(piece, offset) for offset in range(1, ctx_count)]

    first = sum(widths[0])
    rights = [spread(jnp.concatenate(both_cores(projection, 0, first), axis=0))]

    turned = conv_grad(
        ctx_at.astype(jnp.int32).reshape(1),
        ctx_count,
        out_grad,
        gate_in,
        conv_in,
        scan_grad,
        conv_weight,
        conv_bias,
        skip_scale,
    )
    turned, rights[0] = lax.optimization_barrier((turned, rights[0]))
    lefts = [turned[0], to_core(turned[0])]
    received = [to_ctx(turned[offset], offset) for offset in range(1, ctx_count)]
    lefts[1], projection, resid_grad, routes = lax.optimization_barrier((lefts[1], projection, resid_grad, routes))

    routed = jnp.concatenate([routes.T.astype(jnp.float32), gate_probs.T], axis=0)[None]
    offset = 1
    while offset < exp_count:
        other = lax.ppermute(routed, "exp", [(place, place ^ offset) for place in range(exp_count)])
        routed = jnp.concatenate([routed, other], axis=0)
        offset *= 2
    order = (jnp.arange(exp_count)[:, None] ^ exp_at) == jnp.arange(exp_count)[None, :]
    routed = jnp.sum(jnp.where(order[:, :, None, None], routed[None], 0.0), axis=1)

    rest_here, rest_there = both_cores(projection, first, half - first)
    rest = []
    for group, at in list(zip(widths, starts))[1:]:
        cut = slice(at - first, at - first + sum(group))
        rest.append(jnp.concatenate([rest_here[:, cut], rest_there[:, cut]], axis=0))
    resid_here, resid_there = both_cores(resid_grad, 0, half)
    resid = jnp.where(
        core_at == 0,
        jnp.concatenate([resid_here, resid_there], axis=0),
        jnp.concatenate([resid_there, resid_here], axis=0),
    )

    route_width = routes.shape[1]
    all_routes = routed[:, :route_width]
    all_probs = routed[:, route_width:]
    capacity = max(2, 14 * tok_rows // (4 * EXP_DEV * exp_count))
    experts = jnp.stack([exp_at, exp_at ^ 1]).astype(jnp.float32)
    named = all_routes[None] == experts[:, None, None, None]
    hit = jnp.any(named, axis=2)
    prob = jnp.sum(jnp.where(named, all_probs[None], 0.0), axis=2)
    count = hit.astype(jnp.int32)
    rank = jnp.cumsum(count, axis=2) - count
    slot = jnp.where(hit, rank + (jnp.arange(exp_count, dtype=jnp.int32) % 2)[None, :, None] * capacity, -1)
    slot = slot.reshape(2, chips, 1, tile)
    picks = slot == jnp.arange(2 * capacity, dtype=jnp.int32)[None, None, :, None]
    scale = jnp.sum(jnp.where(picks, prob.reshape(2, chips, 1, tile), 0.0), axis=3, keepdims=True)
    picks = picks.astype(jnp.bfloat16)

    rights.append(spread(rest[0]))
    received, rest, rights[1], resid, picks, scale = lax.optimization_barrier(
        (received, rest, rights[1], resid, picks, scale)
    )
    for piece in received:
        lefts += [piece, to_core(piece)]

    if channels < 128:
        lefts = [jnp.concatenate(lefts, axis=1)]
    place = chip_at.astype(jnp.int32).reshape(1)
    pieces = sum(map(len, GROUPS))
    token = [place]

    def chain(*arrays):
        *arrays, token[0] = lax.optimization_barrier((*arrays, token[0]))
        token[0] = arrays[0]
        return arrays

    def products(group_at, right, only=None):
        group, at = widths[group_at], starts[group_at]
        if channels < 128:
            right = [jnp.concatenate(right, axis=0)]
        right = chain(*right)
        found = matmul(lefts, right, resid[:, at : at + sum(group)], place, group, only)
        token[0] = found[0]
        return found if only is None else found[0]

    middle = chips // 2
    distance = jnp.minimum(chip_at, chips - 1 - chip_at)
    rows_own, rows_got, waiting = [], [], []

    def add(one, other):
        return (one.astype(jnp.float32) + other.astype(jnp.float32)).astype(jnp.bfloat16)

    def finish(grads):
        width = grads.shape[1]
        rows = jnp.einsum("eist,itf->eisf", picks, grads.reshape(chips, tile, width), preferred_element_type=jnp.float32)
        rows = (rows * scale).astype(jnp.bfloat16).reshape(2, chips * 2 * capacity, width)
        rows_own.append(rows[0])
        waiting.append(rows[1])
        if len(rows_own) in SWAPS:
            rows_got.append(to_core(jnp.concatenate(waiting, axis=1)))
            waiting.clear()

    square = ctx_count == 4
    hops = middle - 1
    lag = DELAY - 1
    sums = [[None] * pieces for _ in range(hops + 1)]
    ready = [[None] * pieces for _ in range(hops + 1)]
    outer, across = {}, {}
    first_of = [sum(map(len, GROUPS[:at])) for at in range(len(GROUPS))]
    lefts, rest[1] = lax.optimization_barrier((lefts, rest[1]))
    rights.append(spread_near(rest[1]) if square else spread(rest[1]))
    sums[0][0] = products(0, rights[0], 0)
    rights += [None] * (len(GROUPS) - len(rights))
    for step in range(pieces + 2 * lag * hops + DELAY + 1):
        for hop in range(hops):
            if (step - 2, hop) not in outer:
                continue
            got, inward, outward = outer[step - 2, hop]
            if inward is not None:
                own, got = chain(sums[hop][inward], got)
                sums[hop + 1][inward] = token[0] = add(own, got)
                if hop == hops - 1:
                    across[step] = (swap_chips(token[0], middle - 1), inward)
            if outward is not None:
                ready[hop][outward] = jnp.where(distance == hop, got, ready[hop + 1][outward])
                if hop == 0:
                    finish(ready[0][outward])
        if step - 1 in across:
            got, index = across[step - 1]
            own, got = chain(sums[hops][index], got)
            ready[hops][index] = add(own, got)
        if step in SECOND_PHASE and square:
            rights[SECOND_PHASE[step]] = spread_far(rights[SECOND_PHASE[step]])
        group_at = first_of.index(step) if step and step in first_of else None
        if step in FIRST_PHASE:
            coming = FIRST_PHASE[step]
            piece, *rights[group_at] = chain(rest[coming - 1], *rights[group_at])
            rights[coming] = spread_near(piece) if square else spread(piece)
        if 0 < step < pieces:
            group_at = max(at for at, begin in enumerate(first_of) if begin <= step)
            sums[0][step] = products(group_at, rights[group_at], step - first_of[group_at])
        for hop in range(hops):
            inward = step - lag * hop
            outward = inward - DELAY - 2 * lag * (hops - 1 - hop)
            inward = inward if 0 <= inward < pieces else None
            outward = outward if 0 <= outward < pieces else None
            if inward is not None and outward is not None:
                payload = jnp.where(distance == hop, sums[hop][inward], ready[hop + 1][outward])
            elif inward is not None:
                payload = sums[hop][inward]
            elif outward is not None:
                payload = ready[hop + 1][outward]
            else:
                continue
            (payload,) = chain(payload)
            outer[step, hop] = (swap_chips(payload, hop, inward is not None, outward is not None), inward, outward)
        if step == 0 and square:
            (piece,) = chain(rights[2][0])
            rights[2].append(to_ctx(piece, 3))
        if step == 1 and square:
            rights[2][1:3] = chain(*rights[2][1:3])
    result = jnp.where(
        core_at == 0,
        jnp.concatenate(rows_own + rows_got, axis=1),
        jnp.concatenate(rows_got + rows_own, axis=1),
    )
    return result[None]


def solution(mesh):
    placed = (
        P(("ctx", "exp"), None),
        P(("ctx", "exp"), None),
        P(("ctx", "exp"), None),
        P(("ctx", "exp"), None),
        P(None, ("ctx", "exp")),
        P(("ctx", "exp")),
        P(("ctx", "exp")),
        P(("ctx", "exp"), None),
        P(("ctx", "exp"), None),
        P(("ctx", "exp"), None),
        P(("ctx", "exp"), None),
    )
    return jax.shard_map(
        on_device, mesh=mesh, in_specs=placed, out_specs=P("exp", "ctx", None), check_vma=False
    )
```

```python
import functools

import jax
import jax.numpy as jnp
from jax import lax
from jax.experimental import pallas as pl
from jax.experimental.pallas import tpu as pltpu
from jax.sharding import PartitionSpec as P

EXP_DEV = 1
GROUPS = ((1,), (1,), (1, 1), (1, 1), (1, 1))
FIRST_PHASE = {2: 3, 4: 4}
SECOND_PHASE = {3: 3, 5: 4}
UNITS = sum(map(sum, GROUPS))
DELAY = 3
SWAPS = (6, 8)
VMEM_BYTES = 60 * 1024 * 1024


def conv_kernel(tile, at_ctx, out_grad, gate_in, conv_in, scan_grad, taps, bias, skip, *refs):
    turned, flat, columns_of = refs[:-2], refs[-2], refs[-1]
    channels, length = out_grad.shape
    window = length // len(turned)
    kernel_taps = taps.shape[0]
    rows_at_once = 16
    settings = jnp.concatenate(
        [0.5 * taps[...], 0.5 * bias[...], skip[...], jnp.zeros((8 - kernel_taps - 2, channels), jnp.float32)], axis=0
    )
    columns_of[...] = settings.T

    def row_group(group, _):
        row_at = pl.multiple_of(group * rows_at_once, rows_at_once)
        rows = pl.ds(row_at, rows_at_once)

        def spread(index, width=tile):
            column = jnp.broadcast_to(columns_of[rows, index : index + 1], (rows_at_once, 128))
            return jnp.concatenate([column] * (width // 128), axis=1)

        weights = [spread(tap) for tap in range(kernel_taps)]
        wider = [spread(tap, tile + 128) for tap in (0, 1)]
        bias_half = spread(kernel_taps)
        skip_value = spread(kernel_taps + 1)
        after = jnp.zeros((rows_at_once, 128), jnp.float32)
        for at in range(length - tile, -1, -tile):
            columns = pl.ds(at, tile)
            gate = 0.5 * gate_in[rows, columns].astype(jnp.float32)
            gated = out_grad[rows, columns].astype(jnp.float32) * (gate + gate * jnp.tanh(gate))
            here = conv_in[rows, columns].astype(jnp.float32)
            if at:
                before = conv_in[rows, pl.ds(at - 128, 128)].astype(jnp.float32)
            else:
                before = jnp.zeros((rows_at_once, 128), jnp.float32)
            wide = jnp.concatenate([before, here], axis=1)
            one_back = pltpu.roll(wide, 1, 1)
            older = wider[1] * wide + wider[0] * one_back
            half = bias_half + weights[3] * here + weights[2] * one_back[:, 128:]
            half = half + pltpu.roll(older, 2, 1)[:, 128:]
            turn = jnp.tanh(half)
            scan = scan_grad[rows, columns].astype(jnp.float32)
            grad = (scan + skip_value * gated) * (1.0 + turn + half * (1.0 - turn * turn))
            wide_grad = jnp.concatenate([grad, after], axis=1)
            one_on = pltpu.roll(wide_grad, tile + 127, 1)
            later = wider[1] * wide_grad + wider[0] * one_on
            total = weights[3] * grad + weights[2] * one_on[:, :tile]
            total = total + pltpu.roll(later, tile + 126, 1)[:, :tile]
            flat[rows, columns] = total.astype(flat.dtype)
            after = grad[:, :128]
        return 0

    lax.fori_loop(0, channels // rows_at_once, row_group, 0)
    for offset, out in enumerate(turned):
        from_at = (at_ctx[0] ^ offset) * window
        for at in range(0, window, tile):
            out[pl.ds(at, tile), :] = flat[:, pl.ds(pl.multiple_of(from_at + at, tile), tile)].T


def conv_grad(at_ctx, ctx_count, out_grad, gate_in, conv_in, scan_grad, conv_weight, conv_bias, skip_scale):
    channels, length = out_grad.shape
    block = min(128, channels)
    window = length // ctx_count
    tile = min(512, window)
    whole = pl.BlockSpec((block, length), lambda step, at_ctx: (step, 0))
    row = pl.BlockSpec((1, block), lambda step, at_ctx: (0, step))
    return pl.pallas_call(
        functools.partial(conv_kernel, tile),
        grid_spec=pltpu.PrefetchScalarGridSpec(
            num_scalar_prefetch=1,
            grid=(channels // block,),
            in_specs=[whole] * 4
            + [pl.BlockSpec((conv_weight.shape[0], block), lambda step, at_ctx: (0, step)), row, row],
            out_specs=[pl.BlockSpec((window, block), lambda step, at_ctx: (0, step))] * ctx_count,
            scratch_shapes=[pltpu.VMEM((block, length), jnp.bfloat16), pltpu.VMEM((block, 8), jnp.float32)],
        ),
        out_shape=[jax.ShapeDtypeStruct((window, channels), jnp.bfloat16)] * ctx_count,
        compiler_params=pltpu.CompilerParams(vmem_limit_bytes=VMEM_BYTES),
        cost_estimate=pl.CostEstimate(
            flops=40 * channels * length, bytes_accessed=10 * channels * length, transcendentals=2 * channels * length
        ),
        name="conv_grad",
    )(at_ctx, out_grad, gate_in, conv_in, scan_grad, conv_weight, conv_bias[None], skip_scale[None])


def matmul_kernel(lefts, rights, place, *refs):
    left_refs = refs[:lefts]
    right_refs = refs[lefts : lefts + rights]
    resid = refs[lefts + rights]
    outs = refs[lefts + rights + 1 :]
    left = jnp.concatenate([ref[...] for ref in left_refs], axis=1)
    right = jnp.concatenate([ref[...] for ref in right_refs], axis=0)
    total = jnp.dot(left, right, preferred_element_type=jnp.float32)
    many = left.shape[0] // resid.shape[0]
    parts = []
    for part in range(many):
        mine = pl.program_id(0) * many + part == place[0]
        rows = total[part * resid.shape[0] : (part + 1) * resid.shape[0]]
        parts.append(rows + jnp.where(mine, resid[...].astype(jnp.float32), 0.0))
    total = jnp.concatenate(parts, axis=0)
    at = 0
    for out in outs:
        out[...] = total[:, at : at + out.shape[1]].astype(out.dtype)
        at += out.shape[1]


def matmul(lefts, rights, resid, place, widths):
    tokens, depth = lefts[0].shape
    width = rights[0].shape[1]
    tile = 2 * resid.shape[0]
    flops = 2 * tokens * depth * len(lefts) * width
    moved = 2 * (tokens * depth * len(lefts) + depth * len(lefts) * width + tokens * width)
    return pl.pallas_call(
        functools.partial(matmul_kernel, len(lefts), len(rights)),
        grid_spec=pltpu.PrefetchScalarGridSpec(
            num_scalar_prefetch=1,
            grid=(tokens // tile,),
            in_specs=[pl.BlockSpec((tile, depth), lambda step, place: (step, 0))] * len(lefts)
            + [pl.BlockSpec(right.shape, lambda step, place: (0, 0)) for right in rights]
            + [pl.BlockSpec(resid.shape, lambda step, place: (0, 0))],
            out_specs=[pl.BlockSpec((tile, part), lambda step, place: (step, 0)) for part in widths],
        ),
        out_shape=[jax.ShapeDtypeStruct((tokens, part), jnp.bfloat16) for part in widths],
        compiler_params=pltpu.CompilerParams(vmem_limit_bytes=VMEM_BYTES),
        cost_estimate=pl.CostEstimate(flops=flops, bytes_accessed=moved, transcendentals=0),
        name="partial_product",
    )(place, *lefts, *rights, resid)


def on_device(
    out_grad,
    gate_in,
    conv_in,
    scan_grad,
    conv_weight,
    conv_bias,
    skip_scale,
    projection,
    resid_grad,
    routes,
    gate_probs,
):
    ctx_count = lax.axis_size("ctx")
    exp_count = lax.axis_size("exp")
    chips = exp_count // 2
    ctx_at = lax.axis_index("ctx")
    exp_at = lax.axis_index("exp")
    chip_at = exp_at // 2
    core_at = exp_at % 2
    channels, length = out_grad.shape
    features = projection.shape[1]
    half = features // 2
    unit = half // UNITS
    widths = [[unit * part for part in group] for group in GROUPS]
    starts = [sum(map(sum, widths[:at])) for at in range(len(widths))]
    tok_rows = resid_grad.shape[0]
    window = tok_rows * exp_count
    tile = 2 * tok_rows

    def to_core(array):
        return lax.ppermute(array, "exp", [(place, place ^ 1) for place in range(exp_count)])

    def to_ctx(array, offset):
        return lax.ppermute(array, "ctx", [(place, place ^ offset) for place in range(ctx_count)])

    def swap_chips(array, low, inward=True, outward=True):
        pairs = set()
        for core in (0, 1):
            for near, far in ((low, low + 1), (chips - 1 - low, chips - 2 - low)):
                if inward:
                    pairs.add((2 * near + core, 2 * far + core))
                if outward:
                    pairs.add((2 * far + core, 2 * near + core))
        return lax.ppermute(array, "exp", sorted(pairs))

    def columns_of(array, core, at, width):
        return lax.dynamic_slice_in_dim(array, core * half + at, width, 1)

    def both_cores(array, at, width):
        here = columns_of(array, core_at, at, width)
        return here, to_core(columns_of(array, 1 - core_at, at, width))

    def spread_near(piece):
        return [piece, to_ctx(piece, 1), to_ctx(piece, 2)]

    def spread_far(near):
        near = list(chain(*near))
        return near + [to_ctx(near[0], 3)]

    def spread(piece):
        return [piece] + [to_ctx(piece, offset) for offset in range(1, ctx_count)]

    first = sum(widths[0])
    rights = [spread(jnp.concatenate(both_cores(projection, 0, first), axis=0))]

    turned = conv_grad(
        ctx_at.astype(jnp.int32).reshape(1),
        ctx_count,
        out_grad,
        gate_in,
        conv_in,
        scan_grad,
        conv_weight,
        conv_bias,
        skip_scale,
    )
    turned, rights[0] = lax.optimization_barrier((turned, rights[0]))
    lefts = [turned[0], to_core(turned[0])]
    received = [to_ctx(turned[offset], offset) for offset in range(1, ctx_count)]
    lefts[1], projection, resid_grad, routes = lax.optimization_barrier((lefts[1], projection, resid_grad, routes))

    routed = jnp.concatenate([routes.T.astype(jnp.float32), gate_probs.T], axis=0)[None]
    offset = 1
    while offset < exp_count:
        other = lax.ppermute(routed, "exp", [(place, place ^ offset) for place in range(exp_count)])
        routed = jnp.concatenate([routed, other], axis=0)
        offset *= 2
    order = (jnp.arange(exp_count)[:, None] ^ exp_at) == jnp.arange(exp_count)[None, :]
    routed = jnp.sum(jnp.where(order[:, :, None, None], routed[None], 0.0), axis=1)

    rest_here, rest_there = both_cores(projection, first, half - first)
    rest = []
    for group, at in list(zip(widths, starts))[1:]:
        cut = slice(at - first, at - first + sum(group))
        rest.append(jnp.concatenate([rest_here[:, cut], rest_there[:, cut]], axis=0))
    resid_here, resid_there = both_cores(resid_grad, 0, half)
    resid = jnp.where(
        core_at == 0,
        jnp.concatenate([resid_here, resid_there], axis=0),
        jnp.concatenate([resid_there, resid_here], axis=0),
    )

    route_width = routes.shape[1]
    all_routes = routed[:, :route_width]
    all_probs = routed[:, route_width:]
    capacity = max(2, 14 * tok_rows // (4 * EXP_DEV * exp_count))
    experts = jnp.stack([exp_at, exp_at ^ 1]).astype(jnp.float32)
    named = all_routes[None] == experts[:, None, None, None]
    hit = jnp.any(named, axis=2)
    prob = jnp.sum(jnp.where(named, all_probs[None], 0.0), axis=2)
    count = hit.astype(jnp.int32)
    rank = jnp.cumsum(count, axis=2) - count
    slot = jnp.where(hit, rank + (jnp.arange(exp_count, dtype=jnp.int32) % 2)[None, :, None] * capacity, -1)
    slot = slot.reshape(2, chips, 1, tile)
    picks = slot == jnp.arange(2 * capacity, dtype=jnp.int32)[None, None, :, None]
    scale = jnp.sum(jnp.where(picks, prob.reshape(2, chips, 1, tile), 0.0), axis=3, keepdims=True)
    picks = picks.astype(jnp.bfloat16)

    rights.append(spread(rest[0]))
    received, rest, rights[1], resid, picks, scale = lax.optimization_barrier(
        (received, rest, rights[1], resid, picks, scale)
    )
    for piece in received:
        lefts += [piece, to_core(piece)]

    if channels < 128:
        lefts = [jnp.concatenate(lefts, axis=1)]
    place = chip_at.astype(jnp.int32).reshape(1)
    pieces = sum(map(len, GROUPS))
    token = [place]

    def chain(*arrays):
        *arrays, token[0] = lax.optimization_barrier((*arrays, token[0]))
        token[0] = arrays[0]
        return arrays

    def products(group_at, right):
        group, at = widths[group_at], starts[group_at]
        if channels < 128:
            right = [jnp.concatenate(right, axis=0)]
        right = chain(*right)
        found = matmul(lefts, right, resid[:, at : at + sum(group)], place, group)
        token[0] = found[0]
        return found

    middle = chips // 2
    distance = jnp.minimum(chip_at, chips - 1 - chip_at)
    rows_own, rows_got, waiting = [], [], []

    def add(one, other):
        return (one.astype(jnp.float32) + other.astype(jnp.float32)).astype(jnp.bfloat16)

    def finish(grads):
        width = grads.shape[1]
        rows = jnp.einsum("eist,itf->eisf", picks, grads.reshape(chips, tile, width), preferred_element_type=jnp.float32)
        rows = (rows * scale).astype(jnp.bfloat16).reshape(2, chips * 2 * capacity, width)
        rows_own.append(rows[0])
        waiting.append(rows[1])
        if len(rows_own) in SWAPS:
            rows_got.append(to_core(jnp.concatenate(waiting, axis=1)))
            waiting.clear()

    square = ctx_count == 4
    hops = middle - 1
    lag = DELAY - 1
    sums = [[None] * pieces for _ in range(hops + 1)]
    ready = [[None] * pieces for _ in range(hops + 1)]
    outer, across, postponed = {}, {}, []
    first_of = [sum(map(len, GROUPS[:at])) for at in range(len(GROUPS))]
    lefts, rest[1] = lax.optimization_barrier((lefts, rest[1]))
    rights.append(spread_near(rest[1]) if square else spread(rest[1]))
    sums[0][: len(GROUPS[0])] = products(0, rights[0])
    rights += [None] * (len(GROUPS) - len(rights))
    for step in range(pieces + 2 * lag * hops + DELAY + 1):
        for hop in range(hops):
            if (step - 2, hop) not in outer:
                continue
            got, inward, outward = outer[step - 2, hop]
            if inward is not None:
                own, got = chain(sums[hop][inward], got)
                sums[hop + 1][inward] = token[0] = add(own, got)
                if hop == hops - 1:
                    across[step] = (swap_chips(token[0], middle - 1), inward)
            if outward is not None:
                ready[hop][outward] = jnp.where(distance == hop, got, ready[hop + 1][outward])
                if hop == 0:
                    postponed.append(ready[0][outward])
        if step - 1 in across:
            got, index = across[step - 1]
            own, got = chain(sums[hops][index], got)
            ready[hops][index] = add(own, got)
        if step in SECOND_PHASE and square:
            rights[SECOND_PHASE[step]] = spread_far(rights[SECOND_PHASE[step]])
        group_at = first_of.index(step) if step and step in first_of else None
        if step in FIRST_PHASE:
            coming = FIRST_PHASE[step]
            piece, *rights[group_at] = chain(rest[coming - 1], *rights[group_at])
            rights[coming] = spread_near(piece) if square else spread(piece)
        if group_at:
            sums[0][step : step + len(GROUPS[group_at])] = products(group_at, rights[group_at])
        for hop in range(hops):
            inward = step - lag * hop
            outward = inward - DELAY - 2 * lag * (hops - 1 - hop)
            inward = inward if 0 <= inward < pieces else None
            outward = outward if 0 <= outward < pieces else None
            if inward is not None and outward is not None:
                payload = jnp.where(distance == hop, sums[hop][inward], ready[hop + 1][outward])
            elif inward is not None:
                payload = sums[hop][inward]
            elif outward is not None:
                payload = ready[hop + 1][outward]
            else:
                continue
            (payload,) = chain(payload)
            outer[step, hop] = (swap_chips(payload, hop, inward is not None, outward is not None), inward, outward)
        if step == 0 and square:
            (piece,) = chain(rights[2][0])
            rights[2].append(to_ctx(piece, 3))
        if step == 1 and square:
            rights[2][1:3] = chain(*rights[2][1:3])
        if step >= pieces and postponed:
            for grads in chain(*postponed):
                finish(grads)
            postponed.clear()
    result = jnp.where(
        core_at == 0,
        jnp.concatenate(rows_own + rows_got, axis=1),
        jnp.concatenate(rows_got + rows_own, axis=1),
    )
    return result[None]


def solution(mesh):
    placed = (
        P(("ctx", "exp"), None),
        P(("ctx", "exp"), None),
        P(("ctx", "exp"), None),
        P(("ctx", "exp"), None),
        P(None, ("ctx", "exp")),
        P(("ctx", "exp")),
        P(("ctx", "exp")),
        P(("ctx", "exp"), None),
        P(("ctx", "exp"), None),
        P(("ctx", "exp"), None),
        P(("ctx", "exp"), None),
    )
    return jax.shard_map(
        on_device, mesh=mesh, in_specs=placed, out_specs=P("exp", "ctx", None), check_vma=False
    )
```

```python
import functools

import jax
import jax.numpy as jnp
from jax import lax
from jax.experimental import pallas as pl
from jax.experimental.pallas import tpu as pltpu
from jax.sharding import PartitionSpec as P

EXP_DEV = 1
GROUPS = ((1,), (1,), (1, 1), (1, 1), (1, 1))
FIRST_PHASE = {2: 3, 4: 4}
SECOND_PHASE = {3: 3, 5: 4}
UNITS = sum(map(sum, GROUPS))
DELAY = 3
SWAPS = (6, 8)
VMEM_BYTES = 60 * 1024 * 1024


def conv_kernel(tile, at_ctx, out_grad, gate_in, conv_in, scan_grad, taps, bias, skip, *refs):
    turned, flat, columns_of = refs[:-2], refs[-2], refs[-1]
    channels, length = out_grad.shape
    window = length // len(turned)
    kernel_taps = taps.shape[0]
    rows_at_once = 16
    settings = jnp.concatenate(
        [0.5 * taps[...], 0.5 * bias[...], skip[...], jnp.zeros((8 - kernel_taps - 2, channels), jnp.float32)], axis=0
    )
    columns_of[...] = settings.T

    def row_group(group, _):
        row_at = pl.multiple_of(group * rows_at_once, rows_at_once)
        rows = pl.ds(row_at, rows_at_once)

        def spread(index, width=tile):
            column = jnp.broadcast_to(columns_of[rows, index : index + 1], (rows_at_once, 128))
            return jnp.concatenate([column] * (width // 128), axis=1)

        weights = [spread(tap) for tap in range(kernel_taps)]
        wider = [spread(tap, tile + 128) for tap in (0, 1)]
        bias_half = spread(kernel_taps)
        skip_value = spread(kernel_taps + 1)
        after = jnp.zeros((rows_at_once, 128), jnp.float32)
        for at in range(length - tile, -1, -tile):
            columns = pl.ds(at, tile)
            gate = 0.5 * gate_in[rows, columns].astype(jnp.float32)
            gated = out_grad[rows, columns].astype(jnp.float32) * (gate + gate * jnp.tanh(gate))
            here = conv_in[rows, columns].astype(jnp.float32)
            if at:
                before = conv_in[rows, pl.ds(at - 128, 128)].astype(jnp.float32)
            else:
                before = jnp.zeros((rows_at_once, 128), jnp.float32)
            wide = jnp.concatenate([before, here], axis=1)
            one_back = pltpu.roll(wide, 1, 1)
            older = wider[1] * wide + wider[0] * one_back
            half = bias_half + weights[3] * here + weights[2] * one_back[:, 128:]
            half = half + pltpu.roll(older, 2, 1)[:, 128:]
            turn = jnp.tanh(half)
            scan = scan_grad[rows, columns].astype(jnp.float32)
            grad = (scan + skip_value * gated) * (1.0 + turn + half * (1.0 - turn * turn))
            wide_grad = jnp.concatenate([grad, after], axis=1)
            one_on = pltpu.roll(wide_grad, tile + 127, 1)
            later = wider[1] * wide_grad + wider[0] * one_on
            total = weights[3] * grad + weights[2] * one_on[:, :tile]
            total = total + pltpu.roll(later, tile + 126, 1)[:, :tile]
            flat[rows, columns] = total.astype(flat.dtype)
            after = grad[:, :128]
        return 0

    lax.fori_loop(0, channels // rows_at_once, row_group, 0)
    for offset, out in enumerate(turned):
        from_at = (at_ctx[0] ^ offset) * window
        for at in range(0, window, tile):
            out[pl.ds(at, tile), :] = flat[:, pl.ds(pl.multiple_of(from_at + at, tile), tile)].T


def conv_grad(at_ctx, ctx_count, out_grad, gate_in, conv_in, scan_grad, conv_weight, conv_bias, skip_scale):
    channels, length = out_grad.shape
    block = min(128, channels)
    window = length // ctx_count
    tile = min(1024, window)
    whole = pl.BlockSpec((block, length), lambda step, at_ctx: (step, 0))
    row = pl.BlockSpec((1, block), lambda step, at_ctx: (0, step))
    return pl.pallas_call(
        functools.partial(conv_kernel, tile),
        grid_spec=pltpu.PrefetchScalarGridSpec(
            num_scalar_prefetch=1,
            grid=(channels // block,),
            in_specs=[whole] * 4
            + [pl.BlockSpec((conv_weight.shape[0], block), lambda step, at_ctx: (0, step)), row, row],
            out_specs=[pl.BlockSpec((window, block), lambda step, at_ctx: (0, step))] * ctx_count,
            scratch_shapes=[pltpu.VMEM((block, length), jnp.bfloat16), pltpu.VMEM((block, 8), jnp.float32)],
        ),
        out_shape=[jax.ShapeDtypeStruct((window, channels), jnp.bfloat16)] * ctx_count,
        compiler_params=pltpu.CompilerParams(vmem_limit_bytes=VMEM_BYTES),
        cost_estimate=pl.CostEstimate(
            flops=40 * channels * length, bytes_accessed=10 * channels * length, transcendentals=2 * channels * length
        ),
        name="conv_grad",
    )(at_ctx, out_grad, gate_in, conv_in, scan_grad, conv_weight, conv_bias[None], skip_scale[None])


def matmul_kernel(lefts, rights, place, *refs):
    left_refs = refs[:lefts]
    right_refs = refs[lefts : lefts + rights]
    resid = refs[lefts + rights]
    outs = refs[lefts + rights + 1 :]
    left = jnp.concatenate([ref[...] for ref in left_refs], axis=1)
    right = jnp.concatenate([ref[...] for ref in right_refs], axis=0)
    total = jnp.dot(left, right, preferred_element_type=jnp.float32)
    many = left.shape[0] // resid.shape[0]
    parts = []
    for part in range(many):
        mine = pl.program_id(0) * many + part == place[0]
        rows = total[part * resid.shape[0] : (part + 1) * resid.shape[0]]
        parts.append(rows + jnp.where(mine, resid[...].astype(jnp.float32), 0.0))
    total = jnp.concatenate(parts, axis=0)
    at = 0
    for out in outs:
        out[...] = total[:, at : at + out.shape[1]].astype(out.dtype)
        at += out.shape[1]


def matmul(lefts, rights, resid, place, widths):
    tokens, depth = lefts[0].shape
    width = rights[0].shape[1]
    tile = min(tokens, 4 * resid.shape[0])
    flops = 2 * tokens * depth * len(lefts) * width
    moved = 2 * (tokens * depth * len(lefts) + depth * len(lefts) * width + tokens * width)
    return pl.pallas_call(
        functools.partial(matmul_kernel, len(lefts), len(rights)),
        grid_spec=pltpu.PrefetchScalarGridSpec(
            num_scalar_prefetch=1,
            grid=(tokens // tile,),
            in_specs=[pl.BlockSpec((tile, depth), lambda step, place: (step, 0))] * len(lefts)
            + [pl.BlockSpec(right.shape, lambda step, place: (0, 0)) for right in rights]
            + [pl.BlockSpec(resid.shape, lambda step, place: (0, 0))],
            out_specs=[pl.BlockSpec((tile, part), lambda step, place: (step, 0)) for part in widths],
        ),
        out_shape=[jax.ShapeDtypeStruct((tokens, part), jnp.bfloat16) for part in widths],
        compiler_params=pltpu.CompilerParams(vmem_limit_bytes=VMEM_BYTES),
        cost_estimate=pl.CostEstimate(flops=flops, bytes_accessed=moved, transcendentals=0),
        name="partial_product",
    )(place, *lefts, *rights, resid)


def on_device(
    out_grad,
    gate_in,
    conv_in,
    scan_grad,
    conv_weight,
    conv_bias,
    skip_scale,
    projection,
    resid_grad,
    routes,
    gate_probs,
):
    ctx_count = lax.axis_size("ctx")
    exp_count = lax.axis_size("exp")
    chips = exp_count // 2
    ctx_at = lax.axis_index("ctx")
    exp_at = lax.axis_index("exp")
    chip_at = exp_at // 2
    core_at = exp_at % 2
    channels, length = out_grad.shape
    features = projection.shape[1]
    half = features // 2
    unit = half // UNITS
    widths = [[unit * part for part in group] for group in GROUPS]
    starts = [sum(map(sum, widths[:at])) for at in range(len(widths))]
    tok_rows = resid_grad.shape[0]
    window = tok_rows * exp_count
    tile = 2 * tok_rows

    def to_core(array):
        return lax.ppermute(array, "exp", [(place, place ^ 1) for place in range(exp_count)])

    def to_ctx(array, offset):
        return lax.ppermute(array, "ctx", [(place, place ^ offset) for place in range(ctx_count)])

    def swap_chips(array, low, inward=True, outward=True):
        pairs = set()
        for core in (0, 1):
            for near, far in ((low, low + 1), (chips - 1 - low, chips - 2 - low)):
                if inward:
                    pairs.add((2 * near + core, 2 * far + core))
                if outward:
                    pairs.add((2 * far + core, 2 * near + core))
        return lax.ppermute(array, "exp", sorted(pairs))

    def columns_of(array, core, at, width):
        return lax.dynamic_slice_in_dim(array, core * half + at, width, 1)

    def both_cores(array, at, width):
        here = columns_of(array, core_at, at, width)
        return here, to_core(columns_of(array, 1 - core_at, at, width))

    def spread_near(piece):
        return [piece, to_ctx(piece, 1), to_ctx(piece, 2)]

    def spread_far(near):
        near = list(chain(*near))
        return near + [to_ctx(near[0], 3)]

    def spread(piece):
        return [piece] + [to_ctx(piece, offset) for offset in range(1, ctx_count)]

    first = sum(widths[0])
    rights = [spread(jnp.concatenate(both_cores(projection, 0, first), axis=0))]

    turned = conv_grad(
        ctx_at.astype(jnp.int32).reshape(1),
        ctx_count,
        out_grad,
        gate_in,
        conv_in,
        scan_grad,
        conv_weight,
        conv_bias,
        skip_scale,
    )
    turned, rights[0] = lax.optimization_barrier((turned, rights[0]))
    lefts = [turned[0], to_core(turned[0])]
    received = [to_ctx(turned[offset], offset) for offset in range(1, ctx_count)]
    lefts[1], projection, resid_grad, routes = lax.optimization_barrier((lefts[1], projection, resid_grad, routes))

    routed = jnp.concatenate([routes.T.astype(jnp.float32), gate_probs.T], axis=0)[None]
    offset = 1
    while offset < exp_count:
        other = lax.ppermute(routed, "exp", [(place, place ^ offset) for place in range(exp_count)])
        routed = jnp.concatenate([routed, other], axis=0)
        offset *= 2
    order = (jnp.arange(exp_count)[:, None] ^ exp_at) == jnp.arange(exp_count)[None, :]
    routed = jnp.sum(jnp.where(order[:, :, None, None], routed[None], 0.0), axis=1)

    rest_here, rest_there = both_cores(projection, first, half - first)
    rest = []
    for group, at in list(zip(widths, starts))[1:]:
        cut = slice(at - first, at - first + sum(group))
        rest.append(jnp.concatenate([rest_here[:, cut], rest_there[:, cut]], axis=0))
    resid_here, resid_there = both_cores(resid_grad, 0, half)
    resid = jnp.where(
        core_at == 0,
        jnp.concatenate([resid_here, resid_there], axis=0),
        jnp.concatenate([resid_there, resid_here], axis=0),
    )

    route_width = routes.shape[1]
    all_routes = routed[:, :route_width]
    all_probs = routed[:, route_width:]
    capacity = max(2, 14 * tok_rows // (4 * EXP_DEV * exp_count))
    experts = jnp.stack([exp_at, exp_at ^ 1]).astype(jnp.float32)
    named = all_routes[None] == experts[:, None, None, None]
    hit = jnp.any(named, axis=2)
    prob = jnp.sum(jnp.where(named, all_probs[None], 0.0), axis=2)
    count = hit.astype(jnp.int32)
    rank = jnp.cumsum(count, axis=2) - count
    slot = jnp.where(hit, rank + (jnp.arange(exp_count, dtype=jnp.int32) % 2)[None, :, None] * capacity, -1)
    slot = slot.reshape(2, chips, 1, tile)
    picks = slot == jnp.arange(2 * capacity, dtype=jnp.int32)[None, None, :, None]
    scale = jnp.sum(jnp.where(picks, prob.reshape(2, chips, 1, tile), 0.0), axis=3, keepdims=True)
    picks = picks.astype(jnp.bfloat16)

    rights.append(spread(rest[0]))
    received, rest, rights[1], resid, picks, scale = lax.optimization_barrier(
        (received, rest, rights[1], resid, picks, scale)
    )
    for piece in received:
        lefts += [piece, to_core(piece)]

    if channels < 128:
        lefts = [jnp.concatenate(lefts, axis=1)]
    place = chip_at.astype(jnp.int32).reshape(1)
    pieces = sum(map(len, GROUPS))
    token = [place]

    def chain(*arrays):
        *arrays, token[0] = lax.optimization_barrier((*arrays, token[0]))
        token[0] = arrays[0]
        return arrays

    def products(group_at, right):
        group, at = widths[group_at], starts[group_at]
        if channels < 128:
            right = [jnp.concatenate(right, axis=0)]
        right = chain(*right)
        found = matmul(lefts, right, resid[:, at : at + sum(group)], place, group)
        token[0] = found[0]
        return found

    middle = chips // 2
    distance = jnp.minimum(chip_at, chips - 1 - chip_at)
    rows_own, rows_got, waiting = [], [], []

    def add(one, other):
        return (one.astype(jnp.float32) + other.astype(jnp.float32)).astype(jnp.bfloat16)

    def finish(grads):
        width = grads.shape[1]
        rows = jnp.einsum("eist,itf->eisf", picks, grads.reshape(chips, tile, width), preferred_element_type=jnp.float32)
        rows = (rows * scale).astype(jnp.bfloat16).reshape(2, chips * 2 * capacity, width)
        rows_own.append(rows[0])
        waiting.append(rows[1])
        if len(rows_own) in SWAPS:
            rows_got.append(to_core(jnp.concatenate(waiting, axis=1)))
            waiting.clear()

    square = ctx_count == 4
    hops = middle - 1
    lag = DELAY - 1
    sums = [[None] * pieces for _ in range(hops + 1)]
    ready = [[None] * pieces for _ in range(hops + 1)]
    outer, across = {}, {}
    first_of = [sum(map(len, GROUPS[:at])) for at in range(len(GROUPS))]
    lefts, rest[1] = lax.optimization_barrier((lefts, rest[1]))
    rights.append(spread_near(rest[1]) if square else spread(rest[1]))
    sums[0][: len(GROUPS[0])] = products(0, rights[0])
    rights += [None] * (len(GROUPS) - len(rights))
    for step in range(pieces + 2 * lag * hops + DELAY + 1):
        for hop in range(hops):
            if (step - 2, hop) not in outer:
                continue
            got, inward, outward = outer[step - 2, hop]
            if inward is not None:
                own, got = chain(sums[hop][inward], got)
                sums[hop + 1][inward] = token[0] = add(own, got)
                if hop == hops - 1:
                    across[step] = (swap_chips(token[0], middle - 1), inward)
            if outward is not None:
                ready[hop][outward] = jnp.where(distance == hop, got, ready[hop + 1][outward])
                if hop == 0:
                    finish(ready[0][outward])
        if step - 1 in across:
            got, index = across[step - 1]
            own, got = chain(sums[hops][index], got)
            ready[hops][index] = add(own, got)
        if step in SECOND_PHASE and square:
            rights[SECOND_PHASE[step]] = spread_far(rights[SECOND_PHASE[step]])
        group_at = first_of.index(step) if step and step in first_of else None
        if step in FIRST_PHASE:
            coming = FIRST_PHASE[step]
            piece, *rights[group_at] = chain(rest[coming - 1], *rights[group_at])
            rights[coming] = spread_near(piece) if square else spread(piece)
        if group_at:
            sums[0][step : step + len(GROUPS[group_at])] = products(group_at, rights[group_at])
        for hop in range(hops):
            inward = step - lag * hop
            outward = inward - DELAY - 2 * lag * (hops - 1 - hop)
            inward = inward if 0 <= inward < pieces else None
            outward = outward if 0 <= outward < pieces else None
            if inward is not None and outward is not None:
                payload = jnp.where(distance == hop, sums[hop][inward], ready[hop + 1][outward])
            elif inward is not None:
                payload = sums[hop][inward]
            elif outward is not None:
                payload = ready[hop + 1][outward]
            else:
                continue
            (payload,) = chain(payload)
            outer[step, hop] = (swap_chips(payload, hop, inward is not None, outward is not None), inward, outward)
        if step == 0 and square:
            (piece,) = chain(rights[2][0])
            rights[2].append(to_ctx(piece, 3))
        if step == 1 and square:
            rights[2][1:3] = chain(*rights[2][1:3])
    result = jnp.where(
        core_at == 0,
        jnp.concatenate(rows_own + rows_got, axis=1),
        jnp.concatenate(rows_got + rows_own, axis=1),
    )
    return result[None]


def solution(mesh):
    placed = (
        P(("ctx", "exp"), None),
        P(("ctx", "exp"), None),
        P(("ctx", "exp"), None),
        P(("ctx", "exp"), None),
        P(None, ("ctx", "exp")),
        P(("ctx", "exp")),
        P(("ctx", "exp")),
        P(("ctx", "exp"), None),
        P(("ctx", "exp"), None),
        P(("ctx", "exp"), None),
        P(("ctx", "exp"), None),
    )
    return jax.shard_map(
        on_device, mesh=mesh, in_specs=placed, out_specs=P("exp", "ctx", None), check_vma=False
    )
```
